32 devices in a mesh: seq: 8 (over z, core), mp: 4 (over y, x).
Axes of the slice: x: 2, y: 2, z: 4, core: 2. Of those that a mesh axis runs over, the one named last changes fastest.
Arguments:
- continued_prompt_entries: bfloat16 [1024, 4096], P('seq', 'mp'), may hold values from -6 to 6
- padded_prompt_entries: bfloat16 [1024, 4096], P('seq', 'mp'), may hold values from -6 to 6
- prompt_live_extents: int32 [16], P('seq'), may hold values from 8 to 64, as said below
- preceding_entry_line: bfloat16 [4096], P('mp'), may hold values from -6 to 6
- carried_memory: float32 [64, 64, 64], P('mp'), may hold values from -24 to 24
- token_mixing_ratios: float32 [5, 4096], replicated, may hold values from 0.05 to 0.95
- acceptance_transform: bfloat16 [4096, 4096], P('seq', 'mp'), may hold values from -0.09375 to 0.09375
- lookup_transform: bfloat16 [4096, 4096], P('seq', 'mp'), may hold values from -0.09375 to 0.09375
- payload_transform: bfloat16 [4096, 4096], P('seq', 'mp'), may hold values from -0.09375 to 0.09375
- gating_transform: bfloat16 [4096, 4096], P('seq', 'mp'), may hold values from -0.09375 to 0.09375
- fading_baseline: float32 [4096], P('mp'), may hold values from -10 to -3.5
- fading_left_factor: bfloat16 [4096, 128], replicated, may hold values from -0.09375 to 0.09375
- fading_right_factor: bfloat16 [128, 4096], P(None, 'mp'), may hold values from -0.5 to 0.5
- present_reward: float32 [64, 64], P('mp'), may hold values from -3 to 3
- group_layer_scaling: float32 [4096], P('mp'), may hold values from 0.5 to 1.5
- group_layer_shift_term: float32 [4096], P('mp'), may hold values from -1.8 to 1.8
- final_transform: bfloat16 [4096, 4096], P('mp', 'seq'), may hold values from -0.09375 to 0.09375
Outputs:
- mixed: bfloat16 [8, 256, 4096], P('seq', 'mp')
- span_states: float32 [8, 64, 64, 64], P('seq', 'mp')
- request_states: float32 [16, 64, 64, 64], P('seq', 'mp')
The draws below stay inside these ranges and needn't reach their ends.
Inputs may be any that keep to these rules, and one draw needn't show every extreme that they name: `prompt_live_extents`: some request has all 64 rows live.
All inputs are finite; a program needn't handle non-finite values.
Results may differ from the reference program's by a relative error of at most 0.0076.
Values may be sent and summed in bfloat16 or wider, within the bound.
No kernel may reach another device: no remote copies, remote signals or barrier semaphores. Data moves between devices by JAX's collectives and lax.ppermute only.
A program may use at most 128 MiB of HBM per device.

```python
import jax
import jax.numpy as jnp
from jax import lax

D = 4096
ATTENTION_GROUPS = 64
CHANNEL_SPAN = 64
RANK = 128
L_DEV = 128
REQ_DEV = 2
SLOT = 64
GROUPS = 8
LONG = 1024
REQS = 16
SHORT = 1024


def draw_prompt_live_extents(key, part):
    lowest = max(1, SLOT // 8)
    drawn = jax.random.randint(key, (REQS,), lowest, SLOT + 1)
    drawn = drawn.at[0].set(SLOT)
    drawn = drawn.at[REQS - 1].set(lowest)
    return drawn.astype(jnp.int32)


def steps_of(rng, extent, shards, smallest, high):
    factor_of, own = 1.0, jax.random.fold_in(rng, 6)
    for axis_at, parts in shards:
        steps = jnp.exp(jax.random.uniform(jax.random.fold_in(own, axis_at), (parts,), jnp.float32, smallest / len(shards), high / len(shards)))
        factor_of = factor_of * jnp.repeat(steps, extent[axis_at] // parts).reshape([-1 if axis == axis_at else 1 for axis in range(len(extent))])
    return factor_of


def noise(stream_key, shape, deviation, most, split=(), kind=jnp.bfloat16):
    values = deviation * jax.random.normal(stream_key, shape, jnp.float32)
    if split:
        values = values * steps_of(stream_key, shape, split, -0.22, 0.18)
    return jnp.clip(values, -most, most).astype(kind)


def setup_inputs(seed: int = 0) -> dict:
    keys = jax.random.split(jax.random.key(seed), 18)
    return {
        "continued_prompt_entries": noise(keys[0], (LONG, D), 1.0, 6.0, ((0, 8), (1, 4))),
        "padded_prompt_entries": noise(keys[1], (SHORT, D), 1.0, 6.0, ((0, 8), (1, 4))),
        "prompt_live_extents": draw_prompt_live_extents(jax.random.fold_in(keys[17], 71), 0),
        "preceding_entry_line": noise(keys[3], (D,), 1.0, 6.0, ((0, 4),)),
        "carried_memory": noise(keys[4], (ATTENTION_GROUPS, CHANNEL_SPAN, CHANNEL_SPAN), 4.0, 24.0, ((0, 4),), jnp.float32),
        "token_mixing_ratios": jnp.clip(jax.random.uniform(keys[5], (5, D), jnp.float32, 0.05, 0.95), 0.05, 0.95),
        "acceptance_transform": noise(keys[6], (D, D), D ** -0.5, 0.09375, ((0, 8), (1, 4))),
        "lookup_transform": noise(keys[7], (D, D), D ** -0.5, 0.09375, ((0, 8), (1, 4))),
        "payload_transform": noise(keys[8], (D, D), D ** -0.5, 0.09375, ((0, 8), (1, 4))),
        "gating_transform": noise(keys[9], (D, D), D ** -0.5, 0.09375, ((0, 8), (1, 4))),
        "fading_baseline": jnp.clip(-10.0 + 6.5 * jax.random.uniform(keys[10], (D,), jnp.float32) ** steps_of(keys[10], (D,), ((0, 4),), -0.2, 0.2), -10.0, -3.5),
        "fading_left_factor": noise(keys[11], (D, RANK), D ** -0.5, 0.09375),
        "fading_right_factor": noise(keys[12], (RANK, D), RANK ** -0.5, 0.5, ((1, 4),)),
        "present_reward": noise(keys[13], (ATTENTION_GROUPS, CHANNEL_SPAN), 0.5, 3.0, ((0, 4),), jnp.float32),
        "group_layer_scaling": jnp.clip(1.0 + 0.1 * jax.random.normal(keys[14], (D,), jnp.float32), 0.5, 1.5),
        "group_layer_shift_term": noise(keys[15], (D,), 0.3, 1.8, ((0, 4),), jnp.float32),
        "final_transform": noise(keys[16], (D, D), D ** -0.5, 0.09375, ((0, 4), (1, 8))),
    }


def mix_rows(current, previous, weight):
    here = current.astype(jnp.float32)
    return (here + weight[None, :] * (previous.astype(jnp.float32) - here)).astype(jnp.bfloat16)

def reference(continued_prompt_entries, padded_prompt_entries, prompt_live_extents, preceding_entry_line, carried_memory, token_mixing_ratios, acceptance_transform, lookup_transform, payload_transform, gating_transform, fading_baseline, fading_left_factor, fading_right_factor, present_reward, group_layer_scaling, group_layer_shift_term, final_transform):
    long_prev = jnp.concatenate([preceding_entry_line[None, :], continued_prompt_entries[:-1]], axis=0)
    short_view = padded_prompt_entries.reshape(REQS, SLOT, D)
    short_prev = jnp.concatenate([jnp.zeros((REQS, 1, D), padded_prompt_entries.dtype), short_view[:, :-1]], axis=1).reshape(REQS * SLOT, D)
    current = jnp.concatenate([continued_prompt_entries, padded_prompt_entries], axis=0)
    previous = jnp.concatenate([long_prev, short_prev], axis=0)
    mixes = [mix_rows(current, previous, token_mixing_ratios[index]) for index in range(5)]
    acceptance_entries = jnp.dot(mixes[0], acceptance_transform, preferred_element_type=jnp.float32)
    lookup_entries = jnp.dot(mixes[1], lookup_transform, preferred_element_type=jnp.float32)
    payload_entries = jnp.dot(mixes[2], payload_transform, preferred_element_type=jnp.float32)
    gate = jnp.dot(mixes[3], gating_transform, preferred_element_type=jnp.float32)
    squeezed = jnp.tanh(jnp.dot(mixes[4], fading_left_factor, preferred_element_type=jnp.float32)).astype(jnp.bfloat16)
    log_fading_amount = -jnp.exp(fading_baseline[None, :] + jnp.dot(squeezed, fading_right_factor, preferred_element_type=jnp.float32))
    total_rows = LONG + SHORT
    heads_view = [a.reshape(total_rows, ATTENTION_GROUPS, CHANNEL_SPAN) for a in (acceptance_entries, lookup_entries, payload_entries, log_fading_amount)]

    def token_step(evolving_memory, entry_lines):
        acceptance_line, key_row, value_row, decay_row = entry_lines
        rank_one_update = key_row[:, :, None] * value_row[:, None, :]
        answer_lines = jnp.einsum('lr,lry->ly', acceptance_line, evolving_memory + present_reward[:, :, None] * rank_one_update, precision=lax.Precision.HIGHEST)
        return (jnp.exp(decay_row)[:, :, None] * evolving_memory + rank_one_update, answer_lines)

    def group_step(evolving_memory, entry_lines):
        evolving_memory, results = lax.scan(token_step, evolving_memory, entry_lines)
        return (evolving_memory, (results, evolving_memory))
    long_parts = tuple((a[:LONG].reshape(GROUPS, L_DEV, ATTENTION_GROUPS, CHANNEL_SPAN) for a in heads_view))
    final_state, (long_out, span_states) = lax.scan(group_step, carried_memory, long_parts)
    short_parts = tuple((a[LONG:].reshape(REQS, SLOT, ATTENTION_GROUPS, CHANNEL_SPAN) for a in heads_view))
    live_rows = lax.broadcasted_iota(jnp.int32, (REQS, SLOT), 1) < prompt_live_extents[:, None]

    def request_pass(acceptance_lines, lookup_table, payload_table, fading_table, live):

        def masked_step(evolving_memory, entry_lines):
            new_state, answer_lines = token_step(evolving_memory, entry_lines[:4])
            return (jnp.where(entry_lines[4], new_state, evolving_memory), answer_lines)
        return lax.scan(masked_step, jnp.zeros((ATTENTION_GROUPS, CHANNEL_SPAN, CHANNEL_SPAN), jnp.float32), (acceptance_lines, lookup_table, payload_table, fading_table, live))
    request_states, short_out = jax.vmap(request_pass)(*short_parts, live_rows)
    wkv = jnp.concatenate([long_out.reshape(LONG, ATTENTION_GROUPS, CHANNEL_SPAN), short_out.reshape(SHORT, ATTENTION_GROUPS, CHANNEL_SPAN)], axis=0)
    mean = lax.optimization_barrier(jnp.mean(wkv, axis=-1, keepdims=True))
    centred = wkv - mean
    variance = lax.optimization_barrier(jnp.mean(centred * centred, axis=-1, keepdims=True))
    normed = (centred * lax.rsqrt(variance + 0.00064)).reshape(total_rows, D) * group_layer_scaling[None, :] + group_layer_shift_term[None, :]
    row_live = jnp.concatenate([jnp.ones((LONG,), dtype=bool), live_rows.reshape(SHORT)], axis=0)
    hidden = jnp.where(row_live[:, None], normed * jax.nn.silu(gate), 0.0).astype(jnp.bfloat16)
    answer_lines = jnp.dot(hidden, final_transform, preferred_element_type=jnp.float32).astype(jnp.bfloat16)
    mixed = jnp.concatenate([answer_lines[:LONG].reshape(GROUPS, L_DEV, D), answer_lines[LONG:].reshape(GROUPS, REQ_DEV * SLOT, D)], axis=1)
    return (mixed, span_states, request_states)
```

```python
import jax
import jax.numpy as jnp
import numpy as np
from jax import lax
from jax.experimental import pallas as pl
from jax.experimental.pallas import tpu as pltpu
from jax.sharding import Mesh
from jax.sharding import PartitionSpec as P

BLK = 64


norm_eps = 0.00064
highest = lax.Precision.HIGHEST


def passed_along(x, axis, by):
    length = lax.axis_size(axis)
    pairs = [(i, i + by) for i in range(length) if 0 <= i + by < length]
    return lax.ppermute(x, axis, pairs)


def entering(value, axis, join, neutral):
    count, mine = (lax.axis_size(axis), lax.axis_index(axis))
    pieces = jax.tree.map(lambda part: lax.all_gather(part, axis), value)
    total = jax.tree.map(
        lambda part, zero: jnp.full_like(part, 0) + jnp.asarray(zero, part.dtype), value, neutral
    )

    def hop(position, total):
        longer = join(total, jax.tree.map(lambda part: part[position], pieces))
        return jax.tree.map(lambda new, old: jnp.where(position < mine, new, old), longer, total)

    return lax.fori_loop(0, count - 1, hop, total)


def mix_rows(current, previous, weight):
    here = current.astype(jnp.float32)
    return (here + weight[None, :] * (previous.astype(jnp.float32) - here)).astype(jnp.bfloat16)


def block_sweep(
    evolving_memory,
    acceptance_entries,
    lookup_entries,
    payload_entries,
    log_fading_amount,
    diagonal_reward,
):
    inclusive = jnp.cumsum(log_fading_amount, axis=0)
    exclusive = inclusive - log_fading_amount
    recept_scaled = acceptance_entries * jnp.exp(exclusive)
    keys_scaled = lookup_entries * jnp.exp(-inclusive)
    scores = jnp.einsum("ihc,jhc->hij", recept_scaled, keys_scaled, precision=highest)
    count = acceptance_entries.shape[0]
    row_index = lax.broadcasted_iota(jnp.int32, (count, count), 0)
    col_index = lax.broadcasted_iota(jnp.int32, (count, count), 1)
    scores = jnp.where((row_index > col_index)[None], scores, 0.0)
    diagonal_contribution = jnp.sum(
        acceptance_entries * diagonal_reward[None] * lookup_entries, axis=-1, keepdims=True
    )
    answer_lines = (
        jnp.einsum("hij,jhd->ihd", scores, payload_entries, precision=highest)
        + diagonal_contribution * payload_entries
    )
    answer_lines = answer_lines + jnp.einsum(
        "ihc,hcd->ihd", recept_scaled, evolving_memory, precision=highest
    )
    total = inclusive[-1]
    carried = lookup_entries * jnp.exp(total[None] - inclusive)
    new_state = jnp.exp(total)[:, :, None] * evolving_memory + jnp.einsum(
        "jhc,jhd->hcd", carried, payload_entries, precision=highest
    )
    return (new_state, answer_lines)


def continued_recurrence(
    acceptance_entries, lookup_entries, payload_entries, log_fading_amount, diagonal_reward
):
    length, per_group_view, embedding_dimension = acceptance_entries.shape
    blocks = length // BLK

    def step(evolving_memory, entry_lines):
        return block_sweep(
            evolving_memory,
            entry_lines[0],
            entry_lines[1],
            entry_lines[2],
            entry_lines[3],
            diagonal_reward,
        )

    shaped = tuple(
        (
            a.reshape(blocks, BLK, per_group_view, embedding_dimension)
            for a in (acceptance_entries, lookup_entries, payload_entries, log_fading_amount)
        )
    )
    evolving_memory, results = lax.scan(
        step,
        jnp.zeros((per_group_view, embedding_dimension, embedding_dimension), jnp.float32),
        shaped,
    )
    return (evolving_memory, results.reshape(length, per_group_view, embedding_dimension))


def combine(earlier, later):
    return (earlier[0] + later[0], jnp.exp(later[0])[:, :, None] * earlier[1] + later[1])


def shifted_rows(current, edge_row, long_rows, requests, slot_rows):
    feature_part = current.shape[1]
    long_prev = jnp.concatenate([edge_row, current[: long_rows - 1]], axis=0)
    short_view = current[long_rows:].reshape(requests, slot_rows, feature_part)
    short_prev = jnp.concatenate(
        [jnp.zeros((requests, 1, feature_part), current.dtype), short_view[:, :-1]], axis=1
    )
    short_prev = short_prev.reshape(requests * slot_rows, feature_part)
    return jnp.concatenate([long_prev, short_prev], axis=0)


def on_device(
    continued_prompt_entries,
    padded_prompt_entries,
    prompt_live_extents,
    preceding_entry_line,
    carried_memory,
    token_mixing_ratios,
    acceptance_transform,
    lookup_transform,
    payload_transform,
    gating_transform,
    fading_baseline,
    fading_left_factor,
    fading_right_factor,
    present_reward,
    group_layer_scaling,
    group_layer_shift_term,
    final_transform,
):
    long_rows = continued_prompt_entries.shape[0]
    requests = prompt_live_extents.shape[0]
    slot_rows = padded_prompt_entries.shape[0] // requests
    per_group_view, embedding_dimension = present_reward.shape
    arrived = passed_along(continued_prompt_entries[-1:], "seq", 1)
    first = lax.axis_index("seq") == 0
    edge_row = jnp.where(first, preceding_entry_line[None, :], arrived)
    current = jnp.concatenate([continued_prompt_entries, padded_prompt_entries], axis=0)
    current, edge_full = (
        lax.all_gather(current, "mp", axis=1, tiled=True),
        lax.all_gather(edge_row, "mp", axis=1, tiled=True),
    )
    previous = shifted_rows(current, edge_full, long_rows, requests, slot_rows)
    mixes = [mix_rows(current, previous, token_mixing_ratios[index]) for index in range(5)]
    total_rows = current.shape[0]
    columns = acceptance_transform.shape[1]
    pieces = (
        lax.all_gather(acceptance_transform, "seq", axis=0, tiled=True),
        lax.all_gather(lookup_transform, "seq", axis=0, tiled=True),
        lax.all_gather(payload_transform, "seq", axis=0, tiled=True),
        lax.all_gather(gating_transform, "seq", axis=0, tiled=True),
    )
    acceptance_entries, lookup_entries, payload_entries, gate = tuple(
        (
            jnp.dot(source, piece, preferred_element_type=jnp.float32)
            for source, piece in zip(mixes[:4], pieces)
        )
    )
    squeezed = jnp.tanh(
        jnp.dot(mixes[4], fading_left_factor, preferred_element_type=jnp.float32)
    ).astype(jnp.bfloat16)
    log_fading_amount = -jnp.exp(
        fading_baseline[None, :]
        + jnp.dot(squeezed, fading_right_factor, preferred_element_type=jnp.float32)
    )
    recept3, keys3, values3, decay3 = [
        a.reshape(total_rows, per_group_view, embedding_dimension)
        for a in (acceptance_entries, lookup_entries, payload_entries, log_fading_amount)
    ]
    local_state, long_out = continued_recurrence(
        recept3[:long_rows],
        keys3[:long_rows],
        values3[:long_rows],
        decay3[:long_rows],
        present_reward,
    )
    long_decay = decay3[:long_rows]
    group_total = jnp.sum(long_decay, axis=0)
    blank = (
        jnp.zeros((per_group_view, embedding_dimension), jnp.float32),
        jnp.zeros((per_group_view, embedding_dimension, embedding_dimension), jnp.float32),
    )
    prefix_total, prefix_state = entering((group_total, local_state), "seq", combine, blank)
    incoming = jnp.exp(prefix_total)[:, :, None] * carried_memory + prefix_state
    before_row = jnp.cumsum(long_decay, axis=0) - long_decay
    long_out = long_out + jnp.einsum(
        "ihc,hcd->ihd", recept3[:long_rows] * jnp.exp(before_row), incoming, precision=highest
    )
    span_end = jnp.exp(group_total)[:, :, None] * incoming + local_state
    live_rows = (
        lax.broadcasted_iota(jnp.int32, (requests, slot_rows), 1) < prompt_live_extents[:, None]
    )
    live_flat = live_rows.reshape(requests * slot_rows).astype(jnp.float32)[:, None, None]
    short_shape = (requests, slot_rows, per_group_view, embedding_dimension)
    short_recept = recept3[long_rows:].reshape(short_shape)
    short_keys = (keys3[long_rows:] * live_flat).reshape(short_shape)
    short_values = values3[long_rows:].reshape(short_shape)
    short_decay = (decay3[long_rows:] * live_flat).reshape(short_shape)
    zeroed_memory = jnp.zeros(
        (per_group_view, embedding_dimension, embedding_dimension), jnp.float32
    )

    def request_pass(acceptance_lines, lookup_table, payload_table, fading_table):
        return block_sweep(
            zeroed_memory,
            acceptance_lines,
            lookup_table,
            payload_table,
            fading_table,
            present_reward,
        )

    request_states, short_out = jax.vmap(request_pass)(
        short_recept, short_keys, short_values, short_decay
    )
    wkv = jnp.concatenate(
        [long_out, short_out.reshape(requests * slot_rows, per_group_view, embedding_dimension)],
        axis=0,
    )
    mean = jnp.mean(wkv, axis=-1, keepdims=True)
    centred = wkv - mean
    variance = jnp.mean(centred * centred, axis=-1, keepdims=True)
    normed = (centred * lax.rsqrt(variance + norm_eps)).reshape(
        total_rows, columns
    ) * group_layer_scaling[None, :] + group_layer_shift_term[None, :]
    row_live = jnp.concatenate(
        [jnp.ones((long_rows,), dtype=bool), live_rows.reshape(requests * slot_rows)], axis=0
    )
    hidden = jnp.where(row_live[:, None], normed * jax.nn.silu(gate), 0.0).astype(jnp.bfloat16)
    full_out = lax.all_gather(final_transform, "seq", axis=1, tiled=True)
    mixed_rows = lax.psum_scatter(
        jnp.dot(hidden, full_out, preferred_element_type=jnp.float32),
        "mp",
        scatter_dimension=0,
        tiled=True,
    )
    return (mixed_rows.astype(jnp.bfloat16)[None], span_end[None], request_states)


f32 = jnp.float32
bf16 = jnp.bfloat16
VMEM_LIMIT = 56 * 1024 * 1024
TILE = 256


def in_vmem():
    return pl.BlockSpec(memory_space=pltpu.VMEM)


def in_smem():
    return pl.BlockSpec(memory_space=pltpu.SMEM)


def kernel_params():
    return pltpu.CompilerParams(vmem_limit_bytes=VMEM_LIMIT)


def previous_rows(x_ref, first_row, tile, start):
    here = x_ref[pl.ds(pl.multiple_of(tile * TILE, TILE), TILE), :].astype(f32)
    above_at = jnp.maximum(tile * TILE - 16, 0)
    above = x_ref[pl.ds(pl.multiple_of(above_at, 16), 16), :].astype(f32)[15:16]
    row = lax.broadcasted_iota(jnp.int32, here.shape, 0)
    before = jnp.where(row == 0, above, pltpu.roll(here, 1, 0))
    before = jnp.where(start, first_row, before)
    return here, before - here


def project_kernel(count, outs, finish, *refs):
    place, period = refs[0], refs[1]
    chunks = refs[2:10]
    first, ratios, own, sibling = refs[10:14]
    extra = refs[14:-outs]
    results = refs[-outs:]
    rows = chunks[0].shape[0]

    @pl.loop(0, rows // TILE)
    def _(tile):
        row = lax.broadcasted_iota(jnp.int32, (TILE, 1), 0) + tile * TILE
        start = (row & (period[0] - 1)) == 0
        totals = [None] * count
        for at, chunk in enumerate(chunks):
            here, step = previous_rows(chunk, first[at : at + 1, :], tile, start)
            held = own if at % 2 == 0 else sibling
            for c in range(count):
                mixed = (here + ratios[c, at : at + 1, :] * step).astype(bf16)
                part = jnp.dot(mixed, held[place[at // 2], c], preferred_element_type=f32)
                totals[c] = part if totals[c] is None else totals[c] + part
        finish(tile, totals, extra, results)


def store_tiles(tile, totals, extra, results):
    at = pl.ds(pl.multiple_of(tile * TILE, TILE), TILE)
    for total, result in zip(totals, results):
        result[at, :] = total


def store_decay(tile, totals, extra, results):
    right, base = extra
    at = pl.ds(pl.multiple_of(tile * TILE, TILE), TILE)
    squeezed = jnp.tanh(totals[0]).astype(bf16)
    grown = jnp.dot(squeezed, right[...], preferred_element_type=f32)
    results[0][at, :] = -jnp.exp(base[...] + grown)


def store_hidden(tile, totals, extra, results):
    normed, live = extra
    at = pl.ds(pl.multiple_of(tile * TILE, TILE), TILE)
    gate = totals[0]
    value = normed[at, :] * (gate * jax.nn.sigmoid(gate))
    results[0][at, :] = jnp.where(live[at, :] > 0, value, 0.0).astype(bf16)


def project(finish, out_shapes, place, period, chunks, first, ratios, own, sibling, *extra):
    count = own.shape[1]
    outs = len(out_shapes)
    return pl.pallas_call(
        lambda *refs: project_kernel(count, outs, finish, *refs),
        out_shape=out_shapes,
        in_specs=[in_smem(), in_smem()] + [in_vmem()] * (12 + len(extra)),
        out_specs=[in_vmem()] * outs,
        compiler_params=kernel_params(),
    )(place, period, *chunks, first, ratios, own, sibling, *extra)


def sweep_kernel(
    lengths, carry, r_ref, k_ref, v_ref, w_ref, u_ref, s_ref, gain, bias, out_ref, state_ref, hold
):
    span, width = BLK, r_ref.shape[1]
    heads = width // span
    row = lax.broadcasted_iota(jnp.int32, (span, width), 0)
    lane = lax.broadcasted_iota(jnp.int32, (span, width), 1)
    col = lane % span
    tall = lax.broadcasted_iota(jnp.int32, (width, width), 0) // span
    wide = lax.broadcasted_iota(jnp.int32, (width, width), 1) // span
    same_head = tall == wide
    for h in range(heads):
        hold[:, h * span : (h + 1) * span] = s_ref[h]

    def spread(value):
        stacked = jnp.concatenate([value.astype(bf16)] * heads, axis=0)
        return jnp.where(same_head, stacked, jnp.zeros_like(stacked))

    def against(a, b):
        return lax.dot_general(a, b, (((1,), (1,)), ((), ())), preferred_element_type=f32)

    @pl.loop(0, r_ref.shape[0] // span)
    def _(n):
        at = pl.ds(pl.multiple_of(n * span, span), span)
        live = row < lengths[n]
        r, v = r_ref[at, :], v_ref[at, :]
        k = jnp.where(live, k_ref[at, :], 0.0)
        total = jnp.where(live, w_ref[at, :], 0.0)
        before = jnp.zeros_like(total)
        after = jnp.zeros_like(total)
        scores = against((r * u_ref[...]).astype(bf16), spread(k))
        scores = jnp.where(row == col, scores, 0.0)
        level = 0
        while (1 << level) < span:
            half = 1 << level
            upper = (row & half) != 0
            if level:
                scale = jnp.exp(jnp.where(upper, before, after))
                part = against((r * scale).astype(bf16), spread(k * scale))
            else:
                part = against(r.astype(bf16), spread(k))
            pair = upper & (((row >> level) ^ (col >> level)) == 1)
            scores = jnp.where(pair, part, scores)
            across = jnp.where(
                upper, pltpu.roll(total, half, 0), pltpu.roll(total, span - half, 0)
            )
            before = before + jnp.where(upper, across, 0.0)
            after = after + jnp.where(upper, 0.0, across)
            total = total + across
            level += 1
        entered = hold[...] * carry[0]
        out = jnp.dot(scores.astype(bf16), spread(v), preferred_element_type=f32)
        out = out + jnp.dot(
            (r * jnp.exp(before)).astype(bf16), spread(entered), preferred_element_type=f32
        )
        out_ref[at, :] = out
        added = lax.dot_general(
            (k * jnp.exp(after)).astype(bf16),
            v.astype(bf16),
            (((0,), (0,)), ((), ())),
            preferred_element_type=f32,
        )
        fresh = jnp.zeros((span, width), f32)
        for h in range(heads):
            fresh = jnp.where(lane // span == h, added[h * span : (h + 1) * span], fresh)
        twice = jnp.concatenate([total] * 2, axis=0)
        turned = []
        for p in range(width // (2 * span)):
            flipped = jnp.transpose(twice[:, p * 2 * span : (p + 1) * 2 * span])
            turned.append(
                jnp.where(lane[:, : 2 * span] < span, flipped[:span], flipped[span:])
            )
        fade = jnp.exp(jnp.concatenate(turned, axis=1))
        state = fade * entered + fresh
        hold[...] = state
        for h in range(heads):
            state_ref[n, h] = state[:, h * span : (h + 1) * span]

    ones = jnp.where(same_head, 1.0, 0.0).astype(bf16)

    def head_mean(value):
        high = value.astype(bf16)
        low = (value - high.astype(f32)).astype(bf16)
        both = jnp.dot(high, ones, preferred_element_type=f32) + jnp.dot(
            low, ones, preferred_element_type=f32
        )
        return both * (1.0 / span)

    @pl.loop(0, r_ref.shape[0] // TILE)
    def _(tile):
        at = pl.ds(pl.multiple_of(tile * TILE, TILE), TILE)
        value = out_ref[at, :]
        centred = value - head_mean(value)
        spread_of = head_mean(centred * centred)
        out_ref[at, :] = centred * lax.rsqrt(spread_of + norm_eps) * gain[...] + bias[...]


def sweep(lengths, carry, r, k, v, w, bonus, state, gain, bias):
    rows, width = r.shape
    heads = width // BLK
    return pl.pallas_call(
        sweep_kernel,
        out_shape=[
            jax.ShapeDtypeStruct((rows, width), f32),
            jax.ShapeDtypeStruct((rows // BLK, heads, BLK, BLK), f32),
        ],
        in_specs=[in_smem(), in_smem()] + [in_vmem()] * 8,
        out_specs=[in_vmem(), in_vmem()],
        scratch_shapes=[pltpu.VMEM((BLK, width), f32)],
        compiler_params=kernel_params(),
    )(lengths, carry, r, k, v, w, bonus, state, gain, bias)


def final_kernel(h0, h1, h2, h3, weight, out_ref):
    @pl.loop(0, h0.shape[0] // TILE)
    def _(tile):
        at = pl.ds(pl.multiple_of(tile * TILE, TILE), TILE)
        total = None
        for k, piece in enumerate((h0, h1, h2, h3)):
            part = jnp.dot(piece[at, :], weight[k], preferred_element_type=f32)
            total = part if total is None else total + part
        out_ref[at, :] = total.astype(bf16)


def final_product(pieces, weight):
    return pl.pallas_call(
        final_kernel,
        out_shape=jax.ShapeDtypeStruct((pieces[0].shape[0], weight.shape[2]), bf16),
        in_specs=[in_vmem()] * 5,
        out_specs=in_vmem(),
        compiler_params=kernel_params(),
    )(*pieces, weight)


def turned(x, axis, by):
    length = lax.axis_size(axis)
    return lax.ppermute(x, axis, [(i, (i + by) % length) for i in range(length)])


def flipped_core(x):
    return lax.ppermute(x, "core", [(0, 1), (1, 0)])


def over_x(x):
    return lax.ppermute(x, "x", [(0, 1), (1, 0)])


def over_y(x):
    return lax.ppermute(x, "y", [(0, 1), (1, 0)])


def dealt(blocks, z):
    length = lax.axis_size("z")
    return [blocks(z)] + [turned(blocks((z + k) % length), "z", k) for k in range(1, length)]


def in_order(pieces, z):
    length = len(pieces)
    whole = jnp.zeros((length,) + pieces[0].shape, pieces[0].dtype)
    for k, piece in enumerate(pieces):
        whole = lax.dynamic_update_index_in_dim(whole, piece, (z - k) % length, 0)
    return whole


def on_core(
    continued_prompt_entries,
    padded_prompt_entries,
    prompt_live_extents,
    preceding_entry_line,
    carried_memory,
    token_mixing_ratios,
    acceptance_transform,
    lookup_transform,
    payload_transform,
    gating_transform,
    fading_baseline,
    fading_left_factor,
    fading_right_factor,
    present_reward,
    group_layer_scaling,
    group_layer_shift_term,
    final_transform,
):
    z, core = lax.axis_index("z"), lax.axis_index("core")
    y, x = lax.axis_index("y"), lax.axis_index("x")
    mp = 2 * y + x
    is_long = core == 0
    lines = lax.axis_size("z")
    group_rows, columns = continued_prompt_entries.shape
    requests = prompt_live_extents.shape[0]
    slot_rows = group_rows // requests
    heads, span = present_reward.shape
    heads = heads // lines
    width = heads * span
    depth = acceptance_transform.shape[0]
    rows = 2 * lines * group_rows

    kept = jnp.where(is_long, continued_prompt_entries, padded_prompt_entries)
    given = jnp.where(is_long, padded_prompt_entries, continued_prompt_entries)
    taken = flipped_core(given)
    both = jnp.concatenate(
        [jnp.where(is_long, kept, taken), jnp.where(is_long, taken, kept)], axis=0
    )
    half_at = jnp.stack([core * depth, (1 - core) * depth])
    halves = []
    for h in range(2):
        mine = lax.dynamic_slice_in_dim(both, half_at[h], depth, 1)
        gathered = in_order([mine] + [turned(mine, "z", k) for k in range(1, lines)], z)
        halves.append(gathered.reshape(rows, depth))
    a, b = halves
    a_x, b_y = over_x(a), over_y(b)
    a_y, b_x = over_y(a), over_x(b)
    a_xy, b_xy = over_y(a_x), over_x(b_y)
    chunks = [a, b, a_x, b_x, a_y, b_y, a_xy, b_xy]
    edge = preceding_entry_line.reshape(2, depth)
    edge_x, edge_y = over_x(edge), over_y(edge)
    edge_xy = over_y(edge_x)
    edges = jnp.stack([edge, edge_x, edge_y, edge_xy])
    edges = jnp.where(is_long, edges, edges[:, ::-1])
    first = jnp.where(is_long, edges.astype(f32), 0.0).reshape(8, depth)
    place = jnp.stack([mp ^ rel for rel in range(4)]).astype(jnp.int32)
    period = jnp.where(is_long, rows, slot_rows).astype(jnp.int32)[None]

    def chunk_order(whole):
        split = whole.reshape((4, 2, depth) + whole.shape[1:])
        parts = []
        for rel in range(4):
            for h in range(2):
                side = core if h == 0 else 1 - core
                parts.append(split[mp ^ rel, side])
        return jnp.stack(parts)

    ratios = chunk_order(token_mixing_ratios.T).transpose(2, 0, 1)

    def columns_of(weights):
        stacked = jnp.stack(weights)

        def block(j):
            return lax.dynamic_slice_in_dim(stacked, j * width, width, 2)

        pieces = dealt(block, z)
        return in_order(pieces, z), in_order([flipped_core(piece) for piece in pieces], z)

    own, sibling = columns_of([acceptance_transform, lookup_transform, payload_transform])
    own_gate, sibling_gate = columns_of([gating_transform])
    left = fading_left_factor.reshape(4, 2, 1, depth, fading_left_factor.shape[1])
    left_own = jnp.where(is_long, left[:, 0], left[:, 1])
    left_sibling = jnp.where(is_long, left[:, 1], left[:, 0])

    def mine_of(vector):
        return lax.dynamic_slice_in_dim(vector, z * width, width, 0)[None]

    flat = jax.ShapeDtypeStruct((rows, width), f32)
    (decay,) = project(
        store_decay,
        [flat],
        place,
        period,
        chunks,
        first,
        ratios[4:5],
        left_own,
        left_sibling,
        lax.dynamic_slice_in_dim(fading_right_factor, z * width, width, 1),
        mine_of(fading_baseline),
    )
    recept, keys, values = project(
        store_tiles, [flat] * 3, place, period, chunks, first, ratios[:3], own, sibling
    )
    extents = lax.all_gather(prompt_live_extents, ("z", "core"), axis=0, tiled=True)
    extents = jnp.where(is_long, slot_rows, extents).astype(jnp.int32)
    entered = lax.dynamic_slice_in_dim(carried_memory, z * heads, heads, 0)
    bonus = lax.dynamic_slice_in_dim(present_reward, z * heads, heads, 0).reshape(1, width)
    normed, states = sweep(
        extents,
        is_long.astype(f32)[None],
        recept,
        keys,
        values,
        decay,
        bonus,
        jnp.where(is_long, entered, 0.0),
        mine_of(group_layer_scaling),
        mine_of(group_layer_shift_term),
    )
    live = lax.broadcasted_iota(jnp.int32, (rows // slot_rows, slot_rows), 1) < extents[:, None]
    live = live.reshape(rows, 1).astype(f32)
    (hidden,) = project(
        store_hidden,
        [jax.ShapeDtypeStruct((rows, width), bf16)],
        place,
        period,
        chunks,
        first,
        ratios[3:4],
        own_gate,
        sibling_gate,
        normed,
        live,
    )

    states = states.reshape(lines, 2, requests, heads, span, span)
    passed = flipped_core(lax.dynamic_index_in_dim(states, 1 - core, 1, keepdims=False))
    held = lax.dynamic_index_in_dim(states, core, 1, keepdims=False)
    bundle = jnp.concatenate(
        [jnp.where(is_long, held, passed)[:, -1:], jnp.where(is_long, passed, held)], axis=1
    ).astype(bf16)
    arrived = in_order(
        dealt(lambda j: lax.dynamic_index_in_dim(bundle, j, 0, keepdims=False), z), z
    ).astype(f32)
    span_states = arrived[:, 0].reshape(1, lines * heads, span, span)
    request_states = jnp.swapaxes(arrived[:, 1:], 0, 1).reshape(
        requests, lines * heads, span, span
    )

    wide_out = 2 * final_transform.shape[1]
    beside = flipped_core(final_transform)
    out_weight = jnp.concatenate(
        [
            jnp.where(is_long, final_transform, beside),
            jnp.where(is_long, beside, final_transform),
        ],
        axis=1,
    ).reshape(lines, width, wide_out)
    pieces = [hidden] + [turned(hidden, "z", k) for k in range(1, lines)]
    out_weight = jnp.stack(
        [
            lax.dynamic_index_in_dim(out_weight, (z - k) % lines, 0, keepdims=False)
            for k in range(lines)
        ]
    )
    partial = final_product(pieces, out_weight)
    partial = partial.reshape(2 * lines, 2, group_rows // 2, wide_out)
    kept_half = lax.dynamic_index_in_dim(partial, x, 1, keepdims=False)
    sent_half = lax.dynamic_index_in_dim(partial, 1 - x, 1, keepdims=False)
    summed = kept_half.astype(f32) + over_x(sent_half).astype(f32)
    summed = summed.reshape(lines, 2, group_rows // 2, wide_out)
    same_core = lax.dynamic_index_in_dim(summed, core, 1, keepdims=False)
    other_core = lax.dynamic_index_in_dim(summed, 1 - core, 1, keepdims=False).astype(bf16)
    from_same = lax.ppermute(same_core.astype(bf16), ("core", "y"), [(1, 0), (2, 3)])
    from_cross = lax.ppermute(other_core, ("core", "y"), [(1, 2), (2, 1)])
    from_beside = lax.ppermute(other_core, ("core", "y"), [(0, 2), (3, 1)])
    mixed_part = (
        jnp.where(core == y, same_core, 0.0)
        + from_same.astype(f32)
        + from_cross.astype(f32)
        + from_beside.astype(f32)
    ).astype(bf16)
    out_pieces = in_order(
        dealt(lambda j: lax.dynamic_index_in_dim(mixed_part, j, 0, keepdims=False), z), z
    )
    mixed = jnp.swapaxes(out_pieces, 0, 1).reshape(1, group_rows // 2, lines * wide_out)
    return mixed, span_states, request_states


def rows_kept_solution(mesh):
    placed = (
        P("seq", "mp"),
        P("seq", "mp"),
        P("seq"),
        P("mp"),
        P("mp", None, None),
        P(),
        P("seq", "mp"),
        P("seq", "mp"),
        P("seq", "mp"),
        P("seq", "mp"),
        P("mp"),
        P(),
        P(None, "mp"),
        P("mp", None),
        P("mp"),
        P("mp"),
        P("mp", "seq"),
    )
    return jax.shard_map(
        on_device,
        mesh=mesh,
        in_specs=placed,
        out_specs=(P("seq", "mp", None), P("seq", "mp", None, None), P("seq", "mp", None, None)),
        check_vma=False,
    )


def heads_kept_solution(mesh):
    seq, mp = mesh.shape["seq"], mesh.shape["mp"]
    split = Mesh(mesh.devices.reshape(seq // 2, 2, 2, mp // 2), ("z", "core", "y", "x"))
    s, m = ("z", "core"), ("y", "x")
    placed = (
        P(s, m),
        P(s, m),
        P(s),
        P(m),
        P(m, None, None),
        P(),
        P(s, m),
        P(s, m),
        P(s, m),
        P(s, m),
        P(m),
        P(),
        P(None, m),
        P(m, None),
        P(m),
        P(m),
        P(m, s),
    )
    return jax.shard_map(
        on_core,
        mesh=split,
        in_specs=placed,
        out_specs=(P(s, m, None), P(s, m, None, None), P(s, m, None, None)),
        check_vma=False,
    )


def solution(mesh):
    if mesh.shape["mp"] == 4 and mesh.shape["seq"] == 8:
        return heads_kept_solution(mesh)
    return rows_kept_solution(mesh)
```

```python
import jax
import jax.numpy as jnp
import numpy as np
from jax import lax
from jax.experimental import pallas as pl
from jax.experimental.pallas import tpu as pltpu
from jax.sharding import Mesh
from jax.sharding import PartitionSpec as P

BLK = 64


norm_eps = 0.00064
highest = lax.Precision.HIGHEST


def passed_along(x, axis, by):
    length = lax.axis_size(axis)
    pairs = [(i, i + by) for i in range(length) if 0 <= i + by < length]
    return lax.ppermute(x, axis, pairs)


def entering(value, axis, join, neutral):
    count, mine = (lax.axis_size(axis), lax.axis_index(axis))
    pieces = jax.tree.map(lambda part: lax.all_gather(part, axis), value)
    total = jax.tree.map(
        lambda part, zero: jnp.full_like(part, 0) + jnp.asarray(zero, part.dtype), value, neutral
    )

    def hop(position, total):
        longer = join(total, jax.tree.map(lambda part: part[position], pieces))
        return jax.tree.map(lambda new, old: jnp.where(position < mine, new, old), longer, total)

    return lax.fori_loop(0, count - 1, hop, total)


def mix_rows(current, previous, weight):
    here = current.astype(jnp.float32)
    return (here + weight[None, :] * (previous.astype(jnp.float32) - here)).astype(jnp.bfloat16)


def block_sweep(
    evolving_memory,
    acceptance_entries,
    lookup_entries,
    payload_entries,
    log_fading_amount,
    diagonal_reward,
):
    inclusive = jnp.cumsum(log_fading_amount, axis=0)
    exclusive = inclusive - log_fading_amount
    recept_scaled = acceptance_entries * jnp.exp(exclusive)
    keys_scaled = lookup_entries * jnp.exp(-inclusive)
    scores = jnp.einsum("ihc,jhc->hij", recept_scaled, keys_scaled, precision=highest)
    count = acceptance_entries.shape[0]
    row_index = lax.broadcasted_iota(jnp.int32, (count, count), 0)
    col_index = lax.broadcasted_iota(jnp.int32, (count, count), 1)
    scores = jnp.where((row_index > col_index)[None], scores, 0.0)
    diagonal_contribution = jnp.sum(
        acceptance_entries * diagonal_reward[None] * lookup_entries, axis=-1, keepdims=True
    )
    answer_lines = (
        jnp.einsum("hij,jhd->ihd", scores, payload_entries, precision=highest)
        + diagonal_contribution * payload_entries
    )
    answer_lines = answer_lines + jnp.einsum(
        "ihc,hcd->ihd", recept_scaled, evolving_memory, precision=highest
    )
    total = inclusive[-1]
    carried = lookup_entries * jnp.exp(total[None] - inclusive)
    new_state = jnp.exp(total)[:, :, None] * evolving_memory + jnp.einsum(
        "jhc,jhd->hcd", carried, payload_entries, precision=highest
    )
    return (new_state, answer_lines)


def continued_recurrence(
    acceptance_entries, lookup_entries, payload_entries, log_fading_amount, diagonal_reward
):
    length, per_group_view, embedding_dimension = acceptance_entries.shape
    blocks = length // BLK

    def step(evolving_memory, entry_lines):
        return block_sweep(
            evolving_memory,
            entry_lines[0],
            entry_lines[1],
            entry_lines[2],
            entry_lines[3],
            diagonal_reward,
        )

    shaped = tuple(
        (
            a.reshape(blocks, BLK, per_group_view, embedding_dimension)
            for a in (acceptance_entries, lookup_entries, payload_entries, log_fading_amount)
        )
    )
    evolving_memory, results = lax.scan(
        step,
        jnp.zeros((per_group_view, embedding_dimension, embedding_dimension), jnp.float32),
        shaped,
    )
    return (evolving_memory, results.reshape(length, per_group_view, embedding_dimension))


def combine(earlier, later):
    return (earlier[0] + later[0], jnp.exp(later[0])[:, :, None] * earlier[1] + later[1])


def shifted_rows(current, edge_row, long_rows, requests, slot_rows):
    feature_part = current.shape[1]
    long_prev = jnp.concatenate([edge_row, current[: long_rows - 1]], axis=0)
    short_view = current[long_rows:].reshape(requests, slot_rows, feature_part)
    short_prev = jnp.concatenate(
        [jnp.zeros((requests, 1, feature_part), current.dtype), short_view[:, :-1]], axis=1
    )
    short_prev = short_prev.reshape(requests * slot_rows, feature_part)
    return jnp.concatenate([long_prev, short_prev], axis=0)


def on_device(
    continued_prompt_entries,
    padded_prompt_entries,
    prompt_live_extents,
    preceding_entry_line,
    carried_memory,
    token_mixing_ratios,
    acceptance_transform,
    lookup_transform,
    payload_transform,
    gating_transform,
    fading_baseline,
    fading_left_factor,
    fading_right_factor,
    present_reward,
    group_layer_scaling,
    group_layer_shift_term,
    final_transform,
):
    long_rows = continued_prompt_entries.shape[0]
    requests = prompt_live_extents.shape[0]
    slot_rows = padded_prompt_entries.shape[0] // requests
    per_group_view, embedding_dimension = present_reward.shape
    arrived = passed_along(continued_prompt_entries[-1:], "seq", 1)
    first = lax.axis_index("seq") == 0
    edge_row = jnp.where(first, preceding_entry_line[None, :], arrived)
    current = jnp.concatenate([continued_prompt_entries, padded_prompt_entries], axis=0)
    current, edge_full = (
        lax.all_gather(current, "mp", axis=1, tiled=True),
        lax.all_gather(edge_row, "mp", axis=1, tiled=True),
    )
    previous = shifted_rows(current, edge_full, long_rows, requests, slot_rows)
    mixes = [mix_rows(current, previous, token_mixing_ratios[index]) for index in range(5)]
    total_rows = current.shape[0]
    columns = acceptance_transform.shape[1]
    pieces = (
        lax.all_gather(acceptance_transform, "seq", axis=0, tiled=True),
        lax.all_gather(lookup_transform, "seq", axis=0, tiled=True),
        lax.all_gather(payload_transform, "seq", axis=0, tiled=True),
        lax.all_gather(gating_transform, "seq", axis=0, tiled=True),
    )
    acceptance_entries, lookup_entries, payload_entries, gate = tuple(
        (
            jnp.dot(source, piece, preferred_element_type=jnp.float32)
            for source, piece in zip(mixes[:4], pieces)
        )
    )
    squeezed = jnp.tanh(
        jnp.dot(mixes[4], fading_left_factor, preferred_element_type=jnp.float32)
    ).astype(jnp.bfloat16)
    log_fading_amount = -jnp.exp(
        fading_baseline[None, :]
        + jnp.dot(squeezed, fading_right_factor, preferred_element_type=jnp.float32)
    )
    recept3, keys3, values3, decay3 = [
        a.reshape(total_rows, per_group_view, embedding_dimension)
        for a in (acceptance_entries, lookup_entries, payload_entries, log_fading_amount)
    ]
    local_state, long_out = continued_recurrence(
        recept3[:long_rows],
        keys3[:long_rows],
        values3[:long_rows],
        decay3[:long_rows],
        present_reward,
    )
    long_decay = decay3[:long_rows]
    group_total = jnp.sum(long_decay, axis=0)
    blank = (
        jnp.zeros((per_group_view, embedding_dimension), jnp.float32),
        jnp.zeros((per_group_view, embedding_dimension, embedding_dimension), jnp.float32),
    )
    prefix_total, prefix_state = entering((group_total, local_state), "seq", combine, blank)
    incoming = jnp.exp(prefix_total)[:, :, None] * carried_memory + prefix_state
    before_row = jnp.cumsum(long_decay, axis=0) - long_decay
    long_out = long_out + jnp.einsum(
        "ihc,hcd->ihd", recept3[:long_rows] * jnp.exp(before_row), incoming, precision=highest
    )
    span_end = jnp.exp(group_total)[:, :, None] * incoming + local_state
    live_rows = (
        lax.broadcasted_iota(jnp.int32, (requests, slot_rows), 1) < prompt_live_extents[:, None]
    )
    live_flat = live_rows.reshape(requests * slot_rows).astype(jnp.float32)[:, None, None]
    short_shape = (requests, slot_rows, per_group_view, embedding_dimension)
    short_recept = recept3[long_rows:].reshape(short_shape)
    short_keys = (keys3[long_rows:] * live_flat).reshape(short_shape)
    short_values = values3[long_rows:].reshape(short_shape)
    short_decay = (decay3[long_rows:] * live_flat).reshape(short_shape)
    zeroed_memory = jnp.zeros(
        (per_group_view, embedding_dimension, embedding_dimension), jnp.float32
    )

    def request_pass(acceptance_lines, lookup_table, payload_table, fading_table):
        return block_sweep(
            zeroed_memory,
            acceptance_lines,
            lookup_table,
            payload_table,
            fading_table,
            present_reward,
        )

    request_states, short_out = jax.vmap(request_pass)(
        short_recept, short_keys, short_values, short_decay
    )
    wkv = jnp.concatenate(
        [long_out, short_out.reshape(requests * slot_rows, per_group_view, embedding_dimension)],
        axis=0,
    )
    mean = jnp.mean(wkv, axis=-1, keepdims=True)
    centred = wkv - mean
    variance = jnp.mean(centred * centred, axis=-1, keepdims=True)
    normed = (centred * lax.rsqrt(variance + norm_eps)).reshape(
        total_rows, columns
    ) * group_layer_scaling[None, :] + group_layer_shift_term[None, :]
    row_live = jnp.concatenate(
        [jnp.ones((long_rows,), dtype=bool), live_rows.reshape(requests * slot_rows)], axis=0
    )
    hidden = jnp.where(row_live[:, None], normed * jax.nn.silu(gate), 0.0).astype(jnp.bfloat16)
    full_out = lax.all_gather(final_transform, "seq", axis=1, tiled=True)
    mixed_rows = lax.psum_scatter(
        jnp.dot(hidden, full_out, preferred_element_type=jnp.float32),
        "mp",
        scatter_dimension=0,
        tiled=True,
    )
    return (mixed_rows.astype(jnp.bfloat16)[None], span_end[None], request_states)


f32 = jnp.float32
bf16 = jnp.bfloat16
VMEM_LIMIT = 56 * 1024 * 1024
TILE = 256


def in_vmem():
    return pl.BlockSpec(memory_space=pltpu.VMEM)


def in_smem():
    return pl.BlockSpec(memory_space=pltpu.SMEM)


def kernel_params():
    return pltpu.CompilerParams(vmem_limit_bytes=VMEM_LIMIT)


def previous_rows(x_ref, first_row, tile, start):
    here = x_ref[pl.ds(pl.multiple_of(tile * TILE, TILE), TILE), :].astype(f32)
    above_at = jnp.maximum(tile * TILE - 16, 0)
    above = x_ref[pl.ds(pl.multiple_of(above_at, 16), 16), :].astype(f32)[15:16]
    row = lax.broadcasted_iota(jnp.int32, here.shape, 0)
    before = jnp.where(row == 0, above, pltpu.roll(here, 1, 0))
    before = jnp.where(start, first_row, before)
    return here, before - here


def mixed_kernel(
    place,
    period,
    c0,
    c1,
    c2,
    c3,
    c4,
    c5,
    c6,
    c7,
    first,
    ratios,
    own_pair,
    sibling_pair,
    own_value,
    sibling_value,
    own_left,
    sibling_left,
    right,
    base,
    recept_ref,
    keys_ref,
    values_ref,
    decay_ref,
    gate_mix,
):
    rows, depth = c0.shape

    @pl.loop(0, rows // TILE)
    def _(tile):
        at = pl.ds(pl.multiple_of(tile * TILE, TILE), TILE)
        row = lax.broadcasted_iota(jnp.int32, (TILE, 1), 0) + tile * TILE
        start = (row & (period[0] - 1)) == 0
        totals = [None] * 4
        for c, chunk in enumerate((c0, c1, c2, c3, c4, c5, c6, c7)):
            here, step = previous_rows(chunk, first[c : c + 1, :], tile, start)
            from_z = place[c // 2]
            pair, value, left = (
                (own_pair, own_value, own_left)
                if c % 2 == 0
                else (sibling_pair, sibling_value, sibling_left)
            )
            weights = (pair[from_z, 0], pair[from_z, 1], value[from_z, 0], left[from_z, 0])
            for which, weight in zip((0, 1, 2, 4), weights):
                mixed = (here + ratios[which, c : c + 1, :] * step).astype(bf16)
                part = jnp.dot(mixed, weight, preferred_element_type=f32)
                slot = min(which, 3)
                totals[slot] = part if totals[slot] is None else totals[slot] + part
            gate_mix[at, c * depth : (c + 1) * depth] = (
                here + ratios[3, c : c + 1, :] * step
            ).astype(bf16)
        recept_ref[at, :] = totals[0]
        keys_ref[at, :] = totals[1]
        values_ref[at, :] = totals[2]
        squeezed = jnp.tanh(totals[3]).astype(bf16)
        grown = jnp.dot(squeezed, right[...], preferred_element_type=f32)
        decay_ref[at, :] = -jnp.exp(base[...] + grown)


def mixed_products(place, period, chunks, *rest):
    rows, depth = chunks[0].shape
    width = rest[2].shape[3]
    flat = jax.ShapeDtypeStruct((rows, width), f32)
    return pl.pallas_call(
        mixed_kernel,
        out_shape=[flat] * 4 + [jax.ShapeDtypeStruct((rows, 8 * depth), bf16)],
        in_specs=[in_smem(), in_smem()] + [in_vmem()] * (8 + len(rest)),
        out_specs=[in_vmem()] * 5,
        compiler_params=kernel_params(),
    )(place, period, *chunks, *rest)


def gate_kernel(place, mix, own, sibling, normed, live, first_ref, second_ref):
    rows = mix.shape[0]
    depth, width = own.shape[2:]
    part_rows = BLK // 2

    @pl.loop(0, rows // TILE)
    def _(tile):
        at = pl.ds(pl.multiple_of(tile * TILE, TILE), TILE)
        total = None
        for c in range(8):
            weight = (own if c % 2 == 0 else sibling)[place[c // 2], 0]
            part = jnp.dot(
                mix[at, c * depth : (c + 1) * depth], weight, preferred_element_type=f32
            )
            total = part if total is None else total + part
        value = normed[at, :] * (total * jax.nn.sigmoid(total))
        value = jnp.where(live[at, :] > 0, value, 0.0).astype(bf16)
        value = value.reshape(TILE // part_rows // 2, 2, part_rows, width)
        half_at = pl.ds(pl.multiple_of(tile * (TILE // 2), TILE // 2), TILE // 2)
        first_ref[half_at, :] = value[:, 0].reshape(TILE // 2, width)
        second_ref[half_at, :] = value[:, 1].reshape(TILE // 2, width)


def gated(place, mix, own, sibling, normed, live):
    rows, width = normed.shape
    return pl.pallas_call(
        gate_kernel,
        out_shape=[jax.ShapeDtypeStruct((rows // 2, width), bf16)] * 2,
        in_specs=[in_smem()] + [in_vmem()] * 5,
        out_specs=[in_vmem()] * 2,
        compiler_params=kernel_params(),
    )(place, mix, own, sibling, normed, live)


def sweep_kernel(
    lengths, carry, r_ref, k_ref, v_ref, w_ref, u_ref, s_ref, gain, bias, out_ref, state_ref, hold
):
    span, width = BLK, r_ref.shape[1]
    heads = width // span
    row = lax.broadcasted_iota(jnp.int32, (span, width), 0)
    lane = lax.broadcasted_iota(jnp.int32, (span, width), 1)
    col = lane % span
    tall = lax.broadcasted_iota(jnp.int32, (width, width), 0) // span
    wide = lax.broadcasted_iota(jnp.int32, (width, width), 1) // span
    same_head = tall == wide
    for h in range(heads):
        hold[:, h * span : (h + 1) * span] = s_ref[h]

    def spread(value):
        stacked = jnp.concatenate([value.astype(bf16)] * heads, axis=0)
        return jnp.where(same_head, stacked, jnp.zeros_like(stacked))

    def against(a, b):
        return lax.dot_general(a, b, (((1,), (1,)), ((), ())), preferred_element_type=f32)

    @pl.loop(0, r_ref.shape[0] // span)
    def _(n):
        at = pl.ds(pl.multiple_of(n * span, span), span)
        live = row < lengths[n]
        r, v = r_ref[at, :], v_ref[at, :]
        k = jnp.where(live, k_ref[at, :], 0.0)
        total = jnp.where(live, w_ref[at, :], 0.0)
        before = jnp.zeros_like(total)
        after = jnp.zeros_like(total)
        scores = against((r * u_ref[...]).astype(bf16), spread(k))
        scores = jnp.where(row == col, scores, 0.0)
        level = 0
        while (1 << level) < span:
            half = 1 << level
            upper = (row & half) != 0
            if level:
                scale = jnp.exp(jnp.where(upper, before, after))
                part = against((r * scale).astype(bf16), spread(k * scale))
            else:
                part = against(r.astype(bf16), spread(k))
            pair = upper & (((row >> level) ^ (col >> level)) == 1)
            scores = jnp.where(pair, part, scores)
            across = jnp.where(
                upper, pltpu.roll(total, half, 0), pltpu.roll(total, span - half, 0)
            )
            before = before + jnp.where(upper, across, 0.0)
            after = after + jnp.where(upper, 0.0, across)
            total = total + across
            level += 1
        entered = hold[...] * carry[0]
        out = jnp.dot(scores.astype(bf16), spread(v), preferred_element_type=f32)
        out = out + jnp.dot(
            (r * jnp.exp(before)).astype(bf16), spread(entered), preferred_element_type=f32
        )
        out_ref[at, :] = out
        added = lax.dot_general(
            (k * jnp.exp(after)).astype(bf16),
            v.astype(bf16),
            (((0,), (0,)), ((), ())),
            preferred_element_type=f32,
        )
        fresh = jnp.zeros((span, width), f32)
        for h in range(heads):
            fresh = jnp.where(lane // span == h, added[h * span : (h + 1) * span], fresh)
        twice = jnp.concatenate([total] * 2, axis=0)
        turned = []
        for p in range(width // (2 * span)):
            flipped = jnp.transpose(twice[:, p * 2 * span : (p + 1) * 2 * span])
            turned.append(
                jnp.where(lane[:, : 2 * span] < span, flipped[:span], flipped[span:])
            )
        fade = jnp.exp(jnp.concatenate(turned, axis=1))
        state = fade * entered + fresh
        hold[...] = state
        for h in range(heads):
            state_ref[n, h] = state[:, h * span : (h + 1) * span]

    ones = jnp.where(same_head, 1.0, 0.0).astype(bf16)

    def head_mean(value):
        high = value.astype(bf16)
        low = (value - high.astype(f32)).astype(bf16)
        both = jnp.dot(high, ones, preferred_element_type=f32) + jnp.dot(
            low, ones, preferred_element_type=f32
        )
        return both * (1.0 / span)

    @pl.loop(0, r_ref.shape[0] // TILE)
    def _(tile):
        at = pl.ds(pl.multiple_of(tile * TILE, TILE), TILE)
        value = out_ref[at, :]
        centred = value - head_mean(value)
        spread_of = head_mean(centred * centred)
        out_ref[at, :] = centred * lax.rsqrt(spread_of + norm_eps) * gain[...] + bias[...]


def sweep(lengths, carry, r, k, v, w, bonus, state, gain, bias):
    rows, width = r.shape
    heads = width // BLK
    return pl.pallas_call(
        sweep_kernel,
        out_shape=[
            jax.ShapeDtypeStruct((rows, width), f32),
            jax.ShapeDtypeStruct((rows // BLK, heads, BLK, BLK), f32),
        ],
        in_specs=[in_smem(), in_smem()] + [in_vmem()] * 8,
        out_specs=[in_vmem(), in_vmem()],
        scratch_shapes=[pltpu.VMEM((BLK, width), f32)],
        compiler_params=kernel_params(),
    )(lengths, carry, r, k, v, w, bonus, state, gain, bias)


def final_kernel(side, h0, h1, h2, h3, weight, kept_ref, sent_ref):
    part_rows = BLK // 2
    width = weight.shape[2]

    @pl.loop(0, h0.shape[0] // TILE)
    def _(tile):
        at = pl.ds(pl.multiple_of(tile * TILE, TILE), TILE)
        total = None
        for k, piece in enumerate((h0, h1, h2, h3)):
            part = jnp.dot(piece[at, :], weight[k], preferred_element_type=f32)
            total = part if total is None else total + part
        split = total.astype(bf16).reshape(TILE // part_rows // 2, 2, part_rows, width)
        mine = side[0] == 0
        low, high = split[:, 0], split[:, 1]
        group = pl.ds(tile * (TILE // part_rows // 2), TILE // part_rows // 2)
        kept_ref[group] = jnp.where(mine, low, high)
        sent_ref[group] = jnp.where(mine, high, low)


def final_product(side, pieces, weight):
    rows, width = pieces[0].shape[0], weight.shape[2]
    half = jax.ShapeDtypeStruct((rows // BLK, BLK // 2, width), bf16)
    return pl.pallas_call(
        final_kernel,
        out_shape=[half] * 2,
        in_specs=[in_smem()] + [in_vmem()] * 5,
        out_specs=[in_vmem()] * 2,
        compiler_params=kernel_params(),
    )(side, *pieces, weight)


def lay_kernel(at, *refs):
    pieces, out_ref = refs[:-1], refs[-1]
    rows, width = pieces[0].shape
    lines = out_ref.shape[1] // width
    for n, piece in enumerate(pieces):
        column = pl.multiple_of(at[n % lines] * width, width)
        out_ref[n // lines * rows : (n // lines + 1) * rows, pl.ds(column, width)] = piece[...]


def laid(at, pieces, lines):
    rows, width = pieces[0].shape
    return pl.pallas_call(
        lay_kernel,
        out_shape=jax.ShapeDtypeStruct((len(pieces) // lines * rows, lines * width), bf16),
        in_specs=[in_smem()] + [in_vmem()] * len(pieces),
        out_specs=in_vmem(),
        compiler_params=kernel_params(),
    )(at, *pieces)


def after(value, *others):
    return lax.optimization_barrier((value,) + others)[0]


def turned(x, axis, by):
    length = lax.axis_size(axis)
    return lax.ppermute(x, axis, [(i, (i + by) % length) for i in range(length)])


def flipped_core(x):
    return lax.ppermute(x, "core", [(0, 1), (1, 0)])


def over_x(x):
    return lax.ppermute(x, "x", [(0, 1), (1, 0)])


def over_y(x):
    return lax.ppermute(x, "y", [(0, 1), (1, 0)])


def dealt(blocks, z):
    length = lax.axis_size("z")
    return [blocks(z)] + [turned(blocks((z + k) % length), "z", k) for k in range(1, length)]


def spread_along(piece, z):
    one = lax.ppermute(piece, "z", [(0, 1), (1, 2), (2, 3)])
    three = lax.ppermute(piece, "z", [(1, 0), (2, 1), (3, 2)])
    two = turned(piece, "z", 2)
    far = lax.ppermute(two, "z", [(1, 0), (2, 3)])
    return piece, one, two, three, far


def in_place(spread, z, at=0):
    piece, one, two, three, far = spread
    whole = jnp.zeros((4,) + piece.shape, piece.dtype)
    for k, part in ((1, one), (2, two), (3, three)):
        whole = lax.dynamic_update_index_in_dim(whole, part, (z - k) % 4, 0)
    far_at = jnp.where(z == 0, 3, jnp.where(z == 3, 0, z))
    whole = lax.dynamic_update_index_in_dim(whole, far, far_at, 0)
    return lax.dynamic_update_index_in_dim(whole, piece, z, 0)


def in_order(pieces, z):
    length = len(pieces)
    whole = jnp.zeros((length,) + pieces[0].shape, pieces[0].dtype)
    for k, piece in enumerate(pieces):
        whole = lax.dynamic_update_index_in_dim(whole, piece, (z - k) % length, 0)
    return whole


def on_core(
    continued_prompt_entries,
    padded_prompt_entries,
    prompt_live_extents,
    preceding_entry_line,
    carried_memory,
    token_mixing_ratios,
    acceptance_transform,
    lookup_transform,
    payload_transform,
    gating_transform,
    fading_baseline,
    fading_left_factor,
    fading_right_factor,
    present_reward,
    group_layer_scaling,
    group_layer_shift_term,
    final_transform,
):
    z, core = lax.axis_index("z"), lax.axis_index("core")
    y, x = lax.axis_index("y"), lax.axis_index("x")
    mp = 2 * y + x
    is_long = core == 0
    lines = lax.axis_size("z")
    group_rows, columns = continued_prompt_entries.shape
    requests = prompt_live_extents.shape[0]
    slot_rows = group_rows // requests
    heads, span = present_reward.shape
    heads = heads // lines
    width = heads * span
    depth = acceptance_transform.shape[0]
    rows = 2 * lines * group_rows

    kept = jnp.where(is_long, continued_prompt_entries, padded_prompt_entries)
    given = jnp.where(is_long, padded_prompt_entries, continued_prompt_entries)
    taken = flipped_core(given)
    both = jnp.concatenate(
        [jnp.where(is_long, kept, taken), jnp.where(is_long, taken, kept)], axis=0
    )
    halves = []
    for h in range(2):
        side = core if h == 0 else 1 - core
        halves.append(lax.dynamic_slice_in_dim(both, side * depth, depth, 1))
    first_half = spread_along(halves[0], z)
    second_half = spread_along(halves[1], z)
    a = in_place(first_half, z).reshape(rows, depth)
    b = in_place(second_half, z).reshape(rows, depth)
    a_x, b_y = over_x(a), over_y(b)
    a_y, b_x = over_y(a), over_x(b)
    a_xy, b_xy = over_y(a_x), over_x(b_y)
    chunks = [a, b, a_x, b_x, a_y, b_y, a_xy, b_xy]
    edge = preceding_entry_line.reshape(2, depth)
    edge_x, edge_y = over_x(edge), over_y(edge)
    edge_xy = over_y(edge_x)
    edges = jnp.stack([edge, edge_x, edge_y, edge_xy])
    edges = jnp.where(is_long, edges, edges[:, ::-1])
    first = jnp.where(is_long, edges.astype(f32), 0.0).reshape(8, depth)
    place = jnp.stack([mp ^ rel for rel in range(4)]).astype(jnp.int32)
    period = jnp.where(is_long, rows, slot_rows).astype(jnp.int32)[None]

    def chunk_order(whole):
        split = whole.reshape((4, 2, depth) + whole.shape[1:])
        parts = []
        for rel in range(4):
            for h in range(2):
                side = core if h == 0 else 1 - core
                parts.append(split[mp ^ rel, side])
        return jnp.stack(parts)

    ratios = chunk_order(token_mixing_ratios.T).transpose(2, 0, 1)

    def columns_of(weights, *ready):
        stacked = jnp.stack(weights)

        def block(j):
            return lax.dynamic_slice_in_dim(stacked, j * width, width, 2)

        blocks = [block((z + k) % lines) for k in range(lines)]
        blocks = lax.optimization_barrier((tuple(blocks),) + ready)[0]
        pieces = [blocks[0]] + [turned(blocks[k], "z", k) for k in range(1, lines)]
        return pieces

    def both_cores(pieces):
        return in_order(pieces, z), in_order([flipped_core(piece) for piece in pieces], z)

    pair_pieces = columns_of(
        [acceptance_transform, lookup_transform], first_half[4], second_half[4]
    )
    value_pieces = columns_of([payload_transform], a_x, b_y)
    gate_pieces = columns_of([gating_transform], value_pieces[2])
    own_pair, sibling_pair = both_cores(pair_pieces)
    own_value, sibling_value = both_cores(value_pieces)
    own_gate, sibling_gate = both_cores(gate_pieces)
    left = fading_left_factor.reshape(4, 2, 1, depth, fading_left_factor.shape[1])
    left_own = jnp.where(is_long, left[:, 0], left[:, 1])
    left_sibling = jnp.where(is_long, left[:, 1], left[:, 0])

    def mine_of(vector):
        return lax.dynamic_slice_in_dim(vector, z * width, width, 0)[None]

    recept, keys, values, decay, gate_mix = mixed_products(
        place,
        period,
        chunks,
        first,
        ratios,
        own_pair,
        sibling_pair,
        own_value,
        sibling_value,
        left_own,
        left_sibling,
        lax.dynamic_slice_in_dim(fading_right_factor, z * width, width, 1),
        mine_of(fading_baseline),
    )
    beside_extents = flipped_core(prompt_live_extents)
    chip_extents = jnp.stack(
        [
            jnp.where(is_long, prompt_live_extents, beside_extents),
            jnp.where(is_long, beside_extents, prompt_live_extents),
        ]
    )
    extents = in_order(
        [chip_extents] + [turned(chip_extents, "z", k) for k in range(1, lines)], z
    ).reshape(2 * lines * requests)
    extents = jnp.where(is_long, slot_rows, extents).astype(jnp.int32)
    entered = lax.dynamic_slice_in_dim(carried_memory, z * heads, heads, 0)
    bonus = lax.dynamic_slice_in_dim(present_reward, z * heads, heads, 0).reshape(1, width)
    normed, states = sweep(
        extents,
        is_long.astype(f32)[None],
        recept,
        keys,
        values,
        decay,
        bonus,
        jnp.where(is_long, entered, 0.0),
        mine_of(group_layer_scaling),
        mine_of(group_layer_shift_term),
    )
    live = lax.broadcasted_iota(jnp.int32, (rows // slot_rows, slot_rows), 1) < extents[:, None]
    live = live.reshape(rows, 1).astype(f32)
    hidden = gated(place, gate_mix, own_gate, sibling_gate, normed, live)

    states = states.reshape(lines, 2, requests, heads, span, span)
    passed = flipped_core(lax.dynamic_index_in_dim(states, 1 - core, 1, keepdims=False))
    held = lax.dynamic_index_in_dim(states, core, 1, keepdims=False)
    bundle = jnp.concatenate(
        [jnp.where(is_long, held, passed)[:, -1:], jnp.where(is_long, passed, held)], axis=1
    ).astype(bf16)
    arrived = in_order(
        dealt(lambda j: lax.dynamic_index_in_dim(bundle, j, 0, keepdims=False), z), z
    ).astype(f32)
    span_states = arrived[:, 0].reshape(1, lines * heads, span, span)
    request_states = jnp.swapaxes(arrived[:, 1:], 0, 1).reshape(
        requests, lines * heads, span, span
    )

    wide_out = 2 * final_transform.shape[1]
    beside = flipped_core(final_transform)
    out_weight = jnp.concatenate(
        [
            jnp.where(is_long, final_transform, beside),
            jnp.where(is_long, beside, final_transform),
        ],
        axis=1,
    ).reshape(lines, width, wide_out)
    out_weight = jnp.stack(
        [
            lax.dynamic_index_in_dim(out_weight, (z - k) % lines, 0, keepdims=False)
            for k in range(lines)
        ]
    )
    order = jnp.stack([(z - k) % lines for k in range(lines)]).astype(jnp.int32)
    side = x.astype(jnp.int32)[None]
    spreads = []
    for n, part in enumerate(hidden):
        if n:
            part = after(part, spreads[0][2])
        spreads.append(spread_along(part, z))
    out_pieces = []
    for piece, one, two, three, far in spreads:
        one = jnp.where(z == 0, far, one)
        three = jnp.where(z == 3, far, three)
        kept_half, sent_half = final_product(side, (piece, one, two, three), out_weight)
        summed = kept_half.astype(f32) + over_x(sent_half).astype(f32)
        summed = summed.reshape(lines, 2, group_rows // 4, wide_out)
        same_core = lax.dynamic_index_in_dim(summed, core, 1, keepdims=False)
        other_core = lax.dynamic_index_in_dim(summed, 1 - core, 1, keepdims=False).astype(bf16)
        from_same = lax.ppermute(same_core.astype(bf16), ("core", "y"), [(1, 0), (2, 3)])
        from_cross = lax.ppermute(other_core, ("core", "y"), [(1, 2), (2, 1)])
        from_beside = lax.ppermute(other_core, ("core", "y"), [(0, 2), (3, 1)])
        mixed_part = (
            jnp.where(core == y, same_core, 0.0)
            + from_same.astype(f32)
            + from_cross.astype(f32)
            + from_beside.astype(f32)
        ).astype(bf16)
        out_pieces += dealt(
            lambda j: lax.dynamic_index_in_dim(mixed_part, j, 0, keepdims=False), z
        )
    mixed = laid(order, out_pieces, lines)[None]
    return mixed, span_states, request_states


def rows_kept_solution(mesh):
    placed = (
        P("seq", "mp"),
        P("seq", "mp"),
        P("seq"),
        P("mp"),
        P("mp", None, None),
        P(),
        P("seq", "mp"),
        P("seq", "mp"),
        P("seq", "mp"),
        P("seq", "mp"),
        P("mp"),
        P(),
        P(None, "mp"),
        P("mp", None),
        P("mp"),
        P("mp"),
        P("mp", "seq"),
    )
    return jax.shard_map(
        on_device,
        mesh=mesh,
        in_specs=placed,
        out_specs=(P("seq", "mp", None), P("seq", "mp", None, None), P("seq", "mp", None, None)),
        check_vma=False,
    )


def heads_kept_solution(mesh):
    seq, mp = mesh.shape["seq"], mesh.shape["mp"]
    split = Mesh(mesh.devices.reshape(seq // 2, 2, 2, mp // 2), ("z", "core", "y", "x"))
    s, m = ("z", "core"), ("y", "x")
    placed = (
        P(s, m),
        P(s, m),
        P(s),
        P(m),
        P(m, None, None),
        P(),
        P(s, m),
        P(s, m),
        P(s, m),
        P(s, m),
        P(m),
        P(),
        P(None, m),
        P(m, None),
        P(m),
        P(m),
        P(m, s),
    )
    return jax.shard_map(
        on_core,
        mesh=split,
        in_specs=placed,
        out_specs=(P(s, m, None), P(s, m, None, None), P(s, m, None, None)),
        check_vma=False,
    )


def solution(mesh):
    if mesh.shape["mp"] == 4 and mesh.shape["seq"] == 8:
        return heads_kept_solution(mesh)
    return rows_kept_solution(mesh)
```

```python
import jax
import jax.numpy as jnp
import numpy as np
from jax import lax
from jax.experimental import pallas as pl
from jax.experimental.pallas import tpu as pltpu
from jax.sharding import Mesh
from jax.sharding import PartitionSpec as P

BLK = 64


norm_eps = 0.00064
highest = lax.Precision.HIGHEST


def passed_along(x, axis, by):
    length = lax.axis_size(axis)
    pairs = [(i, i + by) for i in range(length) if 0 <= i + by < length]
    return lax.ppermute(x, axis, pairs)


def entering(value, axis, join, neutral):
    count, mine = (lax.axis_size(axis), lax.axis_index(axis))
    pieces = jax.tree.map(lambda part: lax.all_gather(part, axis), value)
    total = jax.tree.map(
        lambda part, zero: jnp.full_like(part, 0) + jnp.asarray(zero, part.dtype), value, neutral
    )

    def hop(position, total):
        longer = join(total, jax.tree.map(lambda part: part[position], pieces))
        return jax.tree.map(lambda new, old: jnp.where(position < mine, new, old), longer, total)

    return lax.fori_loop(0, count - 1, hop, total)


def mix_rows(current, previous, weight):
    here = current.astype(jnp.float32)
    return (here + weight[None, :] * (previous.astype(jnp.float32) - here)).astype(jnp.bfloat16)


def block_sweep(
    evolving_memory,
    acceptance_entries,
    lookup_entries,
    payload_entries,
    log_fading_amount,
    diagonal_reward,
):
    inclusive = jnp.cumsum(log_fading_amount, axis=0)
    exclusive = inclusive - log_fading_amount
    recept_scaled = acceptance_entries * jnp.exp(exclusive)
    keys_scaled = lookup_entries * jnp.exp(-inclusive)
    scores = jnp.einsum("ihc,jhc->hij", recept_scaled, keys_scaled, precision=highest)
    count = acceptance_entries.shape[0]
    row_index = lax.broadcasted_iota(jnp.int32, (count, count), 0)
    col_index = lax.broadcasted_iota(jnp.int32, (count, count), 1)
    scores = jnp.where((row_index > col_index)[None], scores, 0.0)
    diagonal_contribution = jnp.sum(
        acceptance_entries * diagonal_reward[None] * lookup_entries, axis=-1, keepdims=True
    )
    answer_lines = (
        jnp.einsum("hij,jhd->ihd", scores, payload_entries, precision=highest)
        + diagonal_contribution * payload_entries
    )
    answer_lines = answer_lines + jnp.einsum(
        "ihc,hcd->ihd", recept_scaled, evolving_memory, precision=highest
    )
    total = inclusive[-1]
    carried = lookup_entries * jnp.exp(total[None] - inclusive)
    new_state = jnp.exp(total)[:, :, None] * evolving_memory + jnp.einsum(
        "jhc,jhd->hcd", carried, payload_entries, precision=highest
    )
    return (new_state, answer_lines)


def continued_recurrence(
    acceptance_entries, lookup_entries, payload_entries, log_fading_amount, diagonal_reward
):
    length, per_group_view, embedding_dimension = acceptance_entries.shape
    blocks = length // BLK

    def step(evolving_memory, entry_lines):
        return block_sweep(
            evolving_memory,
            entry_lines[0],
            entry_lines[1],
            entry_lines[2],
            entry_lines[3],
            diagonal_reward,
        )

    shaped = tuple(
        (
            a.reshape(blocks, BLK, per_group_view, embedding_dimension)
            for a in (acceptance_entries, lookup_entries, payload_entries, log_fading_amount)
        )
    )
    evolving_memory, results = lax.scan(
        step,
        jnp.zeros((per_group_view, embedding_dimension, embedding_dimension), jnp.float32),
        shaped,
    )
    return (evolving_memory, results.reshape(length, per_group_view, embedding_dimension))


def combine(earlier, later):
    return (earlier[0] + later[0], jnp.exp(later[0])[:, :, None] * earlier[1] + later[1])


def shifted_rows(current, edge_row, long_rows, requests, slot_rows):
    feature_part = current.shape[1]
    long_prev = jnp.concatenate([edge_row, current[: long_rows - 1]], axis=0)
    short_view = current[long_rows:].reshape(requests, slot_rows, feature_part)
    short_prev = jnp.concatenate(
        [jnp.zeros((requests, 1, feature_part), current.dtype), short_view[:, :-1]], axis=1
    )
    short_prev = short_prev.reshape(requests * slot_rows, feature_part)
    return jnp.concatenate([long_prev, short_prev], axis=0)


def on_device(
    continued_prompt_entries,
    padded_prompt_entries,
    prompt_live_extents,
    preceding_entry_line,
    carried_memory,
    token_mixing_ratios,
    acceptance_transform,
    lookup_transform,
    payload_transform,
    gating_transform,
    fading_baseline,
    fading_left_factor,
    fading_right_factor,
    present_reward,
    group_layer_scaling,
    group_layer_shift_term,
    final_transform,
):
    long_rows = continued_prompt_entries.shape[0]
    requests = prompt_live_extents.shape[0]
    slot_rows = padded_prompt_entries.shape[0] // requests
    per_group_view, embedding_dimension = present_reward.shape
    arrived = passed_along(continued_prompt_entries[-1:], "seq", 1)
    first = lax.axis_index("seq") == 0
    edge_row = jnp.where(first, preceding_entry_line[None, :], arrived)
    current = jnp.concatenate([continued_prompt_entries, padded_prompt_entries], axis=0)
    current, edge_full = (
        lax.all_gather(current, "mp", axis=1, tiled=True),
        lax.all_gather(edge_row, "mp", axis=1, tiled=True),
    )
    previous = shifted_rows(current, edge_full, long_rows, requests, slot_rows)
    mixes = [mix_rows(current, previous, token_mixing_ratios[index]) for index in range(5)]
    total_rows = current.shape[0]
    columns = acceptance_transform.shape[1]
    pieces = (
        lax.all_gather(acceptance_transform, "seq", axis=0, tiled=True),
        lax.all_gather(lookup_transform, "seq", axis=0, tiled=True),
        lax.all_gather(payload_transform, "seq", axis=0, tiled=True),
        lax.all_gather(gating_transform, "seq", axis=0, tiled=True),
    )
    acceptance_entries, lookup_entries, payload_entries, gate = tuple(
        (
            jnp.dot(source, piece, preferred_element_type=jnp.float32)
            for source, piece in zip(mixes[:4], pieces)
        )
    )
    squeezed = jnp.tanh(
        jnp.dot(mixes[4], fading_left_factor, preferred_element_type=jnp.float32)
    ).astype(jnp.bfloat16)
    log_fading_amount = -jnp.exp(
        fading_baseline[None, :]
        + jnp.dot(squeezed, fading_right_factor, preferred_element_type=jnp.float32)
    )
    recept3, keys3, values3, decay3 = [
        a.reshape(total_rows, per_group_view, embedding_dimension)
        for a in (acceptance_entries, lookup_entries, payload_entries, log_fading_amount)
    ]
    local_state, long_out = continued_recurrence(
        recept3[:long_rows],
        keys3[:long_rows],
        values3[:long_rows],
        decay3[:long_rows],
        present_reward,
    )
    long_decay = decay3[:long_rows]
    group_total = jnp.sum(long_decay, axis=0)
    blank = (
        jnp.zeros((per_group_view, embedding_dimension), jnp.float32),
        jnp.zeros((per_group_view, embedding_dimension, embedding_dimension), jnp.float32),
    )
    prefix_total, prefix_state = entering((group_total, local_state), "seq", combine, blank)
    incoming = jnp.exp(prefix_total)[:, :, None] * carried_memory + prefix_state
    before_row = jnp.cumsum(long_decay, axis=0) - long_decay
    long_out = long_out + jnp.einsum(
        "ihc,hcd->ihd", recept3[:long_rows] * jnp.exp(before_row), incoming, precision=highest
    )
    span_end = jnp.exp(group_total)[:, :, None] * incoming + local_state
    live_rows = (
        lax.broadcasted_iota(jnp.int32, (requests, slot_rows), 1) < prompt_live_extents[:, None]
    )
    live_flat = live_rows.reshape(requests * slot_rows).astype(jnp.float32)[:, None, None]
    short_shape = (requests, slot_rows, per_group_view, embedding_dimension)
    short_recept = recept3[long_rows:].reshape(short_shape)
    short_keys = (keys3[long_rows:] * live_flat).reshape(short_shape)
    short_values = values3[long_rows:].reshape(short_shape)
    short_decay = (decay3[long_rows:] * live_flat).reshape(short_shape)
    zeroed_memory = jnp.zeros(
        (per_group_view, embedding_dimension, embedding_dimension), jnp.float32
    )

    def request_pass(acceptance_lines, lookup_table, payload_table, fading_table):
        return block_sweep(
            zeroed_memory,
            acceptance_lines,
            lookup_table,
            payload_table,
            fading_table,
            present_reward,
        )

    request_states, short_out = jax.vmap(request_pass)(
        short_recept, short_keys, short_values, short_decay
    )
    wkv = jnp.concatenate(
        [long_out, short_out.reshape(requests * slot_rows, per_group_view, embedding_dimension)],
        axis=0,
    )
    mean = jnp.mean(wkv, axis=-1, keepdims=True)
    centred = wkv - mean
    variance = jnp.mean(centred * centred, axis=-1, keepdims=True)
    normed = (centred * lax.rsqrt(variance + norm_eps)).reshape(
        total_rows, columns
    ) * group_layer_scaling[None, :] + group_layer_shift_term[None, :]
    row_live = jnp.concatenate(
        [jnp.ones((long_rows,), dtype=bool), live_rows.reshape(requests * slot_rows)], axis=0
    )
    hidden = jnp.where(row_live[:, None], normed * jax.nn.silu(gate), 0.0).astype(jnp.bfloat16)
    full_out = lax.all_gather(final_transform, "seq", axis=1, tiled=True)
    mixed_rows = lax.psum_scatter(
        jnp.dot(hidden, full_out, preferred_element_type=jnp.float32),
        "mp",
        scatter_dimension=0,
        tiled=True,
    )
    return (mixed_rows.astype(jnp.bfloat16)[None], span_end[None], request_states)


f32 = jnp.float32
bf16 = jnp.bfloat16
VMEM_LIMIT = 56 * 1024 * 1024
TILE = 256


def in_vmem():
    return pl.BlockSpec(memory_space=pltpu.VMEM)


def in_smem():
    return pl.BlockSpec(memory_space=pltpu.SMEM)


def kernel_params():
    return pltpu.CompilerParams(vmem_limit_bytes=VMEM_LIMIT)


EXTRA = 16


def here_and_step(x_ref, is_long, period, tile):
    rows = x_ref.shape[1] - EXTRA
    here = x_ref[tile, 0:rows, :].astype(f32)
    above = x_ref[jnp.maximum(tile - 1, 0), rows - 16 : rows, :].astype(f32)[15:16]
    first = jnp.where(is_long == 1, x_ref[0, rows : rows + 16, :].astype(f32)[0:1], 0.0)
    row = lax.broadcasted_iota(jnp.int32, here.shape, 0)
    before = jnp.where(row == 0, above, pltpu.roll(here, 1, 0))
    start = ((row + tile * rows) & (period - 1)) == 0
    before = jnp.where(start, first, before)
    return here, before - here


def given_kernel(kind, extents, long_ref, short_ref, out_ref):
    rows = long_ref.shape[0]
    is_long = kind[0] == 1
    out_ref[0:rows, :] = jnp.where(is_long, short_ref[...], long_ref[...])
    lane = lax.broadcasted_iota(jnp.int32, (EXTRA, out_ref.shape[1]), 1)
    line = jnp.zeros(lane.shape, f32)
    for n in range(extents.shape[0]):
        line = jnp.where(lane == n, extents[n].astype(f32), line)
    out_ref[rows : rows + EXTRA, :] = line.astype(bf16)


def given_to_other_core(kind, extents, long_rows, short_rows):
    rows, columns = long_rows.shape
    return pl.pallas_call(
        given_kernel,
        out_shape=jax.ShapeDtypeStruct((rows + EXTRA, columns), bf16),
        in_specs=[in_smem()] * 2 + [in_vmem()] * 2,
        out_specs=in_vmem(),
        compiler_params=kernel_params(),
    )(kind, extents, long_rows, short_rows)


def block_kernel(kind, extents, long_ref, short_ref, taken, edge, out_ref):
    rows = long_ref.shape[0]
    depth = out_ref.shape[2]
    is_long = kind[0] == 1
    count = extents.shape[0]
    row = lax.broadcasted_iota(jnp.int32, (EXTRA, depth), 0)
    lane = lax.broadcasted_iota(jnp.int32, (EXTRA, depth), 1)
    other = taken[rows : rows + EXTRA, 0:depth].astype(f32)
    line = jnp.where(is_long, pltpu.roll(other, count, 1), other)
    own_at = jnp.where(is_long, 0, count)
    for n in range(count):
        line = jnp.where(lane == own_at + n, extents[n].astype(f32), line)
    for half in range(2):
        start = jnp.where(is_long, half, 1 - half) * depth
        at = pl.ds(pl.multiple_of(start, depth), depth)
        got = taken[0:rows, at]
        out_ref[half, 0:rows, :] = jnp.where(is_long, long_ref[:, at], got)
        out_ref[half, rows : 2 * rows, :] = jnp.where(is_long, got, short_ref[:, at])
        first = edge[:, at].astype(f32)
        out_ref[half, 2 * rows :, :] = jnp.where(row == 0, first, line).astype(bf16)


def block_of_chip(kind, extents, long_rows, short_rows, taken, edge):
    rows, columns = long_rows.shape
    return pl.pallas_call(
        block_kernel,
        out_shape=jax.ShapeDtypeStruct((2, 2 * rows + EXTRA, columns // 2), bf16),
        in_specs=[in_smem()] * 2 + [in_vmem()] * 4,
        out_specs=in_vmem(),
        compiler_params=kernel_params(),
    )(kind, extents, long_rows, short_rows, taken, edge)


def half_block(shape):
    return pl.BlockSpec((1,) + shape[1:], lambda i: (i,) + (0,) * (len(shape) - 1))


def mix_kernel(kind, chunk, ratios, left, pair_mix, value_mix, gate_mix, squeezed):
    @pl.loop(0, chunk.shape[1])
    def _(tile):
        here, step = here_and_step(chunk.at[0], kind[0], kind[1], tile)
        at = pl.ds(pl.multiple_of(tile * TILE, TILE), TILE)

        def mix(which):
            return (here + ratios[0, which : which + 1, :] * step).astype(bf16)

        pair_mix[0, 0, at, :] = mix(0)
        pair_mix[0, 1, at, :] = mix(1)
        value_mix[0, at, :] = mix(2)
        gate_mix[0, at, :] = mix(3)
        squeezed[0, at, :] = jnp.dot(mix(4), left[0], preferred_element_type=f32)


def mixes_of(kind, pair, ratios, left):
    lines, rows, depth = pair.shape[1], pair.shape[2] - EXTRA, pair.shape[3]
    whole = lines * rows
    outs = [
        jax.ShapeDtypeStruct((2, 2, whole, depth), bf16),
        jax.ShapeDtypeStruct((2, whole, depth), bf16),
        jax.ShapeDtypeStruct((2, whole, depth), bf16),
        jax.ShapeDtypeStruct((2, whole, left.shape[2]), f32),
    ]
    return pl.pallas_call(
        mix_kernel,
        grid=(2,),
        out_shape=outs,
        in_specs=[in_smem()] + [half_block(a.shape) for a in (pair, ratios, left)],
        out_specs=[half_block(out.shape) for out in outs],
        compiler_params=kernel_params(),
    )(kind, pair, ratios, left)


def mix_project_kernel(rel, ready, kind, chunk, ratios, left, own, sibling, *refs):
    earlier, refs = refs[:ready], refs[ready:]
    value_mix, gate_mix, squeezed, recept_ref, keys_ref = refs
    half = pl.program_id(0)

    @pl.loop(0, chunk.shape[1])
    def _(tile):
        here, step = here_and_step(chunk.at[0], kind[0], kind[1], tile)
        at = pl.ds(pl.multiple_of(tile * TILE, TILE), TILE)

        def mix(which):
            return (here + ratios[0, which : which + 1, :] * step).astype(bf16)

        value_mix[0, at, :] = mix(2)
        gate_mix[0, at, :] = mix(3)
        squeezed[0, at, :] = jnp.dot(mix(4), left[0], preferred_element_type=f32)
        for which, out in enumerate((recept_ref, keys_ref)):
            weight = jnp.where(
                half == 0, own[kind[2 + rel], which], sibling[kind[2 + rel], which]
            )
            part = jnp.dot(mix(which), weight, preferred_element_type=f32)
            if ready == 1:
                weight = jnp.where(half == 0, own[kind[2], which], sibling[kind[2], which])
                part = part + jnp.dot(
                    earlier[0][0, which, at, :], weight, preferred_element_type=f32
                )
                before = jnp.zeros_like(part)
            else:
                before = earlier[which][at, :]
            out[at, :] = part + jnp.where(half == 0, before, out[at, :])


def mix_and_project(rel, kind, pair, ratios, left, own, sibling, *earlier):
    lines, rows, depth = pair.shape[1], pair.shape[2] - EXTRA, pair.shape[3]
    whole, width = lines * rows, own.shape[3]
    outs = [
        jax.ShapeDtypeStruct((2, whole, depth), bf16),
        jax.ShapeDtypeStruct((2, whole, depth), bf16),
        jax.ShapeDtypeStruct((2, whole, left.shape[2]), f32),
    ]
    flat = jax.ShapeDtypeStruct((whole, width), f32)
    ready = len(earlier)
    return pl.pallas_call(
        lambda *refs: mix_project_kernel(rel, ready, *refs),
        grid=(2,),
        out_shape=outs + [flat] * 2,
        in_specs=[in_smem()]
        + [half_block(a.shape) for a in (pair, ratios, left)]
        + [in_vmem()] * 2
        + ([half_block(earlier[0].shape)] if ready == 1 else [in_vmem()] * 2),
        out_specs=[half_block(out.shape) for out in outs]
        + [pl.BlockSpec((whole, width), lambda i: (0, 0))] * 2,
        compiler_params=kernel_params(),
    )(kind, pair, ratios, left, own, sibling, *earlier)


def project_kernel(
    kind,
    mix0,
    mix1,
    mix2,
    low0,
    low1,
    low2,
    recept_part,
    keys_part,
    last0,
    last1,
    ratios,
    left,
    own,
    sibling,
    own_value,
    sibling_value,
    right,
    base,
    recept_ref,
    keys_ref,
    values_ref,
    decay_ref,
    gate_mix,
):
    tile = pl.program_id(0)
    totals = [recept_part[...], keys_part[...], None]
    squeezed = low0[0] + low0[1] + low1[0] + low1[1] + low2[0] + low2[1]
    for half, chunk in enumerate((last0, last1)):
        here, step = here_and_step(chunk, kind[0], kind[1], tile)

        def mix(which):
            return (here + ratios[half, which : which + 1, :] * step).astype(bf16)

        for which in range(2):
            weight = (own, sibling)[half][kind[5], which]
            totals[which] += jnp.dot(mix(which), weight, preferred_element_type=f32)
        weight = (own_value, sibling_value)[half][kind[5], 0]
        part = jnp.dot(mix(2), weight, preferred_element_type=f32)
        totals[2] = part if totals[2] is None else totals[2] + part
        gate_mix[half] = mix(3)
        squeezed = squeezed + jnp.dot(mix(4), left[half], preferred_element_type=f32)
    for rel, mixes in enumerate((mix0, mix1, mix2)):
        for half in range(2):
            weight = (own_value, sibling_value)[half][kind[2 + rel], 0]
            totals[2] += jnp.dot(mixes[half], weight, preferred_element_type=f32)
    recept_ref[...] = totals[0]
    keys_ref[...] = totals[1]
    values_ref[...] = totals[2]
    squeezed = jnp.tanh(squeezed).astype(bf16)
    grown = jnp.dot(squeezed, right[...], preferred_element_type=f32)
    decay_ref[...] = -jnp.exp(base[...] + grown)


def projected(kind, mixes, lows, parts, last, *rest):
    rows, depth = mixes[0].shape[1:]
    width, rank = parts[0].shape[1], lows[0].shape[2]
    flat = jax.ShapeDtypeStruct((rows, width), f32)
    tile_of = pl.BlockSpec((TILE, width), lambda i: (i, 0))
    return pl.pallas_call(
        project_kernel,
        grid=(rows // TILE,),
        out_shape=[flat] * 4 + [jax.ShapeDtypeStruct((2, rows, depth), bf16)],
        in_specs=[in_smem()]
        + [pl.BlockSpec((2, TILE, depth), lambda i: (0, i, 0))] * 3
        + [pl.BlockSpec((2, TILE, rank), lambda i: (0, i, 0))] * 3
        + [tile_of] * 2
        + [in_vmem()] * (2 + len(rest)),
        out_specs=[tile_of] * 4 + [pl.BlockSpec((2, TILE, depth), lambda i: (0, i, 0))],
        compiler_params=kernel_params(),
    )(kind, *mixes, *lows, *parts, *last, *rest)


def gate_kernel(
    kind, mix0, mix1, mix2, mix3, own, sibling, normed, live, kept0, sent0, kept1, sent1, total
):
    half = pl.program_id(0)
    part = None
    for rel, mixes in enumerate((mix0, mix1, mix2, mix3)):
        weight = jnp.where(half == 0, own[kind[2 + rel], 0], sibling[kind[2 + rel], 0])
        new = jnp.dot(mixes[0], weight, preferred_element_type=f32)
        part = new if part is None else part + new

    @pl.when(half == 0)
    def _():
        total[...] = part

    @pl.when(half == 1)
    def _():
        gate = total[...] + part
        value = normed[...] * (gate * jax.nn.sigmoid(gate))
        value = jnp.where(live[...] > 0, value, 0.0).astype(bf16)
        lines = kept0.shape[1]
        value = value.reshape(lines, 2, 2, 2, BLK // 2, value.shape[1])
        is_long = kind[0] == 1
        for block in range(2):
            for at, kept, sent in ((0, kept0, sent0), (1, kept1, sent1)):
                even, odd = value[:, 0, block, at], value[:, 1, block, at]
                kept[block] = jnp.where(is_long, even, odd)
                sent[block] = jnp.where(is_long, odd, even)


def gated(kind, mixes, own, sibling, normed, live):
    rows, width = normed.shape
    quarter = jax.ShapeDtypeStruct((2, rows // TILE, BLK // 2, width), bf16)
    return pl.pallas_call(
        gate_kernel,
        grid=(2,),
        out_shape=[quarter] * 4,
        in_specs=[in_smem()] + [half_block(mix.shape) for mix in mixes] + [in_vmem()] * 4,
        out_specs=[pl.BlockSpec(quarter.shape, lambda i: (0, 0, 0, 0))] * 4,
        scratch_shapes=[pltpu.VMEM((rows, width), f32)],
        compiler_params=kernel_params(),
    )(kind, *mixes, own, sibling, normed, live)


def head_blocks(heads):
    width = heads * BLK
    tall = lax.broadcasted_iota(jnp.int32, (width, width), 0) // BLK
    wide = lax.broadcasted_iota(jnp.int32, (width, width), 1) // BLK
    return tall == wide


def state_kernel(lengths, carry, k_ref, v_ref, w_ref, s_ref, state_ref, entered_ref, hold):
    span, width = BLK, k_ref.shape[1]
    heads = width // span
    row = lax.broadcasted_iota(jnp.int32, (span, width), 0)
    lane = lax.broadcasted_iota(jnp.int32, (span, width), 1)
    for h in range(heads):
        hold[:, h * span : (h + 1) * span] = s_ref[h]

    @pl.loop(0, k_ref.shape[0] // span)
    def _(n):
        at = pl.ds(pl.multiple_of(n * span, span), span)
        live = row < lengths[n]
        k = jnp.where(live, k_ref[at, :], 0.0)
        total = jnp.where(live, w_ref[at, :], 0.0)
        after_row = jnp.zeros_like(total)
        half = 1
        while half < span:
            upper = (row & half) != 0
            across = jnp.where(
                upper, pltpu.roll(total, half, 0), pltpu.roll(total, span - half, 0)
            )
            after_row = after_row + jnp.where(upper, 0.0, across)
            total = total + across
            half *= 2
        added = lax.dot_general(
            (k * jnp.exp(after_row)).astype(bf16),
            v_ref[at, :].astype(bf16),
            (((0,), (0,)), ((), ())),
            preferred_element_type=f32,
        )
        fresh = jnp.zeros((span, width), f32)
        for h in range(heads):
            fresh = jnp.where(lane // span == h, added[h * span : (h + 1) * span], fresh)
        twice = jnp.concatenate([total] * 2, axis=0)
        turned_parts = []
        for p in range(width // (2 * span)):
            flipped = jnp.transpose(twice[:, p * 2 * span : (p + 1) * 2 * span])
            turned_parts.append(
                jnp.where(lane[:, : 2 * span] < span, flipped[:span], flipped[span:])
            )
        fade = jnp.exp(jnp.concatenate(turned_parts, axis=1))
        entered = hold[...] * carry[0]
        entered_ref[n] = entered.astype(bf16)
        state = fade * entered + fresh
        hold[...] = state
        for h in range(heads):
            state_ref[n, h] = state[:, h * span : (h + 1) * span]


def states_of(lengths, carry, k, v, w, state):
    rows, width = k.shape
    heads = width // BLK
    return pl.pallas_call(
        state_kernel,
        out_shape=[
            jax.ShapeDtypeStruct((rows // BLK, heads, BLK, BLK), f32),
            jax.ShapeDtypeStruct((rows // BLK, BLK, width), bf16),
        ],
        in_specs=[in_smem()] * 2 + [in_vmem()] * 4,
        out_specs=[in_vmem()] * 2,
        scratch_shapes=[pltpu.VMEM((BLK, width), f32)],
        compiler_params=kernel_params(),
    )(lengths, carry, k, v, w, state)


def sweep_kernel(lengths, r_ref, k_ref, v_ref, w_ref, entered_ref, u_ref, gain, bias, out_ref):
    span, width = BLK, r_ref.shape[1]
    heads = width // span
    row = lax.broadcasted_iota(jnp.int32, (span, width), 0)
    lane = lax.broadcasted_iota(jnp.int32, (span, width), 1)
    col = lane % span
    same_head = head_blocks(heads)

    def spread(value):
        stacked = jnp.concatenate([value.astype(bf16)] * heads, axis=0)
        return jnp.where(same_head, stacked, jnp.zeros_like(stacked))

    def against(a, b):
        return lax.dot_general(a, b, (((1,), (1,)), ((), ())), preferred_element_type=f32)

    @pl.loop(0, r_ref.shape[0] // span)
    def _(n):
        at = pl.ds(pl.multiple_of(n * span, span), span)
        live = row < lengths[n]
        r, v = r_ref[at, :], v_ref[at, :]
        k = jnp.where(live, k_ref[at, :], 0.0)
        total = jnp.where(live, w_ref[at, :], 0.0)
        before = jnp.zeros_like(total)
        after_row = jnp.zeros_like(total)
        scores = against((r * u_ref[...]).astype(bf16), spread(k))
        scores = jnp.where(row == col, scores, 0.0)
        level = 0
        while (1 << level) < span:
            half = 1 << level
            upper = (row & half) != 0
            if level:
                scale = jnp.exp(jnp.where(upper, before, after_row))
                part = against((r * scale).astype(bf16), spread(k * scale))
            else:
                part = against(r.astype(bf16), spread(k))
            pair = upper & (((row >> level) ^ (col >> level)) == 1)
            scores = jnp.where(pair, part, scores)
            across = jnp.where(
                upper, pltpu.roll(total, half, 0), pltpu.roll(total, span - half, 0)
            )
            before = before + jnp.where(upper, across, 0.0)
            after_row = after_row + jnp.where(upper, 0.0, across)
            total = total + across
            level += 1
        out = jnp.dot(scores.astype(bf16), spread(v), preferred_element_type=f32)
        out = out + jnp.dot(
            (r * jnp.exp(before)).astype(bf16),
            spread(entered_ref[n]),
            preferred_element_type=f32,
        )
        out_ref[at, :] = out

    ones = jnp.where(same_head, 1.0, 0.0).astype(bf16)

    def head_mean(value):
        high = value.astype(bf16)
        low = (value - high.astype(f32)).astype(bf16)
        both = jnp.dot(high, ones, preferred_element_type=f32) + jnp.dot(
            low, ones, preferred_element_type=f32
        )
        return both * (1.0 / span)

    @pl.loop(0, r_ref.shape[0] // TILE)
    def _(tile):
        at = pl.ds(pl.multiple_of(tile * TILE, TILE), TILE)
        value = out_ref[at, :]
        centred = value - head_mean(value)
        spread_of = head_mean(centred * centred)
        out_ref[at, :] = centred * lax.rsqrt(spread_of + norm_eps) * gain[...] + bias[...]


def sweep(lengths, r, k, v, w, entered, bonus, gain, bias):
    return pl.pallas_call(
        sweep_kernel,
        out_shape=jax.ShapeDtypeStruct(r.shape, f32),
        in_specs=[in_smem()] + [in_vmem()] * 8,
        out_specs=in_vmem(),
        compiler_params=kernel_params(),
    )(lengths, r, k, v, w, entered, bonus, gain, bias)


def final_kernel(block_of, h0, h1, h2, h3, weight, o0, o1, o2, o3, hold):
    @pl.loop(0, hold.shape[1] // TILE)
    def _(tile):
        at = pl.ds(pl.multiple_of(tile * TILE, TILE), TILE)
        total = None
        for k, piece in enumerate((h0, h1, h2, h3)):
            part = jnp.dot(piece[...], weight[k, :, at], preferred_element_type=f32)
            total = part if total is None else total + part
        hold[:, at] = total.astype(bf16)

    block = hold.shape[0] // 4
    for rel, out in enumerate((o0, o1, o2, o3)):
        at = pl.ds(pl.multiple_of(block_of[rel] * block, block), block)
        out[...] = hold[at, :].reshape(out.shape)


def final_product(block_of, pieces, weight, lines):
    rows, width = pieces[0].shape[0], weight.shape[2]
    out = jax.ShapeDtypeStruct((lines, rows // 4 // lines, width), bf16)
    return pl.pallas_call(
        final_kernel,
        out_shape=[out] * 4,
        in_specs=[in_smem()] + [in_vmem()] * 5,
        out_specs=[in_vmem()] * 4,
        scratch_shapes=[pltpu.VMEM((rows, width), bf16)],
        compiler_params=kernel_params(),
    )(block_of, *pieces, weight)


def lay_kernel(at, *refs):
    pieces, out_ref = refs[:-1], refs[-1]
    rows, width = pieces[0].shape
    lines = out_ref.shape[1] // width
    for n, piece in enumerate(pieces):
        column = pl.multiple_of(at[n % lines] * width, width)
        out_ref[n // lines * rows : (n // lines + 1) * rows, pl.ds(column, width)] = piece[...]


def laid(at, pieces, lines):
    rows, width = pieces[0].shape
    return pl.pallas_call(
        lay_kernel,
        out_shape=jax.ShapeDtypeStruct((len(pieces) // lines * rows, lines * width), bf16),
        in_specs=[in_smem()] + [in_vmem()] * len(pieces),
        out_specs=in_vmem(),
        compiler_params=kernel_params(),
    )(at, *pieces)


def after(value, *others):
    return lax.optimization_barrier((value,) + others)[0]


def turned(x, axis, by):
    length = lax.axis_size(axis)
    return lax.ppermute(x, axis, [(i, (i + by) % length) for i in range(length)])


def flipped_core(x):
    return lax.ppermute(x, "core", [(0, 1), (1, 0)])


def over_x(x):
    return lax.ppermute(x, "x", [(0, 1), (1, 0)])


def over_y(x):
    return lax.ppermute(x, "y", [(0, 1), (1, 0)])


def dealt(blocks, z):
    length = lax.axis_size("z")
    return [blocks(z)] + [turned(blocks((z + k) % length), "z", k) for k in range(1, length)]


def spread_along(piece, z):
    one = lax.ppermute(piece, "z", [(0, 1), (1, 2), (2, 3)])
    three = lax.ppermute(piece, "z", [(1, 0), (2, 1), (3, 2)])
    two = turned(piece, "z", 2)
    far = lax.ppermute(two, "z", [(1, 0), (2, 3)])
    return piece, one, two, three, far


def in_place(spread, z, at=0):
    piece, one, two, three, far = spread
    whole = jnp.zeros((4,) + piece.shape, piece.dtype)
    for k, part in ((1, one), (2, two), (3, three)):
        whole = lax.dynamic_update_index_in_dim(whole, part, (z - k) % 4, 0)
    far_at = jnp.where(z == 0, 3, jnp.where(z == 3, 0, z))
    whole = lax.dynamic_update_index_in_dim(whole, far, far_at, 0)
    return lax.dynamic_update_index_in_dim(whole, piece, z, 0)


def in_order(pieces, z):
    length = len(pieces)
    whole = jnp.zeros((length,) + pieces[0].shape, pieces[0].dtype)
    for k, piece in enumerate(pieces):
        whole = lax.dynamic_update_index_in_dim(whole, piece, (z - k) % length, 0)
    return whole


def on_core(
    continued_prompt_entries,
    padded_prompt_entries,
    prompt_live_extents,
    preceding_entry_line,
    carried_memory,
    token_mixing_ratios,
    acceptance_transform,
    lookup_transform,
    payload_transform,
    gating_transform,
    fading_baseline,
    fading_left_factor,
    fading_right_factor,
    present_reward,
    group_layer_scaling,
    group_layer_shift_term,
    final_transform,
):
    z, core = lax.axis_index("z"), lax.axis_index("core")
    y, x = lax.axis_index("y"), lax.axis_index("x")
    mp = 2 * y + x
    is_long = core == 0
    lines = lax.axis_size("z")
    group_rows, columns = continued_prompt_entries.shape
    requests = prompt_live_extents.shape[0]
    slot_rows = group_rows // requests
    heads, span = present_reward.shape
    heads = heads // lines
    width = heads * span
    depth = acceptance_transform.shape[0]
    rows = 2 * lines * group_rows

    kind = jnp.stack(
        [is_long.astype(jnp.int32), jnp.where(is_long, rows, slot_rows).astype(jnp.int32)]
        + [(mp ^ rel).astype(jnp.int32) for rel in range(4)]
    )
    given = given_to_other_core(
        kind, prompt_live_extents, continued_prompt_entries, padded_prompt_entries
    )
    taken = flipped_core(given)
    block = block_of_chip(
        kind,
        prompt_live_extents,
        continued_prompt_entries,
        padded_prompt_entries,
        taken,
        preceding_entry_line[None],
    )
    (
        block,
        acceptance_transform,
        lookup_transform,
        payload_transform,
        gating_transform,
        final_transform,
        token_mixing_ratios,
        fading_left_factor,
        fading_right_factor,
        carried_memory,
    ) = lax.optimization_barrier(
        (
            block,
            acceptance_transform,
            lookup_transform,
            payload_transform,
            gating_transform,
            final_transform,
            token_mixing_ratios,
            fading_left_factor,
            fading_right_factor,
            carried_memory,
        )
    )
    spread = spread_along(block, z)
    pair = jnp.swapaxes(in_place(spread, z), 0, 1)
    pair_x, pair_y = over_x(pair), over_y(pair)
    a_xy, b_xy = over_y(pair_x[0]), over_x(pair_y[1])
    extents = pair[0, :, 2 * group_rows + 1, : 2 * requests].reshape(2 * lines * requests)
    extents = jnp.where(is_long, slot_rows, extents.astype(jnp.int32)).astype(jnp.int32)

    def chunk_order(whole):
        split = whole.reshape((4, 2, depth) + whole.shape[1:])
        parts = []
        for rel in range(4):
            both = split[mp ^ rel]
            parts.append(jnp.where(is_long, both, both[::-1]))
        return parts

    ratios = [part.transpose(0, 2, 1) for part in chunk_order(token_mixing_ratios.T)]
    left = chunk_order(fading_left_factor)

    def columns_of(weights, *ready):
        stacked = jnp.stack(weights)

        def block(j):
            return lax.dynamic_slice_in_dim(stacked, j * width, width, 2)

        blocks = [block((z + k) % lines) for k in range(lines)]
        blocks = lax.optimization_barrier((tuple(blocks),) + ready)[0]
        pieces = [blocks[0]] + [turned(blocks[k], "z", k) for k in range(1, lines)]
        return pieces

    def both_cores(pieces):
        return in_order(pieces, z), in_order([flipped_core(piece) for piece in pieces], z)

    pieces = columns_of([acceptance_transform, lookup_transform], pair)
    value_pieces = columns_of([payload_transform], pair_x, pair_y)
    gate_pieces = columns_of([gating_transform], value_pieces[2])
    own, sibling = both_cores(pieces)
    own_value, sibling_value = both_cores(value_pieces)
    own_gate, sibling_gate = both_cores(gate_pieces)

    def mine_of(vector):
        return lax.dynamic_slice_in_dim(vector, z * width, width, 0)[None]

    pair_mix, value0, gate0, low0 = mixes_of(kind, pair, ratios[0], left[0])
    value1, gate1, low1, recept, keys = mix_and_project(
        1, kind, pair_x, ratios[1], left[1], own, sibling, pair_mix
    )
    value2, gate2, low2, recept, keys = mix_and_project(
        2, kind, pair_y, ratios[2], left[2], own, sibling, recept, keys
    )
    recept, keys, values, decay, gate3 = projected(
        kind,
        (value0, value1, value2),
        (low0, low1, low2),
        (recept, keys),
        (a_xy, b_xy),
        ratios[3],
        left[3],
        own,
        sibling,
        own_value,
        sibling_value,
        lax.dynamic_slice_in_dim(fading_right_factor, z * width, width, 1),
        mine_of(fading_baseline),
    )
    entered = lax.dynamic_slice_in_dim(carried_memory, z * heads, heads, 0)
    bonus = lax.dynamic_slice_in_dim(present_reward, z * heads, heads, 0).reshape(1, width)
    states, states_in = states_of(
        extents,
        is_long.astype(f32)[None],
        keys,
        values,
        decay,
        jnp.where(is_long, entered, 0.0),
    )
    normed = sweep(
        extents,
        recept,
        keys,
        values,
        decay,
        states_in,
        bonus,
        mine_of(group_layer_scaling),
        mine_of(group_layer_shift_term),
    )
    live = lax.broadcasted_iota(jnp.int32, (rows // slot_rows, slot_rows), 1) < extents[:, None]
    live = live.reshape(rows, 1).astype(f32)
    kept0, sent0, kept1, sent1 = gated(
        kind,
        (gate0, gate1, gate2, gate3),
        own_gate,
        sibling_gate,
        normed,
        live,
    )

    states = states.reshape(lines, 2, requests, heads, span, span)
    passed = flipped_core(lax.dynamic_index_in_dim(states, 1 - core, 1, keepdims=False))
    held = lax.dynamic_index_in_dim(states, core, 1, keepdims=False)
    bundle = jnp.concatenate(
        [jnp.where(is_long, held, passed)[:, -1:], jnp.where(is_long, passed, held)], axis=1
    ).astype(bf16)
    arrived = in_order(
        dealt(lambda j: lax.dynamic_index_in_dim(bundle, j, 0, keepdims=False), z), z
    ).astype(f32)
    span_states = arrived[:, 0].reshape(1, lines * heads, span, span)
    request_states = jnp.swapaxes(arrived[:, 1:], 0, 1).reshape(
        requests, lines * heads, span, span
    )

    wide_out = 2 * final_transform.shape[1]
    beside = flipped_core(final_transform)
    out_weight = jnp.concatenate(
        [
            jnp.where(is_long, final_transform, beside),
            jnp.where(is_long, beside, final_transform),
        ],
        axis=1,
    ).reshape(lines, width, wide_out)
    out_weight = jnp.stack(
        [
            lax.dynamic_index_in_dim(out_weight, (z - k) % lines, 0, keepdims=False)
            for k in range(lines)
        ]
    )
    order = jnp.stack([(z - k) % lines for k in range(lines)]).astype(jnp.int32)
    block_of = jnp.stack(
        [(((y ^ (rel >> 1)) ^ core) * 2 + (x ^ (rel & 1))).astype(jnp.int32) for rel in range(4)]
    )
    spreads = []
    for kept, sent in ((kept0, sent0), (kept1, sent1)):
        part = jnp.concatenate([kept, flipped_core(sent)], axis=0)
        part = part.reshape(2 * rows // 4, width)
        if spreads:
            part = after(part, spreads[0][2])
        spreads.append(spread_along(part, z))
    out_pieces = []
    for piece, one, two, three, far in spreads:
        one = jnp.where(z == 0, far, one)
        three = jnp.where(z == 3, far, three)
        here, to_x, to_y, to_xy = final_product(
            block_of, (piece, one, two, three), out_weight, lines
        )
        across = lax.ppermute(to_xy, ("y", "x"), [(i, 3 - i) for i in range(4)])
        mixed_part = (
            here.astype(f32)
            + over_x(to_x).astype(f32)
            + over_y(to_y).astype(f32)
            + across.astype(f32)
        ).astype(bf16)
        out_pieces += dealt(
            lambda j: lax.dynamic_index_in_dim(mixed_part, j, 0, keepdims=False), z
        )
    mixed = laid(order, out_pieces, lines)[None]
    return mixed, span_states, request_states


def rows_kept_solution(mesh):
    placed = (
        P("seq", "mp"),
        P("seq", "mp"),
        P("seq"),
        P("mp"),
        P("mp", None, None),
        P(),
        P("seq", "mp"),
        P("seq", "mp"),
        P("seq", "mp"),
        P("seq", "mp"),
        P("mp"),
        P(),
        P(None, "mp"),
        P("mp", None),
        P("mp"),
        P("mp"),
        P("mp", "seq"),
    )
    return jax.shard_map(
        on_device,
        mesh=mesh,
        in_specs=placed,
        out_specs=(P("seq", "mp", None), P("seq", "mp", None, None), P("seq", "mp", None, None)),
        check_vma=False,
    )


def heads_kept_solution(mesh):
    seq, mp = mesh.shape["seq"], mesh.shape["mp"]
    split = Mesh(mesh.devices.reshape(seq // 2, 2, 2, mp // 2), ("z", "core", "y", "x"))
    s, m = ("z", "core"), ("y", "x")
    placed = (
        P(s, m),
        P(s, m),
        P(s),
        P(m),
        P(m, None, None),
        P(),
        P(s, m),
        P(s, m),
        P(s, m),
        P(s, m),
        P(m),
        P(),
        P(None, m),
        P(m, None),
        P(m),
        P(m),
        P(m, s),
    )
    return jax.shard_map(
        on_core,
        mesh=split,
        in_specs=placed,
        out_specs=(P(s, m, None), P(s, m, None, None), P(s, m, None, None)),
        check_vma=False,
    )


def solution(mesh):
    if mesh.shape["mp"] == 4 and mesh.shape["seq"] == 8:
        return heads_kept_solution(mesh)
    return rows_kept_solution(mesh)
```

```python
import jax
import jax.numpy as jnp
import numpy as np
from jax import lax
from jax.experimental import pallas as pl
from jax.experimental.pallas import tpu as pltpu
from jax.sharding import Mesh
from jax.sharding import PartitionSpec as P

BLK = 64


norm_eps = 0.00064
highest = lax.Precision.HIGHEST


def passed_along(x, axis, by):
    length = lax.axis_size(axis)
    pairs = [(i, i + by) for i in range(length) if 0 <= i + by < length]
    return lax.ppermute(x, axis, pairs)


def entering(value, axis, join, neutral):
    count, mine = (lax.axis_size(axis), lax.axis_index(axis))
    pieces = jax.tree.map(lambda part: lax.all_gather(part, axis), value)
    total = jax.tree.map(
        lambda part, zero: jnp.full_like(part, 0) + jnp.asarray(zero, part.dtype), value, neutral
    )

    def hop(position, total):
        longer = join(total, jax.tree.map(lambda part: part[position], pieces))
        return jax.tree.map(lambda new, old: jnp.where(position < mine, new, old), longer, total)

    return lax.fori_loop(0, count - 1, hop, total)


def mix_rows(current, previous, weight):
    here = current.astype(jnp.float32)
    return (here + weight[None, :] * (previous.astype(jnp.float32) - here)).astype(jnp.bfloat16)


def block_sweep(
    evolving_memory,
    acceptance_entries,
    lookup_entries,
    payload_entries,
    log_fading_amount,
    diagonal_reward,
):
    inclusive = jnp.cumsum(log_fading_amount, axis=0)
    exclusive = inclusive - log_fading_amount
    recept_scaled = acceptance_entries * jnp.exp(exclusive)
    keys_scaled = lookup_entries * jnp.exp(-inclusive)
    scores = jnp.einsum("ihc,jhc->hij", recept_scaled, keys_scaled, precision=highest)
    count = acceptance_entries.shape[0]
    row_index = lax.broadcasted_iota(jnp.int32, (count, count), 0)
    col_index = lax.broadcasted_iota(jnp.int32, (count, count), 1)
    scores = jnp.where((row_index > col_index)[None], scores, 0.0)
    diagonal_contribution = jnp.sum(
        acceptance_entries * diagonal_reward[None] * lookup_entries, axis=-1, keepdims=True
    )
    answer_lines = (
        jnp.einsum("hij,jhd->ihd", scores, payload_entries, precision=highest)
        + diagonal_contribution * payload_entries
    )
    answer_lines = answer_lines + jnp.einsum(
        "ihc,hcd->ihd", recept_scaled, evolving_memory, precision=highest
    )
    total = inclusive[-1]
    carried = lookup_entries * jnp.exp(total[None] - inclusive)
    new_state = jnp.exp(total)[:, :, None] * evolving_memory + jnp.einsum(
        "jhc,jhd->hcd", carried, payload_entries, precision=highest
    )
    return (new_state, answer_lines)


def continued_recurrence(
    acceptance_entries, lookup_entries, payload_entries, log_fading_amount, diagonal_reward
):
    length, per_group_view, embedding_dimension = acceptance_entries.shape
    blocks = length // BLK

    def step(evolving_memory, entry_lines):
        return block_sweep(
            evolving_memory,
            entry_lines[0],
            entry_lines[1],
            entry_lines[2],
            entry_lines[3],
            diagonal_reward,
        )

    shaped = tuple(
        (
            a.reshape(blocks, BLK, per_group_view, embedding_dimension)
            for a in (acceptance_entries, lookup_entries, payload_entries, log_fading_amount)
        )
    )
    evolving_memory, results = lax.scan(
        step,
        jnp.zeros((per_group_view, embedding_dimension, embedding_dimension), jnp.float32),
        shaped,
    )
    return (evolving_memory, results.reshape(length, per_group_view, embedding_dimension))


def combine(earlier, later):
    return (earlier[0] + later[0], jnp.exp(later[0])[:, :, None] * earlier[1] + later[1])


def shifted_rows(current, edge_row, long_rows, requests, slot_rows):
    feature_part = current.shape[1]
    long_prev = jnp.concatenate([edge_row, current[: long_rows - 1]], axis=0)
    short_view = current[long_rows:].reshape(requests, slot_rows, feature_part)
    short_prev = jnp.concatenate(
        [jnp.zeros((requests, 1, feature_part), current.dtype), short_view[:, :-1]], axis=1
    )
    short_prev = short_prev.reshape(requests * slot_rows, feature_part)
    return jnp.concatenate([long_prev, short_prev], axis=0)


def on_device(
    continued_prompt_entries,
    padded_prompt_entries,
    prompt_live_extents,
    preceding_entry_line,
    carried_memory,
    token_mixing_ratios,
    acceptance_transform,
    lookup_transform,
    payload_transform,
    gating_transform,
    fading_baseline,
    fading_left_factor,
    fading_right_factor,
    present_reward,
    group_layer_scaling,
    group_layer_shift_term,
    final_transform,
):
    long_rows = continued_prompt_entries.shape[0]
    requests = prompt_live_extents.shape[0]
    slot_rows = padded_prompt_entries.shape[0] // requests
    per_group_view, embedding_dimension = present_reward.shape
    arrived = passed_along(continued_prompt_entries[-1:], "seq", 1)
    first = lax.axis_index("seq") == 0
    edge_row = jnp.where(first, preceding_entry_line[None, :], arrived)
    current = jnp.concatenate([continued_prompt_entries, padded_prompt_entries], axis=0)
    current, edge_full = (
        lax.all_gather(current, "mp", axis=1, tiled=True),
        lax.all_gather(edge_row, "mp", axis=1, tiled=True),
    )
    previous = shifted_rows(current, edge_full, long_rows, requests, slot_rows)
    mixes = [mix_rows(current, previous, token_mixing_ratios[index]) for index in range(5)]
    total_rows = current.shape[0]
    columns = acceptance_transform.shape[1]
    pieces = (
        lax.all_gather(acceptance_transform, "seq", axis=0, tiled=True),
        lax.all_gather(lookup_transform, "seq", axis=0, tiled=True),
        lax.all_gather(payload_transform, "seq", axis=0, tiled=True),
        lax.all_gather(gating_transform, "seq", axis=0, tiled=True),
    )
    acceptance_entries, lookup_entries, payload_entries, gate = tuple(
        (
            jnp.dot(source, piece, preferred_element_type=jnp.float32)
            for source, piece in zip(mixes[:4], pieces)
        )
    )
    squeezed = jnp.tanh(
        jnp.dot(mixes[4], fading_left_factor, preferred_element_type=jnp.float32)
    ).astype(jnp.bfloat16)
    log_fading_amount = -jnp.exp(
        fading_baseline[None, :]
        + jnp.dot(squeezed, fading_right_factor, preferred_element_type=jnp.float32)
    )
    recept3, keys3, values3, decay3 = [
        a.reshape(total_rows, per_group_view, embedding_dimension)
        for a in (acceptance_entries, lookup_entries, payload_entries, log_fading_amount)
    ]
    local_state, long_out = continued_recurrence(
        recept3[:long_rows],
        keys3[:long_rows],
        values3[:long_rows],
        decay3[:long_rows],
        present_reward,
    )
    long_decay = decay3[:long_rows]
    group_total = jnp.sum(long_decay, axis=0)
    blank = (
        jnp.zeros((per_group_view, embedding_dimension), jnp.float32),
        jnp.zeros((per_group_view, embedding_dimension, embedding_dimension), jnp.float32),
    )
    prefix_total, prefix_state = entering((group_total, local_state), "seq", combine, blank)
    incoming = jnp.exp(prefix_total)[:, :, None] * carried_memory + prefix_state
    before_row = jnp.cumsum(long_decay, axis=0) - long_decay
    long_out = long_out + jnp.einsum(
        "ihc,hcd->ihd", recept3[:long_rows] * jnp.exp(before_row), incoming, precision=highest
    )
    span_end = jnp.exp(group_total)[:, :, None] * incoming + local_state
    live_rows = (
        lax.broadcasted_iota(jnp.int32, (requests, slot_rows), 1) < prompt_live_extents[:, None]
    )
    live_flat = live_rows.reshape(requests * slot_rows).astype(jnp.float32)[:, None, None]
    short_shape = (requests, slot_rows, per_group_view, embedding_dimension)
    short_recept = recept3[long_rows:].reshape(short_shape)
    short_keys = (keys3[long_rows:] * live_flat).reshape(short_shape)
    short_values = values3[long_rows:].reshape(short_shape)
    short_decay = (decay3[long_rows:] * live_flat).reshape(short_shape)
    zeroed_memory = jnp.zeros(
        (per_group_view, embedding_dimension, embedding_dimension), jnp.float32
    )

    def request_pass(acceptance_lines, lookup_table, payload_table, fading_table):
        return block_sweep(
            zeroed_memory,
            acceptance_lines,
            lookup_table,
            payload_table,
            fading_table,
            present_reward,
        )

    request_states, short_out = jax.vmap(request_pass)(
        short_recept, short_keys, short_values, short_decay
    )
    wkv = jnp.concatenate(
        [long_out, short_out.reshape(requests * slot_rows, per_group_view, embedding_dimension)],
        axis=0,
    )
    mean = jnp.mean(wkv, axis=-1, keepdims=True)
    centred = wkv - mean
    variance = jnp.mean(centred * centred, axis=-1, keepdims=True)
    normed = (centred * lax.rsqrt(variance + norm_eps)).reshape(
        total_rows, columns
    ) * group_layer_scaling[None, :] + group_layer_shift_term[None, :]
    row_live = jnp.concatenate(
        [jnp.ones((long_rows,), dtype=bool), live_rows.reshape(requests * slot_rows)], axis=0
    )
    hidden = jnp.where(row_live[:, None], normed * jax.nn.silu(gate), 0.0).astype(jnp.bfloat16)
    full_out = lax.all_gather(final_transform, "seq", axis=1, tiled=True)
    mixed_rows = lax.psum_scatter(
        jnp.dot(hidden, full_out, preferred_element_type=jnp.float32),
        "mp",
        scatter_dimension=0,
        tiled=True,
    )
    return (mixed_rows.astype(jnp.bfloat16)[None], span_end[None], request_states)


f32 = jnp.float32
bf16 = jnp.bfloat16
VMEM_LIMIT = 56 * 1024 * 1024
TILE = 256


def in_vmem():
    return pl.BlockSpec(memory_space=pltpu.VMEM)


def in_smem():
    return pl.BlockSpec(memory_space=pltpu.SMEM)


def takes(us):
    return pl.CostEstimate(
        flops=int(us * 1.15e9), bytes_accessed=int(us * 3.0e6), transcendentals=0
    )


def kernel_params():
    return pltpu.CompilerParams(vmem_limit_bytes=VMEM_LIMIT)


EXTRA = 16


def here_and_step(x_ref, is_long, period, tile):
    rows = x_ref.shape[1] - EXTRA
    here = x_ref[tile, 0:rows, :].astype(f32)
    above = x_ref[jnp.maximum(tile - 1, 0), rows - 16 : rows, :].astype(f32)[15:16]
    first = jnp.where(is_long == 1, x_ref[0, rows : rows + 16, :].astype(f32)[0:1], 0.0)
    row = lax.broadcasted_iota(jnp.int32, here.shape, 0)
    before = jnp.where(row == 0, above, pltpu.roll(here, 1, 0))
    start = ((row + tile * rows) & (period - 1)) == 0
    before = jnp.where(start, first, before)
    return here, before - here


def given_kernel(kind, extents, long_ref, short_ref, out_ref):
    rows = long_ref.shape[0]
    is_long = kind[0] == 1
    out_ref[0:rows, :] = jnp.where(is_long, short_ref[...], long_ref[...])
    lane = lax.broadcasted_iota(jnp.int32, (EXTRA, out_ref.shape[1]), 1)
    line = jnp.zeros(lane.shape, f32)
    for n in range(extents.shape[0]):
        line = jnp.where(lane == n, extents[n].astype(f32), line)
    out_ref[rows : rows + EXTRA, :] = line.astype(bf16)


def given_to_other_core(kind, extents, long_rows, short_rows):
    rows, columns = long_rows.shape
    return pl.pallas_call(
        given_kernel,
        out_shape=jax.ShapeDtypeStruct((rows + EXTRA, columns), bf16),
        in_specs=[in_smem()] * 2 + [in_vmem()] * 2,
        out_specs=in_vmem(),
        compiler_params=kernel_params(),
        cost_estimate=takes(1.5),
    )(kind, extents, long_rows, short_rows)


def block_kernel(kind, extents, long_ref, short_ref, taken, edge, out_ref):
    rows = long_ref.shape[0]
    depth = out_ref.shape[2]
    is_long = kind[0] == 1
    count = extents.shape[0]
    row = lax.broadcasted_iota(jnp.int32, (EXTRA, depth), 0)
    lane = lax.broadcasted_iota(jnp.int32, (EXTRA, depth), 1)
    other = taken[rows : rows + EXTRA, 0:depth].astype(f32)
    line = jnp.where(is_long, pltpu.roll(other, count, 1), other)
    own_at = jnp.where(is_long, 0, count)
    for n in range(count):
        line = jnp.where(lane == own_at + n, extents[n].astype(f32), line)
    for half in range(2):
        start = jnp.where(is_long, half, 1 - half) * depth
        at = pl.ds(pl.multiple_of(start, depth), depth)
        got = taken[0:rows, at]
        out_ref[half, 0:rows, :] = jnp.where(is_long, long_ref[:, at], got)
        out_ref[half, rows : 2 * rows, :] = jnp.where(is_long, got, short_ref[:, at])
        first = edge[:, at].astype(f32)
        out_ref[half, 2 * rows :, :] = jnp.where(row == 0, first, line).astype(bf16)


def block_of_chip(kind, extents, long_rows, short_rows, taken, edge):
    rows, columns = long_rows.shape
    return pl.pallas_call(
        block_kernel,
        out_shape=jax.ShapeDtypeStruct((2, 2 * rows + EXTRA, columns // 2), bf16),
        in_specs=[in_smem()] * 2 + [in_vmem()] * 4,
        out_specs=in_vmem(),
        compiler_params=kernel_params(),
        cost_estimate=takes(1.5),
    )(kind, extents, long_rows, short_rows, taken, edge)


def half_block(shape):
    return pl.BlockSpec((1,) + shape[1:], lambda i: (i,) + (0,) * (len(shape) - 1))


def gather_blocks(kind, own, rest, held):
    held[kind[6]] = own[...]
    for k in range(3):
        held[kind[7 + k]] = rest[k]


def mix_kernel(kind, own, rest, ratios, left, kv_mix, r_mix, gate_mix, squeezed, held):
    gather_blocks(kind, own.at[0], rest.at[0], held)

    @pl.loop(0, held.shape[0], unroll=2)
    def _(tile):
        here, step = here_and_step(held, kind[0], kind[1], tile)
        at = pl.ds(pl.multiple_of(tile * TILE, TILE), TILE)

        def mix(which):
            return (here + ratios[0, which : which + 1, :] * step).astype(bf16)

        r_mix[0, at, :] = mix(0)
        kv_mix[0, 0, at, :] = mix(1)
        kv_mix[0, 1, at, :] = mix(2)
        gate_mix[0, at, :] = mix(3)
        squeezed[0, at, :] = jnp.dot(mix(4), left[0], preferred_element_type=f32)


def mixes_of(kind, own, rest, ratios, left):
    rows, depth = own.shape[1] - EXTRA, own.shape[2]
    lines = rest.shape[1] + 1
    whole = lines * rows
    outs = [
        jax.ShapeDtypeStruct((2, 2, whole, depth), bf16),
        jax.ShapeDtypeStruct((2, whole, depth), bf16),
        jax.ShapeDtypeStruct((2, whole, depth), bf16),
        jax.ShapeDtypeStruct((2, whole, left.shape[2]), f32),
    ]
    return pl.pallas_call(
        mix_kernel,
        grid=(2,),
        out_shape=outs,
        in_specs=[in_smem()] + [half_block(a.shape) for a in (own, rest, ratios, left)],
        out_specs=[half_block(out.shape) for out in outs],
        scratch_shapes=[pltpu.VMEM((lines, rows + EXTRA, depth), bf16)],
        compiler_params=kernel_params(),
        cost_estimate=takes(7),
    )(kind, own, rest, ratios, left)


def project_kernel(
    kind,
    mix0,
    mix1,
    mix2,
    low0,
    low1,
    low2,
    own0,
    own1,
    rest0,
    rest1,
    ratios,
    left,
    own_weight,
    sibling_weight,
    right,
    base,
    keys_ref,
    values_ref,
    decay_ref,
    r_mix,
    gate_mix,
    held,
):
    tile = pl.program_id(0)

    @pl.when(tile == 0)
    def _():
        for half, (own, rest) in enumerate(((own0, rest0), (own1, rest1))):
            gather_blocks(kind, own, rest, held.at[half])

    totals = [None] * 2

    def add(which, rel, half, mixed):
        weight = (own_weight, sibling_weight)[half][kind[2 + rel], which]
        part = jnp.dot(mixed, weight, preferred_element_type=f32)
        totals[which] = part if totals[which] is None else totals[which] + part

    squeezed = low0[0] + low0[1] + low1[0] + low1[1] + low2[0] + low2[1]
    for half in range(2):
        here, step = here_and_step(held.at[half], kind[0], kind[1], tile)

        def mix(which):
            return (here + ratios[half, which : which + 1, :] * step).astype(bf16)

        r_mix[half] = mix(0)
        add(0, 3, half, mix(1))
        add(1, 3, half, mix(2))
        gate_mix[half] = mix(3)
        squeezed = squeezed + jnp.dot(mix(4), left[half], preferred_element_type=f32)
    for rel, mixes in enumerate((mix0, mix1, mix2)):
        for half in range(2):
            for which in range(2):
                add(which, rel, half, mixes[half, which])
    keys_ref[...] = totals[0]
    values_ref[...] = totals[1]
    squeezed = jnp.tanh(squeezed).astype(bf16)
    grown = jnp.dot(squeezed, right[...], preferred_element_type=f32)
    decay_ref[...] = -jnp.exp(base[...] + grown)


def projected(kind, mixes, lows, owns, rests, *rest):
    rows, depth = mixes[0].shape[2:]
    own_weight = rest[2]
    width, rank = own_weight.shape[3], lows[0].shape[2]
    flat = jax.ShapeDtypeStruct((rows, width), f32)
    wide = jax.ShapeDtypeStruct((2, rows, depth), bf16)
    tile_of = pl.BlockSpec((TILE, width), lambda i: (i, 0))
    wide_of = pl.BlockSpec((2, TILE, depth), lambda i: (0, i, 0))
    return pl.pallas_call(
        project_kernel,
        grid=(rows // TILE,),
        out_shape=[flat] * 3 + [wide] * 2,
        in_specs=[in_smem()]
        + [pl.BlockSpec((2, 2, TILE, depth), lambda i: (0, 0, i, 0))] * 3
        + [pl.BlockSpec((2, TILE, rank), lambda i: (0, i, 0))] * 3
        + [in_vmem()] * (4 + len(rest)),
        out_specs=[tile_of] * 3 + [wide_of] * 2,
        scratch_shapes=[pltpu.VMEM((2, rests[0].shape[0] + 1) + owns[0].shape, bf16)],
        compiler_params=kernel_params(),
        cost_estimate=takes(12),
    )(kind, *mixes, *lows, *owns, *rests, *rest)


def plain_kernel(kind, mix0, mix1, mix2, mix3, own, sibling, out_ref):
    half = pl.program_id(0)
    part = None
    for rel, mixes in enumerate((mix0, mix1, mix2, mix3)):
        weight = jnp.where(half == 0, own[kind[2 + rel], 0], sibling[kind[2 + rel], 0])
        new = jnp.dot(mixes[0], weight, preferred_element_type=f32)
        part = new if part is None else part + new

    @pl.when(half == 0)
    def _():
        out_ref[...] = part

    @pl.when(half == 1)
    def _():
        out_ref[...] += part


def plain_product(kind, mixes, own, sibling):
    rows, width = mixes[0].shape[1], own.shape[3]
    return pl.pallas_call(
        plain_kernel,
        grid=(2,),
        out_shape=jax.ShapeDtypeStruct((rows, width), f32),
        in_specs=[in_smem()] + [half_block(mix.shape) for mix in mixes] + [in_vmem()] * 2,
        out_specs=pl.BlockSpec((rows, width), lambda i: (0, 0)),
        compiler_params=kernel_params(),
        cost_estimate=takes(6),
    )(kind, *mixes, own, sibling)


def gate_kernel(
    kind,
    lengths,
    mix0,
    mix1,
    mix2,
    mix3,
    own,
    sibling,
    normed,
    kept0,
    sent0,
    kept1,
    sent1,
    total,
):
    half = pl.program_id(0)
    part = None
    for rel, mixes in enumerate((mix0, mix1, mix2, mix3)):
        weight = jnp.where(half == 0, own[kind[2 + rel], 0], sibling[kind[2 + rel], 0])
        new = jnp.dot(mixes[0], weight, preferred_element_type=f32)
        part = new if part is None else part + new

    @pl.when(half == 0)
    def _():
        total[...] = part

    @pl.when(half == 1)
    def _():
        gate = total[...] + part
        value = normed[...] * (gate * jax.nn.sigmoid(gate))
        row = lax.broadcasted_iota(jnp.int32, (BLK, value.shape[1]), 0)
        is_long = kind[0] == 1
        half_rows = BLK // 2

        def lived(n):
            block = value[n * BLK : (n + 1) * BLK]
            return jnp.where(row < lengths[n], block, 0.0).astype(bf16)

        for line in range(kept0.shape[1]):
            for block in range(2):
                even, odd = lived(4 * line + block), lived(4 * line + 2 + block)
                kept = jnp.where(is_long, even, odd)
                sent = jnp.where(is_long, odd, even)
                kept0[block, line] = kept[:half_rows]
                kept1[block, line] = kept[half_rows:]
                sent0[block, line] = sent[:half_rows]
                sent1[block, line] = sent[half_rows:]


def gated(kind, lengths, mixes, own, sibling, normed):
    rows, width = normed.shape
    quarter = jax.ShapeDtypeStruct((2, rows // TILE, BLK // 2, width), bf16)
    return pl.pallas_call(
        gate_kernel,
        grid=(2,),
        out_shape=[quarter] * 4,
        in_specs=[in_smem()] * 2 + [half_block(mix.shape) for mix in mixes] + [in_vmem()] * 3,
        out_specs=[pl.BlockSpec(quarter.shape, lambda i: (0, 0, 0, 0))] * 4,
        scratch_shapes=[pltpu.VMEM((rows, width), f32)],
        compiler_params=kernel_params(),
        cost_estimate=takes(7),
    )(kind, lengths, *mixes, own, sibling, normed)


def head_blocks(heads):
    width = heads * BLK
    tall = lax.broadcasted_iota(jnp.int32, (width, width), 0) // BLK
    wide = lax.broadcasted_iota(jnp.int32, (width, width), 1) // BLK
    return tall == wide


def state_kernel(lengths, carry, k_ref, v_ref, w_ref, s_ref, state_ref, entered_ref, hold):
    span, width = BLK, k_ref.shape[1]
    heads = width // span
    row = lax.broadcasted_iota(jnp.int32, (span, width), 0)
    lane = lax.broadcasted_iota(jnp.int32, (span, width), 1)
    for h in range(heads):
        hold[:, h * span : (h + 1) * span] = s_ref[h]

    @pl.loop(0, k_ref.shape[0] // span, unroll=8)
    def _(n):
        at = pl.ds(pl.multiple_of(n * span, span), span)
        live = row < lengths[n]
        k = jnp.where(live, k_ref[at, :], 0.0)
        total = jnp.where(live, w_ref[at, :], 0.0)
        after_row = jnp.zeros_like(total)
        half = 1
        while half < span:
            upper = (row & half) != 0
            across = jnp.where(
                upper, pltpu.roll(total, half, 0), pltpu.roll(total, span - half, 0)
            )
            after_row = after_row + jnp.where(upper, 0.0, across)
            total = total + across
            half *= 2
        added = lax.dot_general(
            (k * jnp.exp(after_row)).astype(bf16),
            v_ref[at, :].astype(bf16),
            (((0,), (0,)), ((), ())),
            preferred_element_type=f32,
        )
        fresh = jnp.zeros((span, width), f32)
        for h in range(heads):
            fresh = jnp.where(lane // span == h, added[h * span : (h + 1) * span], fresh)
        twice = jnp.concatenate([total] * 2, axis=0)
        turned_parts = []
        for p in range(width // (2 * span)):
            flipped = jnp.transpose(twice[:, p * 2 * span : (p + 1) * 2 * span])
            turned_parts.append(
                jnp.where(lane[:, : 2 * span] < span, flipped[:span], flipped[span:])
            )
        fade = jnp.exp(jnp.concatenate(turned_parts, axis=1))
        entered = hold[...] * carry[0]
        entered_ref[n] = entered.astype(bf16)
        state = fade * entered + fresh
        hold[...] = state
        for h in range(heads):
            state_ref[n, h] = state[:, h * span : (h + 1) * span]


def states_of(lengths, carry, k, v, w, state):
    rows, width = k.shape
    heads = width // BLK
    return pl.pallas_call(
        state_kernel,
        out_shape=[
            jax.ShapeDtypeStruct((rows // BLK, heads, BLK, BLK), f32),
            jax.ShapeDtypeStruct((rows // BLK, BLK, width), bf16),
        ],
        in_specs=[in_smem()] * 2 + [in_vmem()] * 4,
        out_specs=[in_vmem()] * 2,
        scratch_shapes=[pltpu.VMEM((BLK, width), f32)],
        compiler_params=kernel_params(),
        cost_estimate=takes(7),
    )(lengths, carry, k, v, w, state)


def sweep_kernel(lengths, r_ref, k_ref, v_ref, w_ref, entered_ref, u_ref, gain, bias, out_ref):
    span, width = BLK, r_ref.shape[1]
    heads = width // span
    row = lax.broadcasted_iota(jnp.int32, (span, width), 0)
    lane = lax.broadcasted_iota(jnp.int32, (span, width), 1)
    col = lane % span
    same_head = head_blocks(heads)

    def spread(value):
        stacked = jnp.concatenate([value.astype(bf16)] * heads, axis=0)
        return jnp.where(same_head, stacked, jnp.zeros_like(stacked))

    def against(a, b):
        return lax.dot_general(a, b, (((1,), (1,)), ((), ())), preferred_element_type=f32)

    @pl.loop(0, r_ref.shape[0] // span, unroll=4)
    def _(n):
        at = pl.ds(pl.multiple_of(n * span, span), span)
        live = row < lengths[n]
        r, v = r_ref[at, :], v_ref[at, :]
        k = jnp.where(live, k_ref[at, :], 0.0)
        total = jnp.where(live, w_ref[at, :], 0.0)
        before = jnp.zeros_like(total)
        after_row = jnp.zeros_like(total)
        scores = against((r * u_ref[...]).astype(bf16), spread(k))
        scores = jnp.where(row == col, scores, 0.0)
        level = 0
        while (1 << level) < span:
            half = 1 << level
            upper = (row & half) != 0
            if level:
                scale = jnp.exp(jnp.where(upper, before, after_row))
                part = against((r * scale).astype(bf16), spread(k * scale))
            else:
                part = against(r.astype(bf16), spread(k))
            pair = upper & (((row >> level) ^ (col >> level)) == 1)
            scores = jnp.where(pair, part, scores)
            across = jnp.where(
                upper, pltpu.roll(total, half, 0), pltpu.roll(total, span - half, 0)
            )
            before = before + jnp.where(upper, across, 0.0)
            after_row = after_row + jnp.where(upper, 0.0, across)
            total = total + across
            level += 1
        out = jnp.dot(scores.astype(bf16), spread(v), preferred_element_type=f32)
        out = out + jnp.dot(
            (r * jnp.exp(before)).astype(bf16),
            spread(entered_ref[n]),
            preferred_element_type=f32,
        )
        out_ref[at, :] = out

    ones = jnp.where(same_head, 1.0, 0.0).astype(bf16)

    def head_mean(value):
        high = value.astype(bf16)
        low = (value - high.astype(f32)).astype(bf16)
        both = jnp.dot(high, ones, preferred_element_type=f32) + jnp.dot(
            low, ones, preferred_element_type=f32
        )
        return both * (1.0 / span)

    @pl.loop(0, r_ref.shape[0] // TILE, unroll=2)
    def _(tile):
        at = pl.ds(pl.multiple_of(tile * TILE, TILE), TILE)
        value = out_ref[at, :]
        centred = value - head_mean(value)
        spread_of = head_mean(centred * centred)
        out_ref[at, :] = centred * lax.rsqrt(spread_of + norm_eps) * gain[...] + bias[...]


def sweep(lengths, r, k, v, w, entered, bonus, gain, bias):
    return pl.pallas_call(
        sweep_kernel,
        out_shape=jax.ShapeDtypeStruct(r.shape, f32),
        in_specs=[in_smem()] + [in_vmem()] * 8,
        out_specs=in_vmem(),
        compiler_params=kernel_params(),
        cost_estimate=takes(12),
    )(lengths, r, k, v, w, entered, bonus, gain, bias)


def final_kernel(block_of, h0, h1, h2, h3, weight, o0, o1, o2, o3, hold):
    @pl.loop(0, hold.shape[1] // TILE, unroll=2)
    def _(tile):
        at = pl.ds(pl.multiple_of(tile * TILE, TILE), TILE)
        total = None
        for k, piece in enumerate((h0, h1, h2, h3)):
            part = jnp.dot(piece[...], weight[k, :, at], preferred_element_type=f32)
            total = part if total is None else total + part
        hold[:, at] = total.astype(bf16)

    block = hold.shape[0] // 4
    for rel, out in enumerate((o0, o1, o2, o3)):
        at = pl.ds(pl.multiple_of(block_of[rel] * block, block), block)
        out[...] = hold[at, :].reshape(out.shape)


def final_product(block_of, pieces, weight, lines):
    rows, width = pieces[0].shape[0], weight.shape[2]
    out = jax.ShapeDtypeStruct((lines, rows // 4 // lines, width), bf16)
    return pl.pallas_call(
        final_kernel,
        out_shape=[out] * 4,
        in_specs=[in_smem()] + [in_vmem()] * 5,
        out_specs=[in_vmem()] * 4,
        scratch_shapes=[pltpu.VMEM((rows, width), bf16)],
        compiler_params=kernel_params(),
        cost_estimate=takes(4.5),
    )(block_of, *pieces, weight)


def lay_kernel(at, *refs):
    pieces, out_ref = refs[:-1], refs[-1]
    rows, width = pieces[0].shape
    lines = out_ref.shape[1] // width
    for n, piece in enumerate(pieces):
        column = pl.multiple_of(at[n % lines] * width, width)
        out_ref[n // lines * rows : (n // lines + 1) * rows, pl.ds(column, width)] = piece[...]


def laid(at, pieces, lines):
    rows, width = pieces[0].shape
    return pl.pallas_call(
        lay_kernel,
        out_shape=jax.ShapeDtypeStruct((len(pieces) // lines * rows, lines * width), bf16),
        in_specs=[in_smem()] + [in_vmem()] * len(pieces),
        out_specs=in_vmem(),
        compiler_params=kernel_params(),
        cost_estimate=takes(2),
    )(at, *pieces)


def after(value, *others):
    return lax.optimization_barrier((value,) + others)[0]


def turned(x, axis, by):
    length = lax.axis_size(axis)
    return lax.ppermute(x, axis, [(i, (i + by) % length) for i in range(length)])


def flipped_core(x):
    return lax.ppermute(x, "core", [(0, 1), (1, 0)])


def over_x(x):
    return lax.ppermute(x, "x", [(0, 1), (1, 0)])


def over_y(x):
    return lax.ppermute(x, "y", [(0, 1), (1, 0)])


def dealt(blocks, z):
    length = lax.axis_size("z")
    return [blocks(z)] + [turned(blocks((z + k) % length), "z", k) for k in range(1, length)]


def spread_along(piece, z):
    one = lax.ppermute(piece, "z", [(0, 1), (1, 2), (2, 3)])
    three = lax.ppermute(piece, "z", [(1, 0), (2, 1), (3, 2)])
    two = turned(piece, "z", 2)
    far = lax.ppermute(two, "z", [(1, 0), (2, 3)])
    return piece, one, two, three, far


def in_place(spread, z, at=0):
    piece, one, two, three, far = spread
    whole = jnp.zeros((4,) + piece.shape, piece.dtype)
    for k, part in ((1, one), (2, two), (3, three)):
        whole = lax.dynamic_update_index_in_dim(whole, part, (z - k) % 4, 0)
    far_at = jnp.where(z == 0, 3, jnp.where(z == 3, 0, z))
    whole = lax.dynamic_update_index_in_dim(whole, far, far_at, 0)
    return lax.dynamic_update_index_in_dim(whole, piece, z, 0)


def in_order(pieces, z):
    length = len(pieces)
    whole = jnp.zeros((length,) + pieces[0].shape, pieces[0].dtype)
    for k, piece in enumerate(pieces):
        whole = lax.dynamic_update_index_in_dim(whole, piece, (z - k) % length, 0)
    return whole


def on_core(
    continued_prompt_entries,
    padded_prompt_entries,
    prompt_live_extents,
    preceding_entry_line,
    carried_memory,
    token_mixing_ratios,
    acceptance_transform,
    lookup_transform,
    payload_transform,
    gating_transform,
    fading_baseline,
    fading_left_factor,
    fading_right_factor,
    present_reward,
    group_layer_scaling,
    group_layer_shift_term,
    final_transform,
):
    z, core = lax.axis_index("z"), lax.axis_index("core")
    y, x = lax.axis_index("y"), lax.axis_index("x")
    mp = 2 * y + x
    is_long = core == 0
    lines = lax.axis_size("z")
    group_rows, columns = continued_prompt_entries.shape
    requests = prompt_live_extents.shape[0]
    slot_rows = group_rows // requests
    heads, span = present_reward.shape
    heads = heads // lines
    width = heads * span
    depth = acceptance_transform.shape[0]
    rows = 2 * lines * group_rows

    kind = jnp.stack(
        [is_long.astype(jnp.int32), jnp.where(is_long, rows, slot_rows).astype(jnp.int32)]
        + [(mp ^ rel).astype(jnp.int32) for rel in range(4)]
        + [((z - k) % lines).astype(jnp.int32) for k in range(4)]
    )
    given = given_to_other_core(
        kind, prompt_live_extents, continued_prompt_entries, padded_prompt_entries
    )
    taken = flipped_core(given)
    block = block_of_chip(
        kind,
        prompt_live_extents,
        continued_prompt_entries,
        padded_prompt_entries,
        taken,
        preceding_entry_line[None],
    )
    (
        block,
        acceptance_transform,
        lookup_transform,
        payload_transform,
        gating_transform,
        final_transform,
        token_mixing_ratios,
        fading_left_factor,
        fading_right_factor,
        fading_baseline,
        present_reward,
        group_layer_scaling,
        group_layer_shift_term,
        carried_memory,
    ) = lax.optimization_barrier(
        (
            block,
            acceptance_transform,
            lookup_transform,
            payload_transform,
            gating_transform,
            final_transform,
            token_mixing_ratios,
            fading_left_factor,
            fading_right_factor,
            fading_baseline,
            present_reward,
            group_layer_scaling,
            group_layer_shift_term,
            carried_memory,
        )
    )
    spread = spread_along(block, z)
    _, one, two, three, far = spread
    own_x, own_y = over_x(block), over_y(block)
    own_xy = (over_y(own_x[0]), over_x(own_y[1]))
    rest = jnp.stack([jnp.where(z == 0, far, one), two, jnp.where(z == 3, far, three)], axis=1)
    rest_x, rest_y = over_x(rest), over_y(rest)
    rest_xy = (over_y(rest_x[0]), over_x(rest_y[1]))
    extents = in_order(
        [part[2 * group_rows + 1, : 2 * requests] for part in (block[0],) + tuple(rest[0])], z
    ).reshape(2 * lines * requests)
    extents = jnp.where(is_long, slot_rows, extents.astype(jnp.int32)).astype(jnp.int32)

    def chunk_order(whole):
        split = whole.reshape((4, 2, depth) + whole.shape[1:])
        parts = []
        for rel in range(4):
            both = split[mp ^ rel]
            parts.append(jnp.where(is_long, both, both[::-1]))
        return parts

    ratios = [part.transpose(0, 2, 1) for part in chunk_order(token_mixing_ratios.T)]
    left = chunk_order(fading_left_factor)

    def columns_of(weights, *ready):
        stacked = jnp.stack(weights)

        def block(j):
            return lax.dynamic_slice_in_dim(stacked, j * width, width, 2)

        blocks = [block((z + k) % lines) for k in range(lines)]
        blocks = lax.optimization_barrier((tuple(blocks),) + ready)[0]
        pieces = [blocks[0]] + [turned(blocks[k], "z", k) for k in range(1, lines)]
        return pieces

    def both_cores(pieces):
        return in_order(pieces, z), in_order([flipped_core(piece) for piece in pieces], z)

    kv_pieces = columns_of([lookup_transform, payload_transform], rest)
    r_pieces = columns_of([acceptance_transform], kv_pieces[2])
    gate_pieces = columns_of([gating_transform], r_pieces[2])
    own_kv, sibling_kv = both_cores(after(tuple(kv_pieces), rest_x, rest_y))

    def mine_of(vector):
        return lax.dynamic_slice_in_dim(vector, z * width, width, 0)[None]

    kv0, r0, gate0, low0 = mixes_of(kind, block, rest, ratios[0], left[0])
    kv1, r1, gate1, low1 = mixes_of(kind, own_x, rest_x, ratios[1], left[1])
    kv2, r2, gate2, low2 = mixes_of(kind, own_y, rest_y, ratios[2], left[2])
    keys, values, decay, r3, gate3 = projected(
        kind,
        (kv0, kv1, kv2),
        (low0, low1, low2),
        own_xy,
        rest_xy,
        ratios[3],
        left[3],
        own_kv,
        sibling_kv,
        lax.dynamic_slice_in_dim(fading_right_factor, z * width, width, 1),
        mine_of(fading_baseline),
    )
    own_r, sibling_r = both_cores(after(tuple(r_pieces), decay))
    recept = plain_product(kind, (r0, r1, r2, r3), own_r, sibling_r)
    entered = lax.dynamic_slice_in_dim(carried_memory, z * heads, heads, 0)
    bonus = lax.dynamic_slice_in_dim(present_reward, z * heads, heads, 0).reshape(1, width)
    states, states_in = states_of(
        extents,
        is_long.astype(f32)[None],
        keys,
        values,
        decay,
        jnp.where(is_long, entered, 0.0),
    )
    normed = sweep(
        extents,
        recept,
        keys,
        values,
        decay,
        states_in,
        bonus,
        mine_of(group_layer_scaling),
        mine_of(group_layer_shift_term),
    )
    own_gate, sibling_gate = both_cores(after(tuple(gate_pieces), states))
    kept0, sent0, kept1, sent1 = gated(
        kind, extents, (gate0, gate1, gate2, gate3), own_gate, sibling_gate, normed
    )

    states = states.reshape(lines, 2, requests, heads, span, span)
    passed = flipped_core(lax.dynamic_index_in_dim(states, 1 - core, 1, keepdims=False))
    held = lax.dynamic_index_in_dim(states, core, 1, keepdims=False)
    bundle = jnp.concatenate(
        [jnp.where(is_long, held, passed)[:, -1:], jnp.where(is_long, passed, held)], axis=1
    ).astype(bf16)
    bundle = after(bundle, gate_pieces[2])
    arrived = in_order(
        dealt(lambda j: lax.dynamic_index_in_dim(bundle, j, 0, keepdims=False), z), z
    ).astype(f32)
    span_states = arrived[:, 0].reshape(1, lines * heads, span, span)
    request_states = jnp.swapaxes(arrived[:, 1:], 0, 1).reshape(
        requests, lines * heads, span, span
    )

    wide_out = 2 * final_transform.shape[1]
    beside = flipped_core(final_transform)
    out_weight = jnp.concatenate(
        [
            jnp.where(is_long, final_transform, beside),
            jnp.where(is_long, beside, final_transform),
        ],
        axis=1,
    ).reshape(lines, width, wide_out)
    out_weight = jnp.stack(
        [
            lax.dynamic_index_in_dim(out_weight, (z - k) % lines, 0, keepdims=False)
            for k in range(lines)
        ]
    )
    order = jnp.stack([(z - k) % lines for k in range(lines)]).astype(jnp.int32)
    block_of = jnp.stack(
        [(((y ^ (rel >> 1)) ^ core) * 2 + (x ^ (rel & 1))).astype(jnp.int32) for rel in range(4)]
    )
    spreads = []
    for kept, sent in ((kept0, sent0), (kept1, sent1)):
        part = jnp.concatenate([kept, flipped_core(sent)], axis=0)
        part = part.reshape(2 * rows // 4, width)
        if spreads:
            part = after(part, spreads[0][2])
        spreads.append(spread_along(part, z))
    out_pieces = []
    for piece, one, two, three, far in spreads:
        one = jnp.where(z == 0, far, one)
        three = jnp.where(z == 3, far, three)
        here, to_x, to_y, to_xy = final_product(
            block_of, (piece, one, two, three), out_weight, lines
        )
        across = lax.ppermute(to_xy, ("y", "x"), [(i, 3 - i) for i in range(4)])
        mixed_part = (
            here.astype(f32)
            + over_x(to_x).astype(f32)
            + over_y(to_y).astype(f32)
            + across.astype(f32)
        ).astype(bf16)
        out_pieces += dealt(
            lambda j: lax.dynamic_index_in_dim(mixed_part, j, 0, keepdims=False), z
        )
    mixed = laid(order, out_pieces, lines)[None]
    return mixed, span_states, request_states


def rows_kept_solution(mesh):
    placed = (
        P("seq", "mp"),
        P("seq", "mp"),
        P("seq"),
        P("mp"),
        P("mp", None, None),
        P(),
        P("seq", "mp"),
        P("seq", "mp"),
        P("seq", "mp"),
        P("seq", "mp"),
        P("mp"),
        P(),
        P(None, "mp"),
        P("mp", None),
        P("mp"),
        P("mp"),
        P("mp", "seq"),
    )
    return jax.shard_map(
        on_device,
        mesh=mesh,
        in_specs=placed,
        out_specs=(P("seq", "mp", None), P("seq", "mp", None, None), P("seq", "mp", None, None)),
        check_vma=False,
    )


def heads_kept_solution(mesh):
    seq, mp = mesh.shape["seq"], mesh.shape["mp"]
    split = Mesh(mesh.devices.reshape(seq // 2, 2, 2, mp // 2), ("z", "core", "y", "x"))
    s, m = ("z", "core"), ("y", "x")
    placed = (
        P(s, m),
        P(s, m),
        P(s),
        P(m),
        P(m, None, None),
        P(),
        P(s, m),
        P(s, m),
        P(s, m),
        P(s, m),
        P(m),
        P(),
        P(None, m),
        P(m, None),
        P(m),
        P(m),
        P(m, s),
    )
    return jax.shard_map(
        on_core,
        mesh=split,
        in_specs=placed,
        out_specs=(P(s, m, None), P(s, m, None, None), P(s, m, None, None)),
        check_vma=False,
    )


def solution(mesh):
    if mesh.shape["mp"] == 4 and mesh.shape["seq"] == 8:
        return heads_kept_solution(mesh)
    return rows_kept_solution(mesh)
```

```python
import jax
import jax.numpy as jnp
import numpy as np
from jax import lax
from jax.experimental import pallas as pl
from jax.experimental.pallas import tpu as pltpu
from jax.sharding import Mesh
from jax.sharding import PartitionSpec as P

BLK = 64


norm_eps = 0.00064
highest = lax.Precision.HIGHEST


def passed_along(x, axis, by):
    length = lax.axis_size(axis)
    pairs = [(i, i + by) for i in range(length) if 0 <= i + by < length]
    return lax.ppermute(x, axis, pairs)


def entering(value, axis, join, neutral):
    count, mine = (lax.axis_size(axis), lax.axis_index(axis))
    pieces = jax.tree.map(lambda part: lax.all_gather(part, axis), value)
    total = jax.tree.map(
        lambda part, zero: jnp.full_like(part, 0) + jnp.asarray(zero, part.dtype), value, neutral
    )

    def hop(position, total):
        longer = join(total, jax.tree.map(lambda part: part[position], pieces))
        return jax.tree.map(lambda new, old: jnp.where(position < mine, new, old), longer, total)

    return lax.fori_loop(0, count - 1, hop, total)


def mix_rows(current, previous, weight):
    here = current.astype(jnp.float32)
    return (here + weight[None, :] * (previous.astype(jnp.float32) - here)).astype(jnp.bfloat16)


def block_sweep(
    evolving_memory,
    acceptance_entries,
    lookup_entries,
    payload_entries,
    log_fading_amount,
    diagonal_reward,
):
    inclusive = jnp.cumsum(log_fading_amount, axis=0)
    exclusive = inclusive - log_fading_amount
    recept_scaled = acceptance_entries * jnp.exp(exclusive)
    keys_scaled = lookup_entries * jnp.exp(-inclusive)
    scores = jnp.einsum("ihc,jhc->hij", recept_scaled, keys_scaled, precision=highest)
    count = acceptance_entries.shape[0]
    row_index = lax.broadcasted_iota(jnp.int32, (count, count), 0)
    col_index = lax.broadcasted_iota(jnp.int32, (count, count), 1)
    scores = jnp.where((row_index > col_index)[None], scores, 0.0)
    diagonal_contribution = jnp.sum(
        acceptance_entries * diagonal_reward[None] * lookup_entries, axis=-1, keepdims=True
    )
    answer_lines = (
        jnp.einsum("hij,jhd->ihd", scores, payload_entries, precision=highest)
        + diagonal_contribution * payload_entries
    )
    answer_lines = answer_lines + jnp.einsum(
        "ihc,hcd->ihd", recept_scaled, evolving_memory, precision=highest
    )
    total = inclusive[-1]
    carried = lookup_entries * jnp.exp(total[None] - inclusive)
    new_state = jnp.exp(total)[:, :, None] * evolving_memory + jnp.einsum(
        "jhc,jhd->hcd", carried, payload_entries, precision=highest
    )
    return (new_state, answer_lines)


def continued_recurrence(
    acceptance_entries, lookup_entries, payload_entries, log_fading_amount, diagonal_reward
):
    length, per_group_view, embedding_dimension = acceptance_entries.shape
    blocks = length // BLK

    def step(evolving_memory, entry_lines):
        return block_sweep(
            evolving_memory,
            entry_lines[0],
            entry_lines[1],
            entry_lines[2],
            entry_lines[3],
            diagonal_reward,
        )

    shaped = tuple(
        (
            a.reshape(blocks, BLK, per_group_view, embedding_dimension)
            for a in (acceptance_entries, lookup_entries, payload_entries, log_fading_amount)
        )
    )
    evolving_memory, results = lax.scan(
        step,
        jnp.zeros((per_group_view, embedding_dimension, embedding_dimension), jnp.float32),
        shaped,
    )
    return (evolving_memory, results.reshape(length, per_group_view, embedding_dimension))


def combine(earlier, later):
    return (earlier[0] + later[0], jnp.exp(later[0])[:, :, None] * earlier[1] + later[1])


def shifted_rows(current, edge_row, long_rows, requests, slot_rows):
    feature_part = current.shape[1]
    long_prev = jnp.concatenate([edge_row, current[: long_rows - 1]], axis=0)
    short_view = current[long_rows:].reshape(requests, slot_rows, feature_part)
    short_prev = jnp.concatenate(
        [jnp.zeros((requests, 1, feature_part), current.dtype), short_view[:, :-1]], axis=1
    )
    short_prev = short_prev.reshape(requests * slot_rows, feature_part)
    return jnp.concatenate([long_prev, short_prev], axis=0)


def on_device(
    continued_prompt_entries,
    padded_prompt_entries,
    prompt_live_extents,
    preceding_entry_line,
    carried_memory,
    token_mixing_ratios,
    acceptance_transform,
    lookup_transform,
    payload_transform,
    gating_transform,
    fading_baseline,
    fading_left_factor,
    fading_right_factor,
    present_reward,
    group_layer_scaling,
    group_layer_shift_term,
    final_transform,
):
    long_rows = continued_prompt_entries.shape[0]
    requests = prompt_live_extents.shape[0]
    slot_rows = padded_prompt_entries.shape[0] // requests
    per_group_view, embedding_dimension = present_reward.shape
    arrived = passed_along(continued_prompt_entries[-1:], "seq", 1)
    first = lax.axis_index("seq") == 0
    edge_row = jnp.where(first, preceding_entry_line[None, :], arrived)
    current = jnp.concatenate([continued_prompt_entries, padded_prompt_entries], axis=0)
    current, edge_full = (
        lax.all_gather(current, "mp", axis=1, tiled=True),
        lax.all_gather(edge_row, "mp", axis=1, tiled=True),
    )
    previous = shifted_rows(current, edge_full, long_rows, requests, slot_rows)
    mixes = [mix_rows(current, previous, token_mixing_ratios[index]) for index in range(5)]
    total_rows = current.shape[0]
    columns = acceptance_transform.shape[1]
    pieces = (
        lax.all_gather(acceptance_transform, "seq", axis=0, tiled=True),
        lax.all_gather(lookup_transform, "seq", axis=0, tiled=True),
        lax.all_gather(payload_transform, "seq", axis=0, tiled=True),
        lax.all_gather(gating_transform, "seq", axis=0, tiled=True),
    )
    acceptance_entries, lookup_entries, payload_entries, gate = tuple(
        (
            jnp.dot(source, piece, preferred_element_type=jnp.float32)
            for source, piece in zip(mixes[:4], pieces)
        )
    )
    squeezed = jnp.tanh(
        jnp.dot(mixes[4], fading_left_factor, preferred_element_type=jnp.float32)
    ).astype(jnp.bfloat16)
    log_fading_amount = -jnp.exp(
        fading_baseline[None, :]
        + jnp.dot(squeezed, fading_right_factor, preferred_element_type=jnp.float32)
    )
    recept3, keys3, values3, decay3 = [
        a.reshape(total_rows, per_group_view, embedding_dimension)
        for a in (acceptance_entries, lookup_entries, payload_entries, log_fading_amount)
    ]
    local_state, long_out = continued_recurrence(
        recept3[:long_rows],
        keys3[:long_rows],
        values3[:long_rows],
        decay3[:long_rows],
        present_reward,
    )
    long_decay = decay3[:long_rows]
    group_total = jnp.sum(long_decay, axis=0)
    blank = (
        jnp.zeros((per_group_view, embedding_dimension), jnp.float32),
        jnp.zeros((per_group_view, embedding_dimension, embedding_dimension), jnp.float32),
    )
    prefix_total, prefix_state = entering((group_total, local_state), "seq", combine, blank)
    incoming = jnp.exp(prefix_total)[:, :, None] * carried_memory + prefix_state
    before_row = jnp.cumsum(long_decay, axis=0) - long_decay
    long_out = long_out + jnp.einsum(
        "ihc,hcd->ihd", recept3[:long_rows] * jnp.exp(before_row), incoming, precision=highest
    )
    span_end = jnp.exp(group_total)[:, :, None] * incoming + local_state
    live_rows = (
        lax.broadcasted_iota(jnp.int32, (requests, slot_rows), 1) < prompt_live_extents[:, None]
    )
    live_flat = live_rows.reshape(requests * slot_rows).astype(jnp.float32)[:, None, None]
    short_shape = (requests, slot_rows, per_group_view, embedding_dimension)
    short_recept = recept3[long_rows:].reshape(short_shape)
    short_keys = (keys3[long_rows:] * live_flat).reshape(short_shape)
    short_values = values3[long_rows:].reshape(short_shape)
    short_decay = (decay3[long_rows:] * live_flat).reshape(short_shape)
    zeroed_memory = jnp.zeros(
        (per_group_view, embedding_dimension, embedding_dimension), jnp.float32
    )

    def request_pass(acceptance_lines, lookup_table, payload_table, fading_table):
        return block_sweep(
            zeroed_memory,
            acceptance_lines,
            lookup_table,
            payload_table,
            fading_table,
            present_reward,
        )

    request_states, short_out = jax.vmap(request_pass)(
        short_recept, short_keys, short_values, short_decay
    )
    wkv = jnp.concatenate(
        [long_out, short_out.reshape(requests * slot_rows, per_group_view, embedding_dimension)],
        axis=0,
    )
    mean = jnp.mean(wkv, axis=-1, keepdims=True)
    centred = wkv - mean
    variance = jnp.mean(centred * centred, axis=-1, keepdims=True)
    normed = (centred * lax.rsqrt(variance + norm_eps)).reshape(
        total_rows, columns
    ) * group_layer_scaling[None, :] + group_layer_shift_term[None, :]
    row_live = jnp.concatenate(
        [jnp.ones((long_rows,), dtype=bool), live_rows.reshape(requests * slot_rows)], axis=0
    )
    hidden = jnp.where(row_live[:, None], normed * jax.nn.silu(gate), 0.0).astype(jnp.bfloat16)
    full_out = lax.all_gather(final_transform, "seq", axis=1, tiled=True)
    mixed_rows = lax.psum_scatter(
        jnp.dot(hidden, full_out, preferred_element_type=jnp.float32),
        "mp",
        scatter_dimension=0,
        tiled=True,
    )
    return (mixed_rows.astype(jnp.bfloat16)[None], span_end[None], request_states)


f32 = jnp.float32
bf16 = jnp.bfloat16
VMEM_LIMIT = 56 * 1024 * 1024
TILE = 256


def in_vmem():
    return pl.BlockSpec(memory_space=pltpu.VMEM)


def in_smem():
    return pl.BlockSpec(memory_space=pltpu.SMEM)


def takes(us):
    return pl.CostEstimate(
        flops=int(us * 1.15e9), bytes_accessed=int(us * 3.0e6), transcendentals=0
    )


def kernel_params():
    return pltpu.CompilerParams(vmem_limit_bytes=VMEM_LIMIT)


EXTRA = 16


def here_and_step(x_ref, is_long, period, tile):
    rows = x_ref.shape[1] - EXTRA
    here = x_ref[tile, 0:rows, :].astype(f32)
    above = x_ref[jnp.maximum(tile - 1, 0), rows - 16 : rows, :].astype(f32)[15:16]
    first = jnp.where(is_long == 1, x_ref[0, rows : rows + 16, :].astype(f32)[0:1], 0.0)
    row = lax.broadcasted_iota(jnp.int32, here.shape, 0)
    before = jnp.where(row == 0, above, pltpu.roll(here, 1, 0))
    start = ((row + tile * rows) & (period - 1)) == 0
    before = jnp.where(start, first, before)
    return here, before - here


def given_kernel(kind, extents, long_ref, short_ref, out_ref):
    rows = long_ref.shape[0]
    is_long = kind[0] == 1
    out_ref[0:rows, :] = jnp.where(is_long, short_ref[...], long_ref[...])
    lane = lax.broadcasted_iota(jnp.int32, (EXTRA, out_ref.shape[1]), 1)
    line = jnp.zeros(lane.shape, f32)
    for n in range(extents.shape[0]):
        line = jnp.where(lane == n, extents[n].astype(f32), line)
    out_ref[rows : rows + EXTRA, :] = line.astype(bf16)


def given_to_other_core(kind, extents, long_rows, short_rows):
    rows, columns = long_rows.shape
    return pl.pallas_call(
        given_kernel,
        out_shape=jax.ShapeDtypeStruct((rows + EXTRA, columns), bf16),
        in_specs=[in_smem()] * 2 + [in_vmem()] * 2,
        out_specs=in_vmem(),
        compiler_params=kernel_params(),
        cost_estimate=takes(1.5),
    )(kind, extents, long_rows, short_rows)


def block_kernel(kind, extents, long_ref, short_ref, taken, edge, out_ref):
    rows = long_ref.shape[0]
    depth = out_ref.shape[2]
    is_long = kind[0] == 1
    count = extents.shape[0]
    row = lax.broadcasted_iota(jnp.int32, (EXTRA, depth), 0)
    lane = lax.broadcasted_iota(jnp.int32, (EXTRA, depth), 1)
    other = taken[rows : rows + EXTRA, 0:depth].astype(f32)
    line = jnp.where(is_long, pltpu.roll(other, count, 1), other)
    own_at = jnp.where(is_long, 0, count)
    for n in range(count):
        line = jnp.where(lane == own_at + n, extents[n].astype(f32), line)
    for half in range(2):
        start = jnp.where(is_long, half, 1 - half) * depth
        at = pl.ds(pl.multiple_of(start, depth), depth)
        got = taken[0:rows, at]
        out_ref[half, 0:rows, :] = jnp.where(is_long, long_ref[:, at], got)
        out_ref[half, rows : 2 * rows, :] = jnp.where(is_long, got, short_ref[:, at])
        first = edge[:, at].astype(f32)
        out_ref[half, 2 * rows :, :] = jnp.where(row == 0, first, line).astype(bf16)


def block_of_chip(kind, extents, long_rows, short_rows, taken, edge):
    rows, columns = long_rows.shape
    return pl.pallas_call(
        block_kernel,
        out_shape=jax.ShapeDtypeStruct((2, 2 * rows + EXTRA, columns // 2), bf16),
        in_specs=[in_smem()] * 2 + [in_vmem()] * 4,
        out_specs=in_vmem(),
        compiler_params=kernel_params(),
        cost_estimate=takes(1.5),
    )(kind, extents, long_rows, short_rows, taken, edge)


def half_block(shape):
    return pl.BlockSpec((1,) + shape[1:], lambda i: (i,) + (0,) * (len(shape) - 1))


def gather_blocks(kind, own, rest, held):
    held[kind[6]] = own[...]
    for k in range(3):
        held[kind[7 + k]] = rest[k]


def mix_kernel(kind, own, rest, ratios, left, kv_mix, r_mix, gate_mix, squeezed, held):
    gather_blocks(kind, own.at[0], rest.at[0], held)

    @pl.loop(0, held.shape[0], unroll=2)
    def _(tile):
        here, step = here_and_step(held, kind[0], kind[1], tile)
        at = pl.ds(pl.multiple_of(tile * TILE, TILE), TILE)

        def mix(which):
            return (here + ratios[0, which : which + 1, :] * step).astype(bf16)

        r_mix[0, at, :] = mix(0)
        kv_mix[0, 0, at, :] = mix(1)
        kv_mix[0, 1, at, :] = mix(2)
        gate_mix[0, at, :] = mix(3)
        squeezed[0, at, :] = jnp.dot(mix(4), left[0], preferred_element_type=f32)


def mixes_of(kind, own, rest, ratios, left):
    rows, depth = own.shape[1] - EXTRA, own.shape[2]
    lines = rest.shape[1] + 1
    whole = lines * rows
    outs = [
        jax.ShapeDtypeStruct((2, 2, whole, depth), bf16),
        jax.ShapeDtypeStruct((2, whole, depth), bf16),
        jax.ShapeDtypeStruct((2, whole, depth), bf16),
        jax.ShapeDtypeStruct((2, whole, left.shape[2]), f32),
    ]
    return pl.pallas_call(
        mix_kernel,
        grid=(2,),
        out_shape=outs,
        in_specs=[in_smem()] + [half_block(a.shape) for a in (own, rest, ratios, left)],
        out_specs=[half_block(out.shape) for out in outs],
        scratch_shapes=[pltpu.VMEM((lines, rows + EXTRA, depth), bf16)],
        compiler_params=kernel_params(),
        cost_estimate=takes(7),
    )(kind, own, rest, ratios, left)


def project_kernel(
    kind,
    mix0,
    mix1,
    mix2,
    low0,
    low1,
    low2,
    own0,
    own1,
    rest0,
    rest1,
    ratios,
    left,
    own_weight,
    sibling_weight,
    right,
    base,
    keys_ref,
    values_ref,
    decay_ref,
    r_mix,
    gate_mix,
    held,
):
    tile = pl.program_id(0)

    @pl.when(tile == 0)
    def _():
        for half, (own, rest) in enumerate(((own0, rest0), (own1, rest1))):
            gather_blocks(kind, own, rest, held.at[half])

    totals = [None] * 2

    def add(which, rel, half, mixed):
        weight = (own_weight, sibling_weight)[half][kind[10 + rel], which]
        part = jnp.dot(mixed, weight, preferred_element_type=f32)
        totals[which] = part if totals[which] is None else totals[which] + part

    squeezed = low0[0] + low0[1] + low1[0] + low1[1] + low2[0] + low2[1]
    for half in range(2):
        here, step = here_and_step(held.at[half], kind[0], kind[1], tile)

        def mix(which):
            return (here + ratios[half, which : which + 1, :] * step).astype(bf16)

        r_mix[half] = mix(0)
        add(0, 3, half, mix(1))
        add(1, 3, half, mix(2))
        gate_mix[half] = mix(3)
        squeezed = squeezed + jnp.dot(mix(4), left[half], preferred_element_type=f32)
    for rel, mixes in enumerate((mix0, mix1, mix2)):
        for half in range(2):
            for which in range(2):
                add(which, rel, half, mixes[half, which])
    keys_ref[...] = totals[0]
    values_ref[...] = totals[1]
    squeezed = jnp.tanh(squeezed).astype(bf16)
    grown = jnp.dot(squeezed, right[...], preferred_element_type=f32)
    decay_ref[...] = -jnp.exp(base[...] + grown)


def projected(kind, mixes, lows, owns, rests, *rest):
    rows, depth = mixes[0].shape[2:]
    own_weight = rest[2]
    width, rank = own_weight.shape[3], lows[0].shape[2]
    flat = jax.ShapeDtypeStruct((rows, width), f32)
    wide = jax.ShapeDtypeStruct((2, rows, depth), bf16)
    tile_of = pl.BlockSpec((TILE, width), lambda i: (i, 0))
    wide_of = pl.BlockSpec((2, TILE, depth), lambda i: (0, i, 0))
    return pl.pallas_call(
        project_kernel,
        grid=(rows // TILE,),
        out_shape=[flat] * 3 + [wide] * 2,
        in_specs=[in_smem()]
        + [pl.BlockSpec((2, 2, TILE, depth), lambda i: (0, 0, i, 0))] * 3
        + [pl.BlockSpec((2, TILE, rank), lambda i: (0, i, 0))] * 3
        + [in_vmem()] * (4 + len(rest)),
        out_specs=[tile_of] * 3 + [wide_of] * 2,
        scratch_shapes=[pltpu.VMEM((2, rests[0].shape[0] + 1) + owns[0].shape, bf16)],
        compiler_params=kernel_params(),
        cost_estimate=takes(12),
    )(kind, *mixes, *lows, *owns, *rests, *rest)


def plain_kernel(kind, mix0, mix1, mix2, mix3, own, sibling, out_ref):
    half = pl.program_id(0)
    part = None
    for rel, mixes in enumerate((mix0, mix1, mix2, mix3)):
        weight = jnp.where(half == 0, own[kind[10 + rel], 0], sibling[kind[10 + rel], 0])
        new = jnp.dot(mixes[0], weight, preferred_element_type=f32)
        part = new if part is None else part + new

    @pl.when(half == 0)
    def _():
        out_ref[...] = part

    @pl.when(half == 1)
    def _():
        out_ref[...] += part


def plain_product(kind, mixes, own, sibling):
    rows, width = mixes[0].shape[1], own.shape[3]
    return pl.pallas_call(
        plain_kernel,
        grid=(2,),
        out_shape=jax.ShapeDtypeStruct((rows, width), f32),
        in_specs=[in_smem()] + [half_block(mix.shape) for mix in mixes] + [in_vmem()] * 2,
        out_specs=pl.BlockSpec((rows, width), lambda i: (0, 0)),
        compiler_params=kernel_params(),
        cost_estimate=takes(6),
    )(kind, *mixes, own, sibling)


def gate_kernel(
    kind,
    lengths,
    mix0,
    mix1,
    mix2,
    mix3,
    own,
    sibling,
    normed,
    kept0,
    sent0,
    kept1,
    sent1,
    total,
):
    half = pl.program_id(0)
    part = None
    for rel, mixes in enumerate((mix0, mix1, mix2, mix3)):
        weight = jnp.where(half == 0, own[kind[10 + rel], 0], sibling[kind[10 + rel], 0])
        new = jnp.dot(mixes[0], weight, preferred_element_type=f32)
        part = new if part is None else part + new

    @pl.when(half == 0)
    def _():
        total[...] = part

    @pl.when(half == 1)
    def _():
        gate = total[...] + part
        value = normed[...] * (gate * jax.nn.sigmoid(gate))
        row = lax.broadcasted_iota(jnp.int32, (BLK, value.shape[1]), 0)
        is_long = kind[0] == 1
        half_rows = BLK // 2

        def lived(n):
            block = value[n * BLK : (n + 1) * BLK]
            return jnp.where(row < lengths[n], block, 0.0).astype(bf16)

        for line in range(kept0.shape[1]):
            for block in range(2):
                even, odd = lived(4 * line + block), lived(4 * line + 2 + block)
                kept = jnp.where(is_long, even, odd)
                sent = jnp.where(is_long, odd, even)
                kept0[block, line] = kept[:half_rows]
                kept1[block, line] = kept[half_rows:]
                sent0[block, line] = sent[:half_rows]
                sent1[block, line] = sent[half_rows:]


def gated(kind, lengths, mixes, own, sibling, normed):
    rows, width = normed.shape
    quarter = jax.ShapeDtypeStruct((2, rows // TILE, BLK // 2, width), bf16)
    return pl.pallas_call(
        gate_kernel,
        grid=(2,),
        out_shape=[quarter] * 4,
        in_specs=[in_smem()] * 2 + [half_block(mix.shape) for mix in mixes] + [in_vmem()] * 3,
        out_specs=[pl.BlockSpec(quarter.shape, lambda i: (0, 0, 0, 0))] * 4,
        scratch_shapes=[pltpu.VMEM((rows, width), f32)],
        compiler_params=kernel_params(),
        cost_estimate=takes(7),
    )(kind, lengths, *mixes, own, sibling, normed)


def head_blocks(heads):
    width = heads * BLK
    tall = lax.broadcasted_iota(jnp.int32, (width, width), 0) // BLK
    wide = lax.broadcasted_iota(jnp.int32, (width, width), 1) // BLK
    return tall == wide


def state_kernel(lengths, carry, k_ref, v_ref, w_ref, s_ref, state_ref, entered_ref, hold):
    span, width = BLK, k_ref.shape[1]
    heads = width // span
    row = lax.broadcasted_iota(jnp.int32, (span, width), 0)
    lane = lax.broadcasted_iota(jnp.int32, (span, width), 1)
    for h in range(heads):
        hold[:, h * span : (h + 1) * span] = s_ref[h]

    @pl.loop(0, k_ref.shape[0] // span, unroll=8)
    def _(n):
        at = pl.ds(pl.multiple_of(n * span, span), span)
        live = row < lengths[n]
        k = jnp.where(live, k_ref[at, :], 0.0)
        total = jnp.where(live, w_ref[at, :], 0.0)
        after_row = jnp.zeros_like(total)
        half = 1
        while half < span:
            upper = (row & half) != 0
            across = jnp.where(
                upper, pltpu.roll(total, half, 0), pltpu.roll(total, span - half, 0)
            )
            after_row = after_row + jnp.where(upper, 0.0, across)
            total = total + across
            half *= 2
        added = lax.dot_general(
            (k * jnp.exp(after_row)).astype(bf16),
            v_ref[at, :].astype(bf16),
            (((0,), (0,)), ((), ())),
            preferred_element_type=f32,
        )
        fresh = jnp.zeros((span, width), f32)
        for h in range(heads):
            fresh = jnp.where(lane // span == h, added[h * span : (h + 1) * span], fresh)
        twice = jnp.concatenate([total] * 2, axis=0)
        turned_parts = []
        for p in range(width // (2 * span)):
            flipped = jnp.transpose(twice[:, p * 2 * span : (p + 1) * 2 * span])
            turned_parts.append(
                jnp.where(lane[:, : 2 * span] < span, flipped[:span], flipped[span:])
            )
        fade = jnp.exp(jnp.concatenate(turned_parts, axis=1))
        entered = hold[...] * carry[0]
        entered_ref[n] = entered.astype(bf16)
        state = fade * entered + fresh
        hold[...] = state
        for h in range(heads):
            state_ref[n, h] = state[:, h * span : (h + 1) * span]


def states_of(lengths, carry, k, v, w, state):
    rows, width = k.shape
    heads = width // BLK
    return pl.pallas_call(
        state_kernel,
        out_shape=[
            jax.ShapeDtypeStruct((rows // BLK, heads, BLK, BLK), f32),
            jax.ShapeDtypeStruct((rows // BLK, BLK, width), bf16),
        ],
        in_specs=[in_smem()] * 2 + [in_vmem()] * 4,
        out_specs=[in_vmem()] * 2,
        scratch_shapes=[pltpu.VMEM((BLK, width), f32)],
        compiler_params=kernel_params(),
        cost_estimate=takes(7),
    )(lengths, carry, k, v, w, state)


def sweep_kernel(lengths, r_ref, k_ref, v_ref, w_ref, entered_ref, u_ref, gain, bias, out_ref):
    span, width = BLK, r_ref.shape[1]
    heads = width // span
    row = lax.broadcasted_iota(jnp.int32, (span, width), 0)
    lane = lax.broadcasted_iota(jnp.int32, (span, width), 1)
    col = lane % span
    same_head = head_blocks(heads)

    def spread(value):
        stacked = jnp.concatenate([value.astype(bf16)] * heads, axis=0)
        return jnp.where(same_head, stacked, jnp.zeros_like(stacked))

    def against(a, b):
        return lax.dot_general(a, b, (((1,), (1,)), ((), ())), preferred_element_type=f32)

    @pl.loop(0, r_ref.shape[0] // span, unroll=4)
    def _(n):
        at = pl.ds(pl.multiple_of(n * span, span), span)
        live = row < lengths[n]
        r, v = r_ref[at, :], v_ref[at, :]
        k = jnp.where(live, k_ref[at, :], 0.0)
        total = jnp.where(live, w_ref[at, :], 0.0)
        before = jnp.zeros_like(total)
        after_row = jnp.zeros_like(total)
        scores = against((r * u_ref[...]).astype(bf16), spread(k))
        scores = jnp.where(row == col, scores, 0.0)
        level = 0
        while (1 << level) < span:
            half = 1 << level
            upper = (row & half) != 0
            if level:
                scale = jnp.exp(jnp.where(upper, before, after_row))
                part = against((r * scale).astype(bf16), spread(k * scale))
            else:
                part = against(r.astype(bf16), spread(k))
            pair = upper & (((row >> level) ^ (col >> level)) == 1)
            scores = jnp.where(pair, part, scores)
            across = jnp.where(
                upper, pltpu.roll(total, half, 0), pltpu.roll(total, span - half, 0)
            )
            before = before + jnp.where(upper, across, 0.0)
            after_row = after_row + jnp.where(upper, 0.0, across)
            total = total + across
            level += 1
        out = jnp.dot(scores.astype(bf16), spread(v), preferred_element_type=f32)
        out = out + jnp.dot(
            (r * jnp.exp(before)).astype(bf16),
            spread(entered_ref[n]),
            preferred_element_type=f32,
        )
        out_ref[at, :] = out

    ones = jnp.where(same_head, 1.0, 0.0).astype(bf16)

    def head_mean(value):
        high = value.astype(bf16)
        low = (value - high.astype(f32)).astype(bf16)
        both = jnp.dot(high, ones, preferred_element_type=f32) + jnp.dot(
            low, ones, preferred_element_type=f32
        )
        return both * (1.0 / span)

    @pl.loop(0, r_ref.shape[0] // TILE, unroll=2)
    def _(tile):
        at = pl.ds(pl.multiple_of(tile * TILE, TILE), TILE)
        value = out_ref[at, :]
        centred = value - head_mean(value)
        spread_of = head_mean(centred * centred)
        out_ref[at, :] = centred * lax.rsqrt(spread_of + norm_eps) * gain[...] + bias[...]


def sweep(lengths, r, k, v, w, entered, bonus, gain, bias):
    return pl.pallas_call(
        sweep_kernel,
        out_shape=jax.ShapeDtypeStruct(r.shape, f32),
        in_specs=[in_smem()] + [in_vmem()] * 8,
        out_specs=in_vmem(),
        compiler_params=kernel_params(),
        cost_estimate=takes(12),
    )(lengths, r, k, v, w, entered, bonus, gain, bias)


def final_kernel(block_of, h0, h1, h2, h3, weight, o0, o1, o2, o3, hold):
    @pl.loop(0, hold.shape[1] // TILE, unroll=2)
    def _(tile):
        at = pl.ds(pl.multiple_of(tile * TILE, TILE), TILE)
        total = None
        for k, piece in enumerate((h0, h1, h2, h3)):
            part = jnp.dot(piece[...], weight[k, :, at], preferred_element_type=f32)
            total = part if total is None else total + part
        hold[:, at] = total.astype(bf16)

    block = hold.shape[0] // 4
    for rel, out in enumerate((o0, o1, o2, o3)):
        at = pl.ds(pl.multiple_of(block_of[rel] * block, block), block)
        out[...] = hold[at, :].reshape(out.shape)


def final_product(block_of, pieces, weight, lines):
    rows, width = pieces[0].shape[0], weight.shape[2]
    out = jax.ShapeDtypeStruct((lines, rows // 4 // lines, width), bf16)
    return pl.pallas_call(
        final_kernel,
        out_shape=[out] * 4,
        in_specs=[in_smem()] + [in_vmem()] * 5,
        out_specs=[in_vmem()] * 4,
        scratch_shapes=[pltpu.VMEM((rows, width), bf16)],
        compiler_params=kernel_params(),
        cost_estimate=takes(4.5),
    )(block_of, *pieces, weight)


def lay_kernel(at, *refs):
    pieces, out_ref = refs[:-1], refs[-1]
    rows, width = pieces[0].shape
    lines = out_ref.shape[1] // width
    for n, piece in enumerate(pieces):
        column = pl.multiple_of(at[n % lines] * width, width)
        out_ref[n // lines * rows : (n // lines + 1) * rows, pl.ds(column, width)] = piece[...]


def laid(at, pieces, lines):
    rows, width = pieces[0].shape
    return pl.pallas_call(
        lay_kernel,
        out_shape=jax.ShapeDtypeStruct((len(pieces) // lines * rows, lines * width), bf16),
        in_specs=[in_smem()] + [in_vmem()] * len(pieces),
        out_specs=in_vmem(),
        compiler_params=kernel_params(),
        cost_estimate=takes(2),
    )(at, *pieces)


def after(value, *others):
    return lax.optimization_barrier((value,) + others)[0]


def turned(x, axis, by):
    length = lax.axis_size(axis)
    return lax.ppermute(x, axis, [(i, (i + by) % length) for i in range(length)])


def flipped_core(x):
    return lax.ppermute(x, "core", [(0, 1), (1, 0)])


def over_x(x):
    return lax.ppermute(x, "x", [(0, 1), (1, 0)])


def over_y(x):
    return lax.ppermute(x, "y", [(0, 1), (1, 0)])


def dealt(blocks, z):
    length = lax.axis_size("z")
    return [blocks(z)] + [turned(blocks((z + k) % length), "z", k) for k in range(1, length)]


def near_along(piece):
    two = turned(piece, "z", 2)
    one = lax.ppermute(piece, "z", [(0, 1), (1, 2), (2, 3)])
    three = lax.ppermute(piece, "z", [(1, 0), (2, 1), (3, 2)])
    return one, two, three


def far_along(two):
    return lax.ppermute(two, "z", [(1, 0), (2, 3)])


def spread_along(piece, z):
    one, two, three = near_along(piece)
    return piece, one, two, three, far_along(two)


def in_place(spread, z, at=0):
    piece, one, two, three, far = spread
    whole = jnp.zeros((4,) + piece.shape, piece.dtype)
    for k, part in ((1, one), (2, two), (3, three)):
        whole = lax.dynamic_update_index_in_dim(whole, part, (z - k) % 4, 0)
    far_at = jnp.where(z == 0, 3, jnp.where(z == 3, 0, z))
    whole = lax.dynamic_update_index_in_dim(whole, far, far_at, 0)
    return lax.dynamic_update_index_in_dim(whole, piece, z, 0)


def in_order(pieces, z):
    length = len(pieces)
    whole = jnp.zeros((length,) + pieces[0].shape, pieces[0].dtype)
    for k, piece in enumerate(pieces):
        whole = lax.dynamic_update_index_in_dim(whole, piece, (z - k) % length, 0)
    return whole


def on_core(
    continued_prompt_entries,
    padded_prompt_entries,
    prompt_live_extents,
    preceding_entry_line,
    carried_memory,
    token_mixing_ratios,
    acceptance_transform,
    lookup_transform,
    payload_transform,
    gating_transform,
    fading_baseline,
    fading_left_factor,
    fading_right_factor,
    present_reward,
    group_layer_scaling,
    group_layer_shift_term,
    final_transform,
):
    z, core = lax.axis_index("z"), lax.axis_index("core")
    y, x = lax.axis_index("y"), lax.axis_index("x")
    mp = 2 * y + x
    is_long = core == 0
    lines = lax.axis_size("z")
    group_rows, columns = continued_prompt_entries.shape
    requests = prompt_live_extents.shape[0]
    slot_rows = group_rows // requests
    heads, span = present_reward.shape
    heads = heads // lines
    width = heads * span
    depth = acceptance_transform.shape[0]
    rows = 2 * lines * group_rows

    kind = jnp.stack(
        [is_long.astype(jnp.int32), jnp.where(is_long, rows, slot_rows).astype(jnp.int32)]
        + [(mp ^ rel).astype(jnp.int32) for rel in range(4)]
        + [((z - k) % lines).astype(jnp.int32) for k in range(4)]
        + [((z - (mp ^ rel)) % lines).astype(jnp.int32) for rel in range(4)]
    )
    given = given_to_other_core(
        kind, prompt_live_extents, continued_prompt_entries, padded_prompt_entries
    )
    taken = flipped_core(given)
    block = block_of_chip(
        kind,
        prompt_live_extents,
        continued_prompt_entries,
        padded_prompt_entries,
        taken,
        preceding_entry_line[None],
    )
    (
        block,
        acceptance_transform,
        lookup_transform,
        payload_transform,
        gating_transform,
        final_transform,
        token_mixing_ratios,
        fading_left_factor,
        fading_right_factor,
        fading_baseline,
        present_reward,
        group_layer_scaling,
        group_layer_shift_term,
        carried_memory,
    ) = lax.optimization_barrier(
        (
            block,
            acceptance_transform,
            lookup_transform,
            payload_transform,
            gating_transform,
            final_transform,
            token_mixing_ratios,
            fading_left_factor,
            fading_right_factor,
            fading_baseline,
            present_reward,
            group_layer_scaling,
            group_layer_shift_term,
            carried_memory,
        )
    )
    one, two, three = near_along(block)
    own_x, own_y = over_x(block), over_y(block)
    one, two, three, own_x, own_y = lax.optimization_barrier((one, two, three, own_x, own_y))
    far = far_along(two)
    own_xy = (over_y(own_x[0]), over_x(own_y[1]))
    far, own_xy = lax.optimization_barrier((far, own_xy))
    rest = jnp.stack([jnp.where(z == 0, far, one), two, jnp.where(z == 3, far, three)], axis=1)
    rest_x, rest_y = over_x(rest), over_y(rest)
    extents = in_order(
        [part[2 * group_rows + 1, : 2 * requests] for part in (block[0],) + tuple(rest[0])], z
    ).reshape(2 * lines * requests)
    extents = jnp.where(is_long, slot_rows, extents.astype(jnp.int32)).astype(jnp.int32)

    def chunk_order(whole):
        split = whole.reshape((4, 2, depth) + whole.shape[1:])
        parts = []
        for rel in range(4):
            both = split[mp ^ rel]
            parts.append(jnp.where(is_long, both, both[::-1]))
        return parts

    ratios = [part.transpose(0, 2, 1) for part in chunk_order(token_mixing_ratios.T)]
    left = chunk_order(fading_left_factor)

    def columns_of(weights, *ready):
        stacked = jnp.stack(weights)
        blocks = [
            lax.dynamic_slice_in_dim(stacked, (z + k) % lines * width, width, 2)
            for k in range(lines)
        ]
        blocks = lax.optimization_barrier((tuple(blocks),) + ready)[0]
        return (blocks[0],) + tuple(turned(blocks[k], "z", k) for k in range(1, lines))

    def both_cores(pieces):
        own = jnp.stack(pieces)
        return own, flipped_core(own)

    kv_pieces = columns_of([lookup_transform, payload_transform], rest, own_xy)
    kv_pieces, rest_x, rest_y = lax.optimization_barrier((kv_pieces, rest_x, rest_y))
    rest_xy = (over_y(rest_x[0]), over_x(rest_y[1]))
    r_pieces = columns_of([acceptance_transform], rest_x, rest_y, kv_pieces)
    own_kv, sibling_kv = both_cores(kv_pieces)
    rest_xy, r_pieces = lax.optimization_barrier((rest_xy, r_pieces))
    gate_pieces = columns_of([gating_transform], r_pieces, rest_xy)
    own_r, sibling_r = both_cores(r_pieces)

    def mine_of(vector):
        return lax.dynamic_slice_in_dim(vector, z * width, width, 0)[None]

    kv0, r0, gate0, low0 = mixes_of(kind, block, rest, ratios[0], left[0])
    kv1, r1, gate1, low1 = mixes_of(kind, own_x, rest_x, ratios[1], left[1])
    kv2, r2, gate2, low2 = mixes_of(kind, own_y, rest_y, ratios[2], left[2])
    keys, values, decay, r3, gate3 = projected(
        kind,
        (kv0, kv1, kv2),
        (low0, low1, low2),
        own_xy,
        rest_xy,
        ratios[3],
        left[3],
        own_kv,
        sibling_kv,
        lax.dynamic_slice_in_dim(fading_right_factor, z * width, width, 1),
        mine_of(fading_baseline),
    )
    recept = plain_product(kind, (r0, r1, r2, r3), own_r, sibling_r)
    entered = lax.dynamic_slice_in_dim(carried_memory, z * heads, heads, 0)
    bonus = lax.dynamic_slice_in_dim(present_reward, z * heads, heads, 0).reshape(1, width)
    states, states_in = states_of(
        extents,
        is_long.astype(f32)[None],
        keys,
        values,
        decay,
        jnp.where(is_long, entered, 0.0),
    )
    normed = sweep(
        extents,
        recept,
        keys,
        values,
        decay,
        states_in,
        bonus,
        mine_of(group_layer_scaling),
        mine_of(group_layer_shift_term),
    )
    own_gate, sibling_gate = both_cores(after(gate_pieces, states))
    kept0, sent0, kept1, sent1 = gated(
        kind, extents, (gate0, gate1, gate2, gate3), own_gate, sibling_gate, normed
    )

    states = states.reshape(lines, 2, requests, heads, span, span)
    passed = flipped_core(lax.dynamic_index_in_dim(states, 1 - core, 1, keepdims=False))
    held = lax.dynamic_index_in_dim(states, core, 1, keepdims=False)
    bundle = jnp.concatenate(
        [jnp.where(is_long, held, passed)[:, -1:], jnp.where(is_long, passed, held)], axis=1
    ).astype(bf16)
    bundle = after(bundle, gate_pieces)
    arrived = in_order(
        dealt(lambda j: lax.dynamic_index_in_dim(bundle, j, 0, keepdims=False), z), z
    ).astype(f32)
    span_states = arrived[:, 0].reshape(1, lines * heads, span, span)
    request_states = jnp.swapaxes(arrived[:, 1:], 0, 1).reshape(
        requests, lines * heads, span, span
    )

    wide_out = 2 * final_transform.shape[1]
    beside = flipped_core(final_transform)
    out_weight = jnp.concatenate(
        [
            jnp.where(is_long, final_transform, beside),
            jnp.where(is_long, beside, final_transform),
        ],
        axis=1,
    ).reshape(lines, width, wide_out)
    out_weight = jnp.stack(
        [
            lax.dynamic_index_in_dim(out_weight, (z - k) % lines, 0, keepdims=False)
            for k in range(lines)
        ]
    )
    order = jnp.stack([(z - k) % lines for k in range(lines)]).astype(jnp.int32)
    block_of = jnp.stack(
        [(((y ^ (rel >> 1)) ^ core) * 2 + (x ^ (rel & 1))).astype(jnp.int32) for rel in range(4)]
    )
    spreads = []
    for kept, sent in ((kept0, sent0), (kept1, sent1)):
        part = jnp.concatenate([kept, flipped_core(sent)], axis=0)
        part = part.reshape(2 * rows // 4, width)
        if spreads:
            part = after(part, spreads[0][2])
        spreads.append(spread_along(part, z))
    out_pieces = []
    for piece, one, two, three, far in spreads:
        one = jnp.where(z == 0, far, one)
        three = jnp.where(z == 3, far, three)
        here, to_x, to_y, to_xy = final_product(
            block_of, (piece, one, two, three), out_weight, lines
        )
        across = lax.ppermute(to_xy, ("y", "x"), [(i, 3 - i) for i in range(4)])
        mixed_part = (
            here.astype(f32)
            + over_x(to_x).astype(f32)
            + over_y(to_y).astype(f32)
            + across.astype(f32)
        ).astype(bf16)
        out_pieces += dealt(
            lambda j: lax.dynamic_index_in_dim(mixed_part, j, 0, keepdims=False), z
        )
    mixed = laid(order, out_pieces, lines)[None]
    return mixed, span_states, request_states


def rows_kept_solution(mesh):
    placed = (
        P("seq", "mp"),
        P("seq", "mp"),
        P("seq"),
        P("mp"),
        P("mp", None, None),
        P(),
        P("seq", "mp"),
        P("seq", "mp"),
        P("seq", "mp"),
        P("seq", "mp"),
        P("mp"),
        P(),
        P(None, "mp"),
        P("mp", None),
        P("mp"),
        P("mp"),
        P("mp", "seq"),
    )
    return jax.shard_map(
        on_device,
        mesh=mesh,
        in_specs=placed,
        out_specs=(P("seq", "mp", None), P("seq", "mp", None, None), P("seq", "mp", None, None)),
        check_vma=False,
    )


def heads_kept_solution(mesh):
    seq, mp = mesh.shape["seq"], mesh.shape["mp"]
    split = Mesh(mesh.devices.reshape(seq // 2, 2, 2, mp // 2), ("z", "core", "y", "x"))
    s, m = ("z", "core"), ("y", "x")
    placed = (
        P(s, m),
        P(s, m),
        P(s),
        P(m),
        P(m, None, None),
        P(),
        P(s, m),
        P(s, m),
        P(s, m),
        P(s, m),
        P(m),
        P(),
        P(None, m),
        P(m, None),
        P(m),
        P(m),
        P(m, s),
    )
    return jax.shard_map(
        on_core,
        mesh=split,
        in_specs=placed,
        out_specs=(P(s, m, None), P(s, m, None, None), P(s, m, None, None)),
        check_vma=False,
    )


def solution(mesh):
    if mesh.shape["mp"] == 4 and mesh.shape["seq"] == 8:
        return heads_kept_solution(mesh)
    return rows_kept_solution(mesh)
```

```python
import jax
import jax.numpy as jnp
import numpy as np
from jax import lax
from jax.experimental import pallas as pl
from jax.experimental.pallas import tpu as pltpu
from jax.sharding import Mesh
from jax.sharding import PartitionSpec as P

BLK = 64


norm_eps = 0.00064
highest = lax.Precision.HIGHEST


def passed_along(x, axis, by):
    length = lax.axis_size(axis)
    pairs = [(i, i + by) for i in range(length) if 0 <= i + by < length]
    return lax.ppermute(x, axis, pairs)


def entering(value, axis, join, neutral):
    count, mine = (lax.axis_size(axis), lax.axis_index(axis))
    pieces = jax.tree.map(lambda part: lax.all_gather(part, axis), value)
    total = jax.tree.map(
        lambda part, zero: jnp.full_like(part, 0) + jnp.asarray(zero, part.dtype), value, neutral
    )

    def hop(position, total):
        longer = join(total, jax.tree.map(lambda part: part[position], pieces))
        return jax.tree.map(lambda new, old: jnp.where(position < mine, new, old), longer, total)

    return lax.fori_loop(0, count - 1, hop, total)


def mix_rows(current, previous, weight):
    here = current.astype(jnp.float32)
    return (here + weight[None, :] * (previous.astype(jnp.float32) - here)).astype(jnp.bfloat16)


def block_sweep(
    evolving_memory,
    acceptance_entries,
    lookup_entries,
    payload_entries,
    log_fading_amount,
    diagonal_reward,
):
    inclusive = jnp.cumsum(log_fading_amount, axis=0)
    exclusive = inclusive - log_fading_amount
    recept_scaled = acceptance_entries * jnp.exp(exclusive)
    keys_scaled = lookup_entries * jnp.exp(-inclusive)
    scores = jnp.einsum("ihc,jhc->hij", recept_scaled, keys_scaled, precision=highest)
    count = acceptance_entries.shape[0]
    row_index = lax.broadcasted_iota(jnp.int32, (count, count), 0)
    col_index = lax.broadcasted_iota(jnp.int32, (count, count), 1)
    scores = jnp.where((row_index > col_index)[None], scores, 0.0)
    diagonal_contribution = jnp.sum(
        acceptance_entries * diagonal_reward[None] * lookup_entries, axis=-1, keepdims=True
    )
    answer_lines = (
        jnp.einsum("hij,jhd->ihd", scores, payload_entries, precision=highest)
        + diagonal_contribution * payload_entries
    )
    answer_lines = answer_lines + jnp.einsum(
        "ihc,hcd->ihd", recept_scaled, evolving_memory, precision=highest
    )
    total = inclusive[-1]
    carried = lookup_entries * jnp.exp(total[None] - inclusive)
    new_state = jnp.exp(total)[:, :, None] * evolving_memory + jnp.einsum(
        "jhc,jhd->hcd", carried, payload_entries, precision=highest
    )
    return (new_state, answer_lines)


def continued_recurrence(
    acceptance_entries, lookup_entries, payload_entries, log_fading_amount, diagonal_reward
):
    length, per_group_view, embedding_dimension = acceptance_entries.shape
    blocks = length // BLK

    def step(evolving_memory, entry_lines):
        return block_sweep(
            evolving_memory,
            entry_lines[0],
            entry_lines[1],
            entry_lines[2],
            entry_lines[3],
            diagonal_reward,
        )

    shaped = tuple(
        (
            a.reshape(blocks, BLK, per_group_view, embedding_dimension)
            for a in (acceptance_entries, lookup_entries, payload_entries, log_fading_amount)
        )
    )
    evolving_memory, results = lax.scan(
        step,
        jnp.zeros((per_group_view, embedding_dimension, embedding_dimension), jnp.float32),
        shaped,
    )
    return (evolving_memory, results.reshape(length, per_group_view, embedding_dimension))


def combine(earlier, later):
    return (earlier[0] + later[0], jnp.exp(later[0])[:, :, None] * earlier[1] + later[1])


def shifted_rows(current, edge_row, long_rows, requests, slot_rows):
    feature_part = current.shape[1]
    long_prev = jnp.concatenate([edge_row, current[: long_rows - 1]], axis=0)
    short_view = current[long_rows:].reshape(requests, slot_rows, feature_part)
    short_prev = jnp.concatenate(
        [jnp.zeros((requests, 1, feature_part), current.dtype), short_view[:, :-1]], axis=1
    )
    short_prev = short_prev.reshape(requests * slot_rows, feature_part)
    return jnp.concatenate([long_prev, short_prev], axis=0)


def on_device(
    continued_prompt_entries,
    padded_prompt_entries,
    prompt_live_extents,
    preceding_entry_line,
    carried_memory,
    token_mixing_ratios,
    acceptance_transform,
    lookup_transform,
    payload_transform,
    gating_transform,
    fading_baseline,
    fading_left_factor,
    fading_right_factor,
    present_reward,
    group_layer_scaling,
    group_layer_shift_term,
    final_transform,
):
    long_rows = continued_prompt_entries.shape[0]
    requests = prompt_live_extents.shape[0]
    slot_rows = padded_prompt_entries.shape[0] // requests
    per_group_view, embedding_dimension = present_reward.shape
    arrived = passed_along(continued_prompt_entries[-1:], "seq", 1)
    first = lax.axis_index("seq") == 0
    edge_row = jnp.where(first, preceding_entry_line[None, :], arrived)
    current = jnp.concatenate([continued_prompt_entries, padded_prompt_entries], axis=0)
    current, edge_full = (
        lax.all_gather(current, "mp", axis=1, tiled=True),
        lax.all_gather(edge_row, "mp", axis=1, tiled=True),
    )
    previous = shifted_rows(current, edge_full, long_rows, requests, slot_rows)
    mixes = [mix_rows(current, previous, token_mixing_ratios[index]) for index in range(5)]
    total_rows = current.shape[0]
    columns = acceptance_transform.shape[1]
    pieces = (
        lax.all_gather(acceptance_transform, "seq", axis=0, tiled=True),
        lax.all_gather(lookup_transform, "seq", axis=0, tiled=True),
        lax.all_gather(payload_transform, "seq", axis=0, tiled=True),
        lax.all_gather(gating_transform, "seq", axis=0, tiled=True),
    )
    acceptance_entries, lookup_entries, payload_entries, gate = tuple(
        (
            jnp.dot(source, piece, preferred_element_type=jnp.float32)
            for source, piece in zip(mixes[:4], pieces)
        )
    )
    squeezed = jnp.tanh(
        jnp.dot(mixes[4], fading_left_factor, preferred_element_type=jnp.float32)
    ).astype(jnp.bfloat16)
    log_fading_amount = -jnp.exp(
        fading_baseline[None, :]
        + jnp.dot(squeezed, fading_right_factor, preferred_element_type=jnp.float32)
    )
    recept3, keys3, values3, decay3 = [
        a.reshape(total_rows, per_group_view, embedding_dimension)
        for a in (acceptance_entries, lookup_entries, payload_entries, log_fading_amount)
    ]
    local_state, long_out = continued_recurrence(
        recept3[:long_rows],
        keys3[:long_rows],
        values3[:long_rows],
        decay3[:long_rows],
        present_reward,
    )
    long_decay = decay3[:long_rows]
    group_total = jnp.sum(long_decay, axis=0)
    blank = (
        jnp.zeros((per_group_view, embedding_dimension), jnp.float32),
        jnp.zeros((per_group_view, embedding_dimension, embedding_dimension), jnp.float32),
    )
    prefix_total, prefix_state = entering((group_total, local_state), "seq", combine, blank)
    incoming = jnp.exp(prefix_total)[:, :, None] * carried_memory + prefix_state
    before_row = jnp.cumsum(long_decay, axis=0) - long_decay
    long_out = long_out + jnp.einsum(
        "ihc,hcd->ihd", recept3[:long_rows] * jnp.exp(before_row), incoming, precision=highest
    )
    span_end = jnp.exp(group_total)[:, :, None] * incoming + local_state
    live_rows = (
        lax.broadcasted_iota(jnp.int32, (requests, slot_rows), 1) < prompt_live_extents[:, None]
    )
    live_flat = live_rows.reshape(requests * slot_rows).astype(jnp.float32)[:, None, None]
    short_shape = (requests, slot_rows, per_group_view, embedding_dimension)
    short_recept = recept3[long_rows:].reshape(short_shape)
    short_keys = (keys3[long_rows:] * live_flat).reshape(short_shape)
    short_values = values3[long_rows:].reshape(short_shape)
    short_decay = (decay3[long_rows:] * live_flat).reshape(short_shape)
    zeroed_memory = jnp.zeros(
        (per_group_view, embedding_dimension, embedding_dimension), jnp.float32
    )

    def request_pass(acceptance_lines, lookup_table, payload_table, fading_table):
        return block_sweep(
            zeroed_memory,
            acceptance_lines,
            lookup_table,
            payload_table,
            fading_table,
            present_reward,
        )

    request_states, short_out = jax.vmap(request_pass)(
        short_recept, short_keys, short_values, short_decay
    )
    wkv = jnp.concatenate(
        [long_out, short_out.reshape(requests * slot_rows, per_group_view, embedding_dimension)],
        axis=0,
    )
    mean = jnp.mean(wkv, axis=-1, keepdims=True)
    centred = wkv - mean
    variance = jnp.mean(centred * centred, axis=-1, keepdims=True)
    normed = (centred * lax.rsqrt(variance + norm_eps)).reshape(
        total_rows, columns
    ) * group_layer_scaling[None, :] + group_layer_shift_term[None, :]
    row_live = jnp.concatenate(
        [jnp.ones((long_rows,), dtype=bool), live_rows.reshape(requests * slot_rows)], axis=0
    )
    hidden = jnp.where(row_live[:, None], normed * jax.nn.silu(gate), 0.0).astype(jnp.bfloat16)
    full_out = lax.all_gather(final_transform, "seq", axis=1, tiled=True)
    mixed_rows = lax.psum_scatter(
        jnp.dot(hidden, full_out, preferred_element_type=jnp.float32),
        "mp",
        scatter_dimension=0,
        tiled=True,
    )
    return (mixed_rows.astype(jnp.bfloat16)[None], span_end[None], request_states)


f32 = jnp.float32
bf16 = jnp.bfloat16
VMEM_LIMIT = 56 * 1024 * 1024
TILE = 256


def in_vmem():
    return pl.BlockSpec(memory_space=pltpu.VMEM)


def in_smem():
    return pl.BlockSpec(memory_space=pltpu.SMEM)


def takes(us):
    return pl.CostEstimate(
        flops=int(us * 1.15e9), bytes_accessed=int(us * 3.0e6), transcendentals=0
    )


def kernel_params():
    return pltpu.CompilerParams(vmem_limit_bytes=VMEM_LIMIT)


FIRST_PART = 48
EXTRA = 16


def here_and_step(x_ref, is_long, period, tile):
    rows = x_ref.shape[1] - EXTRA
    here = x_ref[tile, 0:rows, :].astype(f32)
    above = x_ref[jnp.maximum(tile - 1, 0), rows - 16 : rows, :].astype(f32)[15:16]
    first = jnp.where(is_long == 1, x_ref[0, rows : rows + 16, :].astype(f32)[0:1], 0.0)
    row = lax.broadcasted_iota(jnp.int32, here.shape, 0)
    before = jnp.where(row == 0, above, pltpu.roll(here, 1, 0))
    start = ((row + tile * rows) & (period - 1)) == 0
    before = jnp.where(start, first, before)
    return here, before - here


def given_kernel(kind, extents, long_ref, short_ref, out_ref):
    rows = long_ref.shape[0]
    is_long = kind[0] == 1
    out_ref[0:rows, :] = jnp.where(is_long, short_ref[...], long_ref[...])
    lane = lax.broadcasted_iota(jnp.int32, (EXTRA, out_ref.shape[1]), 1)
    line = jnp.zeros(lane.shape, f32)
    for n in range(extents.shape[0]):
        line = jnp.where(lane == n, extents[n].astype(f32), line)
    out_ref[rows : rows + EXTRA, :] = line.astype(bf16)


def given_to_other_core(kind, extents, long_rows, short_rows):
    rows, columns = long_rows.shape
    return pl.pallas_call(
        given_kernel,
        out_shape=jax.ShapeDtypeStruct((rows + EXTRA, columns), bf16),
        in_specs=[in_smem()] * 2 + [in_vmem()] * 2,
        out_specs=in_vmem(),
        compiler_params=kernel_params(),
        cost_estimate=takes(1.5),
    )(kind, extents, long_rows, short_rows)


def block_kernel(kind, extents, long_ref, short_ref, taken, edge, out_ref):
    rows = long_ref.shape[0]
    depth = out_ref.shape[2]
    is_long = kind[0] == 1
    count = extents.shape[0]
    row = lax.broadcasted_iota(jnp.int32, (EXTRA, depth), 0)
    lane = lax.broadcasted_iota(jnp.int32, (EXTRA, depth), 1)
    other = taken[rows : rows + EXTRA, 0:depth].astype(f32)
    line = jnp.where(is_long, pltpu.roll(other, count, 1), other)
    own_at = jnp.where(is_long, 0, count)
    for n in range(count):
        line = jnp.where(lane == own_at + n, extents[n].astype(f32), line)
    for half in range(2):
        start = jnp.where(is_long, half, 1 - half) * depth
        at = pl.ds(pl.multiple_of(start, depth), depth)
        got = taken[0:rows, at]
        out_ref[half, 0:rows, :] = jnp.where(is_long, long_ref[:, at], got)
        out_ref[half, rows : 2 * rows, :] = jnp.where(is_long, got, short_ref[:, at])
        first = edge[:, at].astype(f32)
        out_ref[half, 2 * rows :, :] = jnp.where(row == 0, first, line).astype(bf16)


def block_of_chip(kind, extents, long_rows, short_rows, taken, edge):
    rows, columns = long_rows.shape
    return pl.pallas_call(
        block_kernel,
        out_shape=jax.ShapeDtypeStruct((2, 2 * rows + EXTRA, columns // 2), bf16),
        in_specs=[in_smem()] * 2 + [in_vmem()] * 4,
        out_specs=in_vmem(),
        compiler_params=kernel_params(),
        cost_estimate=takes(1.5),
    )(kind, extents, long_rows, short_rows, taken, edge)


def half_block(shape):
    return pl.BlockSpec((1,) + shape[1:], lambda i: (i,) + (0,) * (len(shape) - 1))


def gather_blocks(kind, own, rest, held):
    held[kind[6]] = own[...]
    for k in range(3):
        held[kind[7 + k]] = rest[k]


def mix_kernel(kind, own, rest, ratios, left, kv_mix, r_mix, gate_mix, squeezed, held):
    gather_blocks(kind, own.at[0], rest.at[0], held)

    @pl.loop(0, held.shape[0], unroll=2)
    def _(tile):
        here, step = here_and_step(held, kind[0], kind[1], tile)
        at = pl.ds(pl.multiple_of(tile * TILE, TILE), TILE)

        def mix(which):
            return (here + ratios[0, which : which + 1, :] * step).astype(bf16)

        r_mix[0, at, :] = mix(0)
        kv_mix[0, 0, at, :] = mix(1)
        kv_mix[0, 1, at, :] = mix(2)
        gate_mix[0, at, :] = mix(3)
        squeezed[0, at, :] = jnp.dot(mix(4), left[0], preferred_element_type=f32)


def mixes_of(kind, own, rest, ratios, left):
    rows, depth = own.shape[1] - EXTRA, own.shape[2]
    lines = rest.shape[1] + 1
    whole = lines * rows
    outs = [
        jax.ShapeDtypeStruct((2, 2, whole, depth), bf16),
        jax.ShapeDtypeStruct((2, whole, depth), bf16),
        jax.ShapeDtypeStruct((2, whole, depth), bf16),
        jax.ShapeDtypeStruct((2, whole, left.shape[2]), f32),
    ]
    return pl.pallas_call(
        mix_kernel,
        grid=(2,),
        out_shape=outs,
        in_specs=[in_smem()] + [half_block(a.shape) for a in (own, rest, ratios, left)],
        out_specs=[half_block(out.shape) for out in outs],
        scratch_shapes=[pltpu.VMEM((lines, rows + EXTRA, depth), bf16)],
        compiler_params=kernel_params(),
        cost_estimate=takes(7),
    )(kind, own, rest, ratios, left)


def pair_kernel(kind, mix0, mix1, mix2, own, sibling, keys_ref, values_ref):
    half = pl.program_id(0)
    for which, out in enumerate((keys_ref, values_ref)):
        part = None
        for rel, mixes in enumerate((mix0, mix1, mix2)):
            at = kind[10 + rel]
            weight = jnp.where(half == 0, own[at, which], sibling[at, which])
            new = jnp.dot(mixes[0, which], weight, preferred_element_type=f32)
            part = new if part is None else part + new

        @pl.when(half == 0)
        def _():
            out[...] = part

        @pl.when(half == 1)
        def _():
            out[...] += part


def pair_product(kind, mixes, own, sibling):
    rows, width = mixes[0].shape[2], own.shape[3]
    return pl.pallas_call(
        pair_kernel,
        grid=(2,),
        out_shape=[jax.ShapeDtypeStruct((rows, width), f32)] * 2,
        in_specs=[in_smem()] + [half_block(mix.shape) for mix in mixes] + [in_vmem()] * 2,
        out_specs=[pl.BlockSpec((rows, width), lambda i: (0, 0))] * 2,
        compiler_params=kernel_params(),
        cost_estimate=takes(8),
    )(kind, *mixes, own, sibling)


def project_kernel(
    kind,
    mix0,
    mix1,
    mix2,
    low0,
    low1,
    low2,
    keys_part,
    values_part,
    own0,
    own1,
    rest0,
    rest1,
    ratios,
    left,
    own_kv,
    sibling_kv,
    own_r,
    sibling_r,
    right,
    base,
    recept_ref,
    keys_ref,
    values_ref,
    decay_ref,
    gate_mix,
    held,
):
    tile = pl.program_id(0)

    @pl.when(tile == 0)
    def _():
        for half, (own, rest) in enumerate(((own0, rest0), (own1, rest1))):
            gather_blocks(kind, own, rest, held.at[half])

    last = kind[13]
    totals = [jnp.zeros(recept_ref.shape, f32), keys_part[...], values_part[...]]
    squeezed = low0[0] + low0[1] + low1[0] + low1[1] + low2[0] + low2[1]
    for half in range(2):
        here, step = here_and_step(held.at[half], kind[0], kind[1], tile)
        kv, r = ((own_kv, own_r), (sibling_kv, sibling_r))[half]

        def mix(which):
            return (here + ratios[half, which : which + 1, :] * step).astype(bf16)

        for which, weight in enumerate((r[last, 0], kv[last, 0], kv[last, 1])):
            totals[which] += jnp.dot(mix(which), weight, preferred_element_type=f32)
        gate_mix[half] = mix(3)
        squeezed = squeezed + jnp.dot(mix(4), left[half], preferred_element_type=f32)
    for rel, mixes in enumerate((mix0, mix1, mix2)):
        for half in range(2):
            weight = (own_r, sibling_r)[half][kind[10 + rel], 0]
            totals[0] += jnp.dot(mixes[half], weight, preferred_element_type=f32)
    recept_ref[...] = totals[0]
    keys_ref[...] = totals[1]
    values_ref[...] = totals[2]
    squeezed = jnp.tanh(squeezed).astype(bf16)
    grown = jnp.dot(squeezed, right[...], preferred_element_type=f32)
    decay_ref[...] = -jnp.exp(base[...] + grown)


def projected(kind, mixes, lows, parts, owns, rests, *rest):
    rows, depth = mixes[0].shape[1:]
    width, rank = parts[0].shape[1], lows[0].shape[2]
    flat = jax.ShapeDtypeStruct((rows, width), f32)
    tile_of = pl.BlockSpec((TILE, width), lambda i: (i, 0))
    wide_of = pl.BlockSpec((2, TILE, depth), lambda i: (0, i, 0))
    return pl.pallas_call(
        project_kernel,
        grid=(rows // TILE,),
        out_shape=[flat] * 4 + [jax.ShapeDtypeStruct((2, rows, depth), bf16)],
        in_specs=[in_smem()]
        + [wide_of] * 3
        + [pl.BlockSpec((2, TILE, rank), lambda i: (0, i, 0))] * 3
        + [tile_of] * 2
        + [in_vmem()] * (4 + len(rest)),
        out_specs=[tile_of] * 4 + [wide_of],
        scratch_shapes=[pltpu.VMEM((2, rests[0].shape[0] + 1) + owns[0].shape, bf16)],
        compiler_params=kernel_params(),
        cost_estimate=takes(11),
    )(kind, *mixes, *lows, *parts, *owns, *rests, *rest)


def gate_kernel(
    kind,
    lengths,
    mix0,
    mix1,
    mix2,
    mix3,
    own,
    sibling,
    normed,
    kept0,
    sent0,
    kept1,
    sent1,
    total,
):
    half = pl.program_id(0)
    part = None
    for rel, mixes in enumerate((mix0, mix1, mix2, mix3)):
        weight = jnp.where(half == 0, own[kind[10 + rel], 0], sibling[kind[10 + rel], 0])
        new = jnp.dot(mixes[0], weight, preferred_element_type=f32)
        part = new if part is None else part + new

    @pl.when(half == 0)
    def _():
        total[...] = part

    @pl.when(half == 1)
    def _():
        gate = total[...] + part
        value = normed[...] * (gate * jax.nn.sigmoid(gate))
        row = lax.broadcasted_iota(jnp.int32, (BLK, value.shape[1]), 0)
        is_long = kind[0] == 1
        cut = kept0.shape[2]

        def lived(n):
            block = value[n * BLK : (n + 1) * BLK]
            return jnp.where(row < lengths[n], block, 0.0).astype(bf16)

        for line in range(kept0.shape[1]):
            for block in range(2):
                even, odd = lived(4 * line + block), lived(4 * line + 2 + block)
                kept = jnp.where(is_long, even, odd)
                sent = jnp.where(is_long, odd, even)
                kept0[block, line] = kept[:cut]
                kept1[block, line] = kept[cut:]
                sent0[block, line] = sent[:cut]
                sent1[block, line] = sent[cut:]


def gated(kind, lengths, mixes, own, sibling, normed):
    rows, width = normed.shape
    outs = [
        jax.ShapeDtypeStruct((2, rows // TILE, part, width), bf16)
        for part in (FIRST_PART, FIRST_PART, BLK - FIRST_PART, BLK - FIRST_PART)
    ]
    return pl.pallas_call(
        gate_kernel,
        grid=(2,),
        out_shape=outs,
        in_specs=[in_smem()] * 2 + [half_block(mix.shape) for mix in mixes] + [in_vmem()] * 3,
        out_specs=[pl.BlockSpec(out.shape, lambda i: (0, 0, 0, 0)) for out in outs],
        scratch_shapes=[pltpu.VMEM((rows, width), f32)],
        compiler_params=kernel_params(),
        cost_estimate=takes(7),
    )(kind, lengths, *mixes, own, sibling, normed)


def head_blocks(heads):
    width = heads * BLK
    tall = lax.broadcasted_iota(jnp.int32, (width, width), 0) // BLK
    wide = lax.broadcasted_iota(jnp.int32, (width, width), 1) // BLK
    return tall == wide


def state_kernel(lengths, carry, k_ref, v_ref, w_ref, s_ref, state_ref, entered_ref, hold):
    span, width = BLK, k_ref.shape[1]
    heads = width // span
    row = lax.broadcasted_iota(jnp.int32, (span, width), 0)
    lane = lax.broadcasted_iota(jnp.int32, (span, width), 1)
    for h in range(heads):
        hold[:, h * span : (h + 1) * span] = s_ref[h]

    @pl.loop(0, k_ref.shape[0] // span, unroll=8)
    def _(n):
        at = pl.ds(pl.multiple_of(n * span, span), span)
        live = row < lengths[n]
        k = jnp.where(live, k_ref[at, :], 0.0)
        total = jnp.where(live, w_ref[at, :], 0.0)
        after_row = jnp.zeros_like(total)
        half = 1
        while half < span:
            upper = (row & half) != 0
            across = jnp.where(
                upper, pltpu.roll(total, half, 0), pltpu.roll(total, span - half, 0)
            )
            after_row = after_row + jnp.where(upper, 0.0, across)
            total = total + across
            half *= 2
        added = lax.dot_general(
            (k * jnp.exp(after_row)).astype(bf16),
            v_ref[at, :].astype(bf16),
            (((0,), (0,)), ((), ())),
            preferred_element_type=f32,
        )
        fresh = jnp.zeros((span, width), f32)
        for h in range(heads):
            fresh = jnp.where(lane // span == h, added[h * span : (h + 1) * span], fresh)
        twice = jnp.concatenate([total] * 2, axis=0)
        turned_parts = []
        for p in range(width // (2 * span)):
            flipped = jnp.transpose(twice[:, p * 2 * span : (p + 1) * 2 * span])
            turned_parts.append(
                jnp.where(lane[:, : 2 * span] < span, flipped[:span], flipped[span:])
            )
        fade = jnp.exp(jnp.concatenate(turned_parts, axis=1))
        entered = hold[...] * carry[0]
        entered_ref[n] = entered.astype(bf16)
        state = fade * entered + fresh
        hold[...] = state
        for h in range(heads):
            state_ref[n, h] = state[:, h * span : (h + 1) * span]


def states_of(lengths, carry, k, v, w, state):
    rows, width = k.shape
    heads = width // BLK
    return pl.pallas_call(
        state_kernel,
        out_shape=[
            jax.ShapeDtypeStruct((rows // BLK, heads, BLK, BLK), f32),
            jax.ShapeDtypeStruct((rows // BLK, BLK, width), bf16),
        ],
        in_specs=[in_smem()] * 2 + [in_vmem()] * 4,
        out_specs=[in_vmem()] * 2,
        scratch_shapes=[pltpu.VMEM((BLK, width), f32)],
        compiler_params=kernel_params(),
        cost_estimate=takes(7),
    )(lengths, carry, k, v, w, state)


def sweep_kernel(lengths, r_ref, k_ref, v_ref, w_ref, entered_ref, u_ref, gain, bias, out_ref):
    span, width = BLK, r_ref.shape[1]
    heads = width // span
    row = lax.broadcasted_iota(jnp.int32, (span, width), 0)
    lane = lax.broadcasted_iota(jnp.int32, (span, width), 1)
    col = lane % span
    same_head = head_blocks(heads)

    def spread(value):
        stacked = jnp.concatenate([value.astype(bf16)] * heads, axis=0)
        return jnp.where(same_head, stacked, jnp.zeros_like(stacked))

    def against(a, b):
        return lax.dot_general(a, b, (((1,), (1,)), ((), ())), preferred_element_type=f32)

    @pl.loop(0, r_ref.shape[0] // span, unroll=4)
    def _(n):
        at = pl.ds(pl.multiple_of(n * span, span), span)
        live = row < lengths[n]
        r, v = r_ref[at, :], v_ref[at, :]
        k = jnp.where(live, k_ref[at, :], 0.0)
        total = jnp.where(live, w_ref[at, :], 0.0)
        before = jnp.zeros_like(total)
        after_row = jnp.zeros_like(total)
        scores = against((r * u_ref[...]).astype(bf16), spread(k))
        scores = jnp.where(row == col, scores, 0.0)
        level = 0
        while (1 << level) < span:
            half = 1 << level
            upper = (row & half) != 0
            if level:
                scale = jnp.exp(jnp.where(upper, before, after_row))
                part = against((r * scale).astype(bf16), spread(k * scale))
            else:
                part = against(r.astype(bf16), spread(k))
            pair = upper & (((row >> level) ^ (col >> level)) == 1)
            scores = jnp.where(pair, part, scores)
            across = jnp.where(
                upper, pltpu.roll(total, half, 0), pltpu.roll(total, span - half, 0)
            )
            before = before + jnp.where(upper, across, 0.0)
            after_row = after_row + jnp.where(upper, 0.0, across)
            total = total + across
            level += 1
        out = jnp.dot(scores.astype(bf16), spread(v), preferred_element_type=f32)
        out = out + jnp.dot(
            (r * jnp.exp(before)).astype(bf16),
            spread(entered_ref[n]),
            preferred_element_type=f32,
        )
        out_ref[at, :] = out

    ones = jnp.where(same_head, 1.0, 0.0).astype(bf16)

    def head_mean(value):
        high = value.astype(bf16)
        low = (value - high.astype(f32)).astype(bf16)
        both = jnp.dot(high, ones, preferred_element_type=f32) + jnp.dot(
            low, ones, preferred_element_type=f32
        )
        return both * (1.0 / span)

    @pl.loop(0, r_ref.shape[0] // TILE, unroll=2)
    def _(tile):
        at = pl.ds(pl.multiple_of(tile * TILE, TILE), TILE)
        value = out_ref[at, :]
        centred = value - head_mean(value)
        spread_of = head_mean(centred * centred)
        out_ref[at, :] = centred * lax.rsqrt(spread_of + norm_eps) * gain[...] + bias[...]


def sweep(lengths, r, k, v, w, entered, bonus, gain, bias):
    return pl.pallas_call(
        sweep_kernel,
        out_shape=jax.ShapeDtypeStruct(r.shape, f32),
        in_specs=[in_smem()] + [in_vmem()] * 8,
        out_specs=in_vmem(),
        compiler_params=kernel_params(),
        cost_estimate=takes(12),
    )(lengths, r, k, v, w, entered, bonus, gain, bias)


def final_kernel(block_of, h0, h1, h2, h3, weight, o0, o1, o2, o3, hold):
    @pl.loop(0, hold.shape[1] // TILE, unroll=2)
    def _(tile):
        at = pl.ds(pl.multiple_of(tile * TILE, TILE), TILE)
        total = None
        for k, piece in enumerate((h0, h1, h2, h3)):
            part = jnp.dot(piece[...], weight[k, :, at], preferred_element_type=f32)
            total = part if total is None else total + part
        hold[:, at] = total.astype(bf16)

    block = hold.shape[0] // 4
    for rel, out in enumerate((o0, o1, o2, o3)):
        at = pl.ds(pl.multiple_of(block_of[rel] * block, block), block)
        out[...] = hold[at, :].reshape(out.shape)


def final_product(block_of, pieces, weight, lines):
    rows, width = pieces[0].shape[0], weight.shape[2]
    out = jax.ShapeDtypeStruct((lines, rows // 4 // lines, width), bf16)
    return pl.pallas_call(
        final_kernel,
        out_shape=[out] * 4,
        in_specs=[in_smem()] + [in_vmem()] * 5,
        out_specs=[in_vmem()] * 4,
        scratch_shapes=[pltpu.VMEM((rows, width), bf16)],
        compiler_params=kernel_params(),
        cost_estimate=takes(4.5),
    )(block_of, *pieces, weight)


def lay_kernel(at, *refs):
    pieces, out_ref = refs[:-1], refs[-1]
    width = pieces[0].shape[1]
    lines = out_ref.shape[1] // width
    row = 0
    for n, piece in enumerate(pieces):
        column = pl.multiple_of(at[n % lines] * width, width)
        out_ref[row : row + piece.shape[0], pl.ds(column, width)] = piece[...]
        if n % lines == lines - 1:
            row += piece.shape[0]


def laid(at, pieces, lines):
    rows, width = sum(piece.shape[0] for piece in pieces) // lines, pieces[0].shape[1]
    return pl.pallas_call(
        lay_kernel,
        out_shape=jax.ShapeDtypeStruct((rows, lines * width), bf16),
        in_specs=[in_smem()] + [in_vmem()] * len(pieces),
        out_specs=in_vmem(),
        compiler_params=kernel_params(),
        cost_estimate=takes(2),
    )(at, *pieces)


def after(value, *others):
    return lax.optimization_barrier((value,) + others)[0]


def turned(x, axis, by):
    length = lax.axis_size(axis)
    return lax.ppermute(x, axis, [(i, (i + by) % length) for i in range(length)])


def flipped_core(x):
    return lax.ppermute(x, "core", [(0, 1), (1, 0)])


def over_x(x):
    return lax.ppermute(x, "x", [(0, 1), (1, 0)])


def over_y(x):
    return lax.ppermute(x, "y", [(0, 1), (1, 0)])


def dealt(blocks, z):
    length = lax.axis_size("z")
    return [blocks(z)] + [turned(blocks((z + k) % length), "z", k) for k in range(1, length)]


def near_along(piece):
    two = turned(piece, "z", 2)
    one = lax.ppermute(piece, "z", [(0, 1), (1, 2), (2, 3)])
    three = lax.ppermute(piece, "z", [(1, 0), (2, 1), (3, 2)])
    return one, two, three


def far_along(two):
    return lax.ppermute(two, "z", [(1, 0), (2, 3)])


def spread_along(piece, z):
    one, two, three = near_along(piece)
    return piece, one, two, three, far_along(two)


def in_place(spread, z, at=0):
    piece, one, two, three, far = spread
    whole = jnp.zeros((4,) + piece.shape, piece.dtype)
    for k, part in ((1, one), (2, two), (3, three)):
        whole = lax.dynamic_update_index_in_dim(whole, part, (z - k) % 4, 0)
    far_at = jnp.where(z == 0, 3, jnp.where(z == 3, 0, z))
    whole = lax.dynamic_update_index_in_dim(whole, far, far_at, 0)
    return lax.dynamic_update_index_in_dim(whole, piece, z, 0)


def in_order(pieces, z):
    length = len(pieces)
    whole = jnp.zeros((length,) + pieces[0].shape, pieces[0].dtype)
    for k, piece in enumerate(pieces):
        whole = lax.dynamic_update_index_in_dim(whole, piece, (z - k) % length, 0)
    return whole


def on_core(
    continued_prompt_entries,
    padded_prompt_entries,
    prompt_live_extents,
    preceding_entry_line,
    carried_memory,
    token_mixing_ratios,
    acceptance_transform,
    lookup_transform,
    payload_transform,
    gating_transform,
    fading_baseline,
    fading_left_factor,
    fading_right_factor,
    present_reward,
    group_layer_scaling,
    group_layer_shift_term,
    final_transform,
):
    z, core = lax.axis_index("z"), lax.axis_index("core")
    y, x = lax.axis_index("y"), lax.axis_index("x")
    mp = 2 * y + x
    is_long = core == 0
    lines = lax.axis_size("z")
    group_rows, columns = continued_prompt_entries.shape
    requests = prompt_live_extents.shape[0]
    slot_rows = group_rows // requests
    heads, span = present_reward.shape
    heads = heads // lines
    width = heads * span
    depth = acceptance_transform.shape[0]
    rows = 2 * lines * group_rows

    kind = jnp.stack(
        [is_long.astype(jnp.int32), jnp.where(is_long, rows, slot_rows).astype(jnp.int32)]
        + [(mp ^ rel).astype(jnp.int32) for rel in range(4)]
        + [((z - k) % lines).astype(jnp.int32) for k in range(4)]
        + [((z - (mp ^ rel)) % lines).astype(jnp.int32) for rel in range(4)]
    )
    given = given_to_other_core(
        kind, prompt_live_extents, continued_prompt_entries, padded_prompt_entries
    )
    taken = flipped_core(given)
    block = block_of_chip(
        kind,
        prompt_live_extents,
        continued_prompt_entries,
        padded_prompt_entries,
        taken,
        preceding_entry_line[None],
    )
    (
        block,
        acceptance_transform,
        lookup_transform,
        payload_transform,
        gating_transform,
        final_transform,
        token_mixing_ratios,
        fading_left_factor,
        fading_right_factor,
        fading_baseline,
        present_reward,
        group_layer_scaling,
        group_layer_shift_term,
        carried_memory,
    ) = lax.optimization_barrier(
        (
            block,
            acceptance_transform,
            lookup_transform,
            payload_transform,
            gating_transform,
            final_transform,
            token_mixing_ratios,
            fading_left_factor,
            fading_right_factor,
            fading_baseline,
            present_reward,
            group_layer_scaling,
            group_layer_shift_term,
            carried_memory,
        )
    )
    one, two, three = near_along(block)
    own_x, own_y = over_x(block), over_y(block)
    one, two, three, own_x, own_y = lax.optimization_barrier((one, two, three, own_x, own_y))
    def blocks_of(*weights):
        stacked = jnp.stack(weights)
        return tuple(
            lax.dynamic_slice_in_dim(stacked, (z + k) % lines * width, width, 2)
            for k in range(lines)
        )

    def both_cores(*pieces):
        own = jnp.stack(pieces)
        return own, flipped_core(own)

    kv = blocks_of(lookup_transform, payload_transform)
    r = blocks_of(acceptance_transform)
    gate = blocks_of(gating_transform)
    kv = after(kv, two)
    far = far_along(two)
    own_xy = (over_y(own_x[0]), over_x(own_y[1]))
    kv_two = turned(kv[2], "z", 2)
    far, own_xy, kv_two, kv, r = lax.optimization_barrier((far, own_xy, kv_two, kv, r))
    rest = jnp.stack([jnp.where(z == 0, far, one), two, jnp.where(z == 3, far, three)], axis=1)
    rest_x, rest_y = over_x(rest), over_y(rest)
    extents = in_order(
        [part[2 * group_rows + 1, : 2 * requests] for part in (block[0],) + tuple(rest[0])], z
    ).reshape(2 * lines * requests)
    extents = jnp.where(is_long, slot_rows, extents.astype(jnp.int32)).astype(jnp.int32)

    def chunk_order(whole):
        split = whole.reshape((4, 2, depth) + whole.shape[1:])
        parts = []
        for rel in range(4):
            both = split[mp ^ rel]
            parts.append(jnp.where(is_long, both, both[::-1]))
        return parts

    ratios = [part.transpose(0, 2, 1) for part in chunk_order(token_mixing_ratios.T)]
    left = chunk_order(fading_left_factor)

    kv_one, kv_three = turned(kv[1], "z", 1), turned(kv[3], "z", 3)
    r_two = turned(r[2], "z", 2)
    rest_x, rest_y, kv_one, kv_three, r_two, r = lax.optimization_barrier(
        (rest_x, rest_y, kv_one, kv_three, r_two, r)
    )
    rest_xy = (over_y(rest_x[0]), over_x(rest_y[1]))
    own_kv, sibling_kv = both_cores(kv[0], kv_one, kv_two, kv_three)
    r_one, r_three = turned(r[1], "z", 1), turned(r[3], "z", 3)
    rest_xy, r_one, r_three, gate = lax.optimization_barrier((rest_xy, r_one, r_three, gate))
    own_r, sibling_r = both_cores(r[0], r_one, r_two, r_three)
    gate_pieces = (gate[0],) + tuple(turned(gate[k], "z", k) for k in range(1, lines))

    def mine_of(vector):
        return lax.dynamic_slice_in_dim(vector, z * width, width, 0)[None]

    kv0, r0, gate0, low0 = mixes_of(kind, block, rest, ratios[0], left[0])
    kv1, r1, gate1, low1 = mixes_of(kind, own_x, rest_x, ratios[1], left[1])
    kv2, r2, gate2, low2 = mixes_of(kind, own_y, rest_y, ratios[2], left[2])
    parts = pair_product(kind, (kv0, kv1, kv2), own_kv, sibling_kv)
    recept, keys, values, decay, gate3 = projected(
        kind,
        (r0, r1, r2),
        (low0, low1, low2),
        parts,
        own_xy,
        rest_xy,
        ratios[3],
        left[3],
        own_kv,
        sibling_kv,
        own_r,
        sibling_r,
        lax.dynamic_slice_in_dim(fading_right_factor, z * width, width, 1),
        mine_of(fading_baseline),
    )
    entered = lax.dynamic_slice_in_dim(carried_memory, z * heads, heads, 0)
    bonus = lax.dynamic_slice_in_dim(present_reward, z * heads, heads, 0).reshape(1, width)
    states, states_in = states_of(
        extents,
        is_long.astype(f32)[None],
        keys,
        values,
        decay,
        jnp.where(is_long, entered, 0.0),
    )
    states = states.reshape(lines, 2, requests, heads, span, span)
    passed = flipped_core(lax.dynamic_index_in_dim(states, 1 - core, 1, keepdims=False))
    held = lax.dynamic_index_in_dim(states, core, 1, keepdims=False)
    bundle = jnp.concatenate(
        [jnp.where(is_long, held, passed)[:, -1:], jnp.where(is_long, passed, held)], axis=1
    ).astype(bf16)
    bundle = after(bundle, gate_pieces)
    states_in = after(states_in, bundle)
    arrived = dealt(lambda j: lax.dynamic_index_in_dim(bundle, j, 0, keepdims=False), z)
    normed = sweep(
        extents,
        recept,
        keys,
        values,
        decay,
        states_in,
        bonus,
        mine_of(group_layer_scaling),
        mine_of(group_layer_shift_term),
    )
    own_gate, sibling_gate = both_cores(*after(gate_pieces, states))
    normed, arrived = lax.optimization_barrier((normed, arrived))
    kept0, sent0, kept1, sent1 = gated(
        kind, extents, (gate0, gate1, gate2, gate3), own_gate, sibling_gate, normed
    )

    arrived = in_order(arrived, z).astype(f32)
    span_states = arrived[:, 0].reshape(1, lines * heads, span, span)
    request_states = jnp.swapaxes(arrived[:, 1:], 0, 1).reshape(
        requests, lines * heads, span, span
    )

    wide_out = 2 * final_transform.shape[1]
    beside = flipped_core(final_transform)
    out_weight = jnp.concatenate(
        [
            jnp.where(is_long, final_transform, beside),
            jnp.where(is_long, beside, final_transform),
        ],
        axis=1,
    ).reshape(lines, width, wide_out)
    out_weight = jnp.stack(
        [
            lax.dynamic_index_in_dim(out_weight, (z - k) % lines, 0, keepdims=False)
            for k in range(lines)
        ]
    )
    order = jnp.stack([(z - k) % lines for k in range(lines)]).astype(jnp.int32)
    block_of = jnp.stack(
        [(((y ^ (rel >> 1)) ^ core) * 2 + (x ^ (rel & 1))).astype(jnp.int32) for rel in range(4)]
    )
    spreads = []
    for kept, sent in ((kept0, sent0), (kept1, sent1)):
        part = jnp.concatenate([kept, flipped_core(sent)], axis=0)
        part = part.reshape(-1, width)
        if spreads:
            part = after(part, spreads[0][2])
        spreads.append(spread_along(part, z))
    out_pieces = []
    for piece, one, two, three, far in spreads:
        one = jnp.where(z == 0, far, one)
        three = jnp.where(z == 3, far, three)
        here, to_x, to_y, to_xy = final_product(
            block_of, (piece, one, two, three), out_weight, lines
        )
        across = lax.ppermute(to_xy, ("y", "x"), [(i, 3 - i) for i in range(4)])
        mixed_part = (
            here.astype(f32)
            + over_x(to_x).astype(f32)
            + over_y(to_y).astype(f32)
            + across.astype(f32)
        ).astype(bf16)
        out_pieces += dealt(
            lambda j: lax.dynamic_index_in_dim(mixed_part, j, 0, keepdims=False), z
        )
    mixed = laid(order, out_pieces, lines)[None]
    return mixed, span_states, request_states


def rows_kept_solution(mesh):
    placed = (
        P("seq", "mp"),
        P("seq", "mp"),
        P("seq"),
        P("mp"),
        P("mp", None, None),
        P(),
        P("seq", "mp"),
        P("seq", "mp"),
        P("seq", "mp"),
        P("seq", "mp"),
        P("mp"),
        P(),
        P(None, "mp"),
        P("mp", None),
        P("mp"),
        P("mp"),
        P("mp", "seq"),
    )
    return jax.shard_map(
        on_device,
        mesh=mesh,
        in_specs=placed,
        out_specs=(P("seq", "mp", None), P("seq", "mp", None, None), P("seq", "mp", None, None)),
        check_vma=False,
    )


def heads_kept_solution(mesh):
    seq, mp = mesh.shape["seq"], mesh.shape["mp"]
    split = Mesh(mesh.devices.reshape(seq // 2, 2, 2, mp // 2), ("z", "core", "y", "x"))
    s, m = ("z", "core"), ("y", "x")
    placed = (
        P(s, m),
        P(s, m),
        P(s),
        P(m),
        P(m, None, None),
        P(),
        P(s, m),
        P(s, m),
        P(s, m),
        P(s, m),
        P(m),
        P(),
        P(None, m),
        P(m, None),
        P(m),
        P(m),
        P(m, s),
    )
    return jax.shard_map(
        on_core,
        mesh=split,
        in_specs=placed,
        out_specs=(P(s, m, None), P(s, m, None, None), P(s, m, None, None)),
        check_vma=False,
    )


def solution(mesh):
    if mesh.shape["mp"] == 4 and mesh.shape["seq"] == 8:
        return heads_kept_solution(mesh)
    return rows_kept_solution(mesh)
```

```python
import jax
import jax.numpy as jnp
from jax import lax
from jax.experimental import pallas as pl
from jax.experimental.pallas import tpu as pltpu
from jax.sharding import Mesh
from jax.sharding import PartitionSpec as P

BLK = 64


norm_eps = 0.00064
highest = lax.Precision.HIGHEST


def passed_along(x, axis, by):
    length = lax.axis_size(axis)
    pairs = [(i, i + by) for i in range(length) if 0 <= i + by < length]
    return lax.ppermute(x, axis, pairs)


def entering(value, axis, join, neutral):
    count, mine = (lax.axis_size(axis), lax.axis_index(axis))
    pieces = jax.tree.map(lambda part: lax.all_gather(part, axis), value)
    total = jax.tree.map(
        lambda part, zero: jnp.full_like(part, 0) + jnp.asarray(zero, part.dtype), value, neutral
    )

    def hop(position, total):
        longer = join(total, jax.tree.map(lambda part: part[position], pieces))
        return jax.tree.map(lambda new, old: jnp.where(position < mine, new, old), longer, total)

    return lax.fori_loop(0, count - 1, hop, total)


def mix_rows(current, previous, weight):
    here = current.astype(jnp.float32)
    return (here + weight[None, :] * (previous.astype(jnp.float32) - here)).astype(jnp.bfloat16)


def block_sweep(
    evolving_memory,
    acceptance_entries,
    lookup_entries,
    payload_entries,
    log_fading_amount,
    diagonal_reward,
):
    inclusive = jnp.cumsum(log_fading_amount, axis=0)
    exclusive = inclusive - log_fading_amount
    recept_scaled = acceptance_entries * jnp.exp(exclusive)
    keys_scaled = lookup_entries * jnp.exp(-inclusive)
    scores = jnp.einsum("ihc,jhc->hij", recept_scaled, keys_scaled, precision=highest)
    count = acceptance_entries.shape[0]
    row_index = lax.broadcasted_iota(jnp.int32, (count, count), 0)
    col_index = lax.broadcasted_iota(jnp.int32, (count, count), 1)
    scores = jnp.where((row_index > col_index)[None], scores, 0.0)
    diagonal_contribution = jnp.sum(
        acceptance_entries * diagonal_reward[None] * lookup_entries, axis=-1, keepdims=True
    )
    answer_lines = (
        jnp.einsum("hij,jhd->ihd", scores, payload_entries, precision=highest)
        + diagonal_contribution * payload_entries
    )
    answer_lines = answer_lines + jnp.einsum(
        "ihc,hcd->ihd", recept_scaled, evolving_memory, precision=highest
    )
    total = inclusive[-1]
    carried = lookup_entries * jnp.exp(total[None] - inclusive)
    new_state = jnp.exp(total)[:, :, None] * evolving_memory + jnp.einsum(
        "jhc,jhd->hcd", carried, payload_entries, precision=highest
    )
    return (new_state, answer_lines)


def continued_recurrence(
    acceptance_entries, lookup_entries, payload_entries, log_fading_amount, diagonal_reward
):
    length, per_group_view, embedding_dimension = acceptance_entries.shape
    blocks = length // BLK

    def step(evolving_memory, entry_lines):
        return block_sweep(
            evolving_memory,
            entry_lines[0],
            entry_lines[1],
            entry_lines[2],
            entry_lines[3],
            diagonal_reward,
        )

    shaped = tuple(
        (
            a.reshape(blocks, BLK, per_group_view, embedding_dimension)
            for a in (acceptance_entries, lookup_entries, payload_entries, log_fading_amount)
        )
    )
    evolving_memory, results = lax.scan(
        step,
        jnp.zeros((per_group_view, embedding_dimension, embedding_dimension), jnp.float32),
        shaped,
    )
    return (evolving_memory, results.reshape(length, per_group_view, embedding_dimension))


def combine(earlier, later):
    return (earlier[0] + later[0], jnp.exp(later[0])[:, :, None] * earlier[1] + later[1])


def shifted_rows(current, edge_row, long_rows, requests, slot_rows):
    feature_part = current.shape[1]
    long_prev = jnp.concatenate([edge_row, current[: long_rows - 1]], axis=0)
    short_view = current[long_rows:].reshape(requests, slot_rows, feature_part)
    short_prev = jnp.concatenate(
        [jnp.zeros((requests, 1, feature_part), current.dtype), short_view[:, :-1]], axis=1
    )
    short_prev = short_prev.reshape(requests * slot_rows, feature_part)
    return jnp.concatenate([long_prev, short_prev], axis=0)


def on_device(
    continued_prompt_entries,
    padded_prompt_entries,
    prompt_live_extents,
    preceding_entry_line,
    carried_memory,
    token_mixing_ratios,
    acceptance_transform,
    lookup_transform,
    payload_transform,
    gating_transform,
    fading_baseline,
    fading_left_factor,
    fading_right_factor,
    present_reward,
    group_layer_scaling,
    group_layer_shift_term,
    final_transform,
):
    long_rows = continued_prompt_entries.shape[0]
    requests = prompt_live_extents.shape[0]
    slot_rows = padded_prompt_entries.shape[0] // requests
    per_group_view, embedding_dimension = present_reward.shape
    arrived = passed_along(continued_prompt_entries[-1:], "seq", 1)
    first = lax.axis_index("seq") == 0
    edge_row = jnp.where(first, preceding_entry_line[None, :], arrived)
    current = jnp.concatenate([continued_prompt_entries, padded_prompt_entries], axis=0)
    current, edge_full = (
        lax.all_gather(current, "mp", axis=1, tiled=True),
        lax.all_gather(edge_row, "mp", axis=1, tiled=True),
    )
    previous = shifted_rows(current, edge_full, long_rows, requests, slot_rows)
    mixes = [mix_rows(current, previous, token_mixing_ratios[index]) for index in range(5)]
    total_rows = current.shape[0]
    columns = acceptance_transform.shape[1]
    pieces = (
        lax.all_gather(acceptance_transform, "seq", axis=0, tiled=True),
        lax.all_gather(lookup_transform, "seq", axis=0, tiled=True),
        lax.all_gather(payload_transform, "seq", axis=0, tiled=True),
        lax.all_gather(gating_transform, "seq", axis=0, tiled=True),
    )
    acceptance_entries, lookup_entries, payload_entries, gate = tuple(
        (
            jnp.dot(source, piece, preferred_element_type=jnp.float32)
            for source, piece in zip(mixes[:4], pieces)
        )
    )
    squeezed = jnp.tanh(
        jnp.dot(mixes[4], fading_left_factor, preferred_element_type=jnp.float32)
    ).astype(jnp.bfloat16)
    log_fading_amount = -jnp.exp(
        fading_baseline[None, :]
        + jnp.dot(squeezed, fading_right_factor, preferred_element_type=jnp.float32)
    )
    recept3, keys3, values3, decay3 = [
        a.reshape(total_rows, per_group_view, embedding_dimension)
        for a in (acceptance_entries, lookup_entries, payload_entries, log_fading_amount)
    ]
    local_state, long_out = continued_recurrence(
        recept3[:long_rows],
        keys3[:long_rows],
        values3[:long_rows],
        decay3[:long_rows],
        present_reward,
    )
    long_decay = decay3[:long_rows]
    group_total = jnp.sum(long_decay, axis=0)
    blank = (
        jnp.zeros((per_group_view, embedding_dimension), jnp.float32),
        jnp.zeros((per_group_view, embedding_dimension, embedding_dimension), jnp.float32),
    )
    prefix_total, prefix_state = entering((group_total, local_state), "seq", combine, blank)
    incoming = jnp.exp(prefix_total)[:, :, None] * carried_memory + prefix_state
    before_row = jnp.cumsum(long_decay, axis=0) - long_decay
    long_out = long_out + jnp.einsum(
        "ihc,hcd->ihd", recept3[:long_rows] * jnp.exp(before_row), incoming, precision=highest
    )
    span_end = jnp.exp(group_total)[:, :, None] * incoming + local_state
    live_rows = (
        lax.broadcasted_iota(jnp.int32, (requests, slot_rows), 1) < prompt_live_extents[:, None]
    )
    live_flat = live_rows.reshape(requests * slot_rows).astype(jnp.float32)[:, None, None]
    short_shape = (requests, slot_rows, per_group_view, embedding_dimension)
    short_recept = recept3[long_rows:].reshape(short_shape)
    short_keys = (keys3[long_rows:] * live_flat).reshape(short_shape)
    short_values = values3[long_rows:].reshape(short_shape)
    short_decay = (decay3[long_rows:] * live_flat).reshape(short_shape)
    zeroed_memory = jnp.zeros(
        (per_group_view, embedding_dimension, embedding_dimension), jnp.float32
    )

    def request_pass(acceptance_lines, lookup_table, payload_table, fading_table):
        return block_sweep(
            zeroed_memory,
            acceptance_lines,
            lookup_table,
            payload_table,
            fading_table,
            present_reward,
        )

    request_states, short_out = jax.vmap(request_pass)(
        short_recept, short_keys, short_values, short_decay
    )
    wkv = jnp.concatenate(
        [long_out, short_out.reshape(requests * slot_rows, per_group_view, embedding_dimension)],
        axis=0,
    )
    mean = jnp.mean(wkv, axis=-1, keepdims=True)
    centred = wkv - mean
    variance = jnp.mean(centred * centred, axis=-1, keepdims=True)
    normed = (centred * lax.rsqrt(variance + norm_eps)).reshape(
        total_rows, columns
    ) * group_layer_scaling[None, :] + group_layer_shift_term[None, :]
    row_live = jnp.concatenate(
        [jnp.ones((long_rows,), dtype=bool), live_rows.reshape(requests * slot_rows)], axis=0
    )
    hidden = jnp.where(row_live[:, None], normed * jax.nn.silu(gate), 0.0).astype(jnp.bfloat16)
    full_out = lax.all_gather(final_transform, "seq", axis=1, tiled=True)
    mixed_rows = lax.psum_scatter(
        jnp.dot(hidden, full_out, preferred_element_type=jnp.float32),
        "mp",
        scatter_dimension=0,
        tiled=True,
    )
    return (mixed_rows.astype(jnp.bfloat16)[None], span_end[None], request_states)


f32 = jnp.float32
bf16 = jnp.bfloat16
VMEM_LIMIT = 24 * 1024 * 1024
TILE = 256


def in_vmem():
    return pl.BlockSpec(memory_space=pltpu.VMEM)


def in_smem():
    return pl.BlockSpec(memory_space=pltpu.SMEM)


def takes(us):
    return pl.CostEstimate(
        flops=int(us * 1.15e9), bytes_accessed=int(us * 3.0e6), transcendentals=0
    )


def kernel_params():
    return pltpu.CompilerParams(vmem_limit_bytes=VMEM_LIMIT)


EXTRA = 16


def here_and_step(x_ref, is_long, period, tile):
    rows = x_ref.shape[1] - EXTRA
    here = x_ref[tile, 0:rows, :].astype(f32)
    above = x_ref[jnp.maximum(tile - 1, 0), rows - 16 : rows, :].astype(f32)[15:16]
    first = jnp.where(is_long == 1, x_ref[0, rows : rows + 16, :].astype(f32)[0:1], 0.0)
    row = lax.broadcasted_iota(jnp.int32, here.shape, 0)
    before = jnp.where(row == 0, above, pltpu.roll(here, 1, 0))
    start = ((row + tile * rows) & (period - 1)) == 0
    before = jnp.where(start, first, before)
    return here, before - here


def given_kernel(kind, extents, long_ref, short_ref, out_ref):
    rows = long_ref.shape[0]
    is_long = kind[0] == 1
    out_ref[0:rows, :] = jnp.where(is_long, short_ref[...], long_ref[...])
    lane = lax.broadcasted_iota(jnp.int32, (EXTRA, out_ref.shape[1]), 1)
    line = jnp.zeros(lane.shape, f32)
    for n in range(extents.shape[0]):
        line = jnp.where(lane == n, extents[n].astype(f32), line)
    out_ref[rows : rows + EXTRA, :] = line.astype(bf16)


def given_to_other_core(kind, extents, long_rows, short_rows):
    rows, columns = long_rows.shape
    return pl.pallas_call(
        given_kernel,
        out_shape=jax.ShapeDtypeStruct((rows + EXTRA, columns), bf16),
        in_specs=[in_smem()] * 2 + [in_vmem()] * 2,
        out_specs=in_vmem(),
        compiler_params=kernel_params(),
        cost_estimate=takes(1.5),
    )(kind, extents, long_rows, short_rows)


def block_kernel(kind, extents, long_ref, short_ref, taken, edge, out_ref):
    rows = long_ref.shape[0]
    depth = out_ref.shape[2]
    is_long = kind[0] == 1
    count = extents.shape[0]
    row = lax.broadcasted_iota(jnp.int32, (EXTRA, depth), 0)
    lane = lax.broadcasted_iota(jnp.int32, (EXTRA, depth), 1)
    other = taken[rows : rows + EXTRA, 0:depth].astype(f32)
    line = jnp.where(is_long, pltpu.roll(other, count, 1), other)
    own_at = jnp.where(is_long, 0, count)
    for n in range(count):
        line = jnp.where(lane == own_at + n, extents[n].astype(f32), line)
    for half in range(2):
        start = jnp.where(is_long, half, 1 - half) * depth
        at = pl.ds(pl.multiple_of(start, depth), depth)
        got = taken[0:rows, at]
        out_ref[half, 0:rows, :] = jnp.where(is_long, long_ref[:, at], got)
        out_ref[half, rows : 2 * rows, :] = jnp.where(is_long, got, short_ref[:, at])
        first = edge[:, at].astype(f32)
        out_ref[half, 2 * rows :, :] = jnp.where(row == 0, first, line).astype(bf16)


def block_of_chip(kind, extents, long_rows, short_rows, taken, edge):
    rows, columns = long_rows.shape
    return pl.pallas_call(
        block_kernel,
        out_shape=jax.ShapeDtypeStruct((2, 2 * rows + EXTRA, columns // 2), bf16),
        in_specs=[in_smem()] * 2 + [in_vmem()] * 4,
        out_specs=in_vmem(),
        compiler_params=kernel_params(),
        cost_estimate=takes(1.5),
    )(kind, extents, long_rows, short_rows, taken, edge)


def half_block(shape):
    return pl.BlockSpec((1,) + shape[1:], lambda i: (i,) + (0,) * (len(shape) - 1))


def gather_blocks(kind, own, rest, held):
    held[kind[6]] = own[...]
    for k in range(3):
        held[kind[7 + k]] = rest[k]


def keep_kv(half, which, at, value, kv_own, kv_sibling):
    @pl.when(half == 0)
    def _():
        kv_own[which, at, :] = value

    @pl.when(half == 1)
    def _():
        kv_sibling[which, at, :] = value


def mix_kernel(
    kind, own, rest, ratios, left, kv_own, kv_sibling, r_mix, gate_mix, squeezed, held
):
    gather_blocks(kind, own.at[0], rest.at[0], held)

    @pl.loop(0, held.shape[0], unroll=2)
    def _(tile):
        here, step = here_and_step(held, kind[0], kind[1], tile)
        at = pl.ds(pl.multiple_of(tile * TILE, TILE), TILE)

        def mix(which):
            return (here + ratios[0, which : which + 1, :] * step).astype(bf16)

        r_mix[0, at, :] = mix(0)
        for which in range(2):
            keep_kv(pl.program_id(0), which, at, mix(1 + which), kv_own, kv_sibling)
        gate_mix[0, at, :] = mix(3)
        squeezed[0, at, :] = jnp.dot(mix(4), left[0], preferred_element_type=f32)


def mixes_of(kind, own, rest, ratios, left):
    rows, depth = own.shape[1] - EXTRA, own.shape[2]
    lines = rest.shape[1] + 1
    whole = lines * rows
    outs = [
        jax.ShapeDtypeStruct((2, whole, depth), bf16),
        jax.ShapeDtypeStruct((2, whole, depth), bf16),
        jax.ShapeDtypeStruct((2, whole, depth), bf16),
        jax.ShapeDtypeStruct((2, whole, depth), bf16),
        jax.ShapeDtypeStruct((2, whole, left.shape[2]), f32),
    ]
    return pl.pallas_call(
        mix_kernel,
        grid=(2,),
        out_shape=outs,
        in_specs=[in_smem()] + [half_block(a.shape) for a in (own, rest, ratios, left)],
        out_specs=[pl.BlockSpec(outs[0].shape, lambda i: (0, 0, 0))] * 2
        + [half_block(out.shape) for out in outs[2:]],
        scratch_shapes=[pltpu.VMEM((lines, rows + EXTRA, depth), bf16)],
        compiler_params=kernel_params(),
        cost_estimate=takes(7),
    )(kind, own, rest, ratios, left)


def mix_project_kernel(rel, kind, own, rest, ratios, left, own_kv, *refs):
    earlier = refs[:-7]
    kv_sibling, r_mix, gate_mix, squeezed, keys_ref, values_ref, held = refs[-7:]
    half = pl.program_id(0)
    gather_blocks(kind, own.at[0], rest.at[0], held)

    @pl.loop(0, held.shape[0], unroll=2)
    def _(tile):
        here, step = here_and_step(held, kind[0], kind[1], tile)
        at = pl.ds(pl.multiple_of(tile * TILE, TILE), TILE)

        def mix(which):
            return (here + ratios[0, which : which + 1, :] * step).astype(bf16)

        r_mix[0, at, :] = mix(0)
        gate_mix[0, at, :] = mix(3)
        squeezed[0, at, :] = jnp.dot(mix(4), left[0], preferred_element_type=f32)

        @pl.when(half == 0)
        def _():
            for which, out in enumerate((keys_ref, values_ref)):
                part = jnp.dot(
                    mix(1 + which), own_kv[kind[10 + rel], which], preferred_element_type=f32
                )
                if len(earlier) == 1:
                    part = part + jnp.dot(
                        earlier[0][which, at, :],
                        own_kv[kind[10], which],
                        preferred_element_type=f32,
                    )
                else:
                    part = part + earlier[which][at, :]
                out[at, :] = part

        @pl.when(half == 1)
        def _():
            for which in range(2):
                kv_sibling[which, at, :] = mix(1 + which)


def mix_and_project(rel, kind, own, rest, ratios, left, own_kv, *earlier):
    rows, depth = own.shape[1] - EXTRA, own.shape[2]
    lines = rest.shape[1] + 1
    whole, width = lines * rows, own_kv.shape[3]
    kept = jax.ShapeDtypeStruct((2, whole, depth), bf16)
    outs = [
        jax.ShapeDtypeStruct((2, whole, depth), bf16),
        jax.ShapeDtypeStruct((2, whole, depth), bf16),
        jax.ShapeDtypeStruct((2, whole, left.shape[2]), f32),
    ]
    flat = jax.ShapeDtypeStruct((whole, width), f32)
    whole_of = pl.BlockSpec((whole, width), lambda i: (0, 0))
    return pl.pallas_call(
        lambda *refs: mix_project_kernel(rel, *refs),
        grid=(2,),
        out_shape=[kept] + outs + [flat] * 2,
        in_specs=[in_smem()]
        + [half_block(a.shape) for a in (own, rest, ratios, left)]
        + [in_vmem()] * (1 + len(earlier)),
        out_specs=[pl.BlockSpec(kept.shape, lambda i: (0, 0, 0))]
        + [half_block(out.shape) for out in outs]
        + [whole_of] * 2,
        scratch_shapes=[pltpu.VMEM((lines, rows + EXTRA, depth), bf16)],
        compiler_params=kernel_params(),
        cost_estimate=takes(6),
    )(kind, own, rest, ratios, left, own_kv, *earlier)


def project_kernel(
    kind,
    mix0,
    mix1,
    mix2,
    low0,
    low1,
    low2,
    keys_part,
    values_part,
    own0,
    own1,
    rest0,
    rest1,
    ratios,
    left,
    own_kv,
    sibling_kv,
    right,
    base,
    keys_ref,
    values_ref,
    decay_ref,
    r_mix,
    gate_mix,
    held,
):
    tile = pl.program_id(0)

    @pl.when(tile == 0)
    def _():
        for half, (own, rest) in enumerate(((own0, rest0), (own1, rest1))):
            gather_blocks(kind, own, rest, held.at[half])

    totals = [keys_part[...], values_part[...]]
    squeezed = low0[0] + low0[1] + low1[0] + low1[1] + low2[0] + low2[1]
    for half in range(2):
        here, step = here_and_step(held.at[half], kind[0], kind[1], tile)
        weight = (own_kv, sibling_kv)[half]

        def mix(which):
            return (here + ratios[half, which : which + 1, :] * step).astype(bf16)

        r_mix[half] = mix(0)
        gate_mix[half] = mix(3)
        for which in range(2):
            totals[which] += jnp.dot(
                mix(1 + which), weight[kind[13], which], preferred_element_type=f32
            )
        squeezed = squeezed + jnp.dot(mix(4), left[half], preferred_element_type=f32)
    for rel, mixes in enumerate((mix0, mix1, mix2)):
        for which in range(2):
            totals[which] += jnp.dot(
                mixes[which], sibling_kv[kind[10 + rel], which], preferred_element_type=f32
            )
    keys_ref[...] = totals[0]
    values_ref[...] = totals[1]
    squeezed = jnp.tanh(squeezed).astype(bf16)
    grown = jnp.dot(squeezed, right[...], preferred_element_type=f32)
    decay_ref[...] = -jnp.exp(base[...] + grown)


def projected(kind, mixes, lows, parts, owns, rests, *rest):
    rows, width = parts[0].shape
    rank, depth = lows[0].shape[2], owns[0].shape[1]
    flat = jax.ShapeDtypeStruct((rows, width), f32)
    wide = jax.ShapeDtypeStruct((2, rows, depth), bf16)
    tile_of = pl.BlockSpec((TILE, width), lambda i: (i, 0))
    wide_of = pl.BlockSpec((2, TILE, depth), lambda i: (0, i, 0))
    return pl.pallas_call(
        project_kernel,
        grid=(rows // TILE,),
        out_shape=[flat] * 3 + [wide] * 2,
        in_specs=[in_smem()]
        + [wide_of] * 3
        + [pl.BlockSpec((2, TILE, rank), lambda i: (0, i, 0))] * 3
        + [tile_of] * 2
        + [in_vmem()] * (4 + len(rest)),
        out_specs=[tile_of] * 3 + [wide_of] * 2,
        scratch_shapes=[pltpu.VMEM((2, rests[0].shape[0] + 1) + owns[0].shape, bf16)],
        compiler_params=kernel_params(),
        cost_estimate=takes(8),
    )(kind, *mixes, *lows, *parts, *owns, *rests, *rest)


def plain_kernel(kind, mix0, mix1, mix2, mix3, own, sibling, out_ref):
    half = pl.program_id(0)
    part = None
    for rel, mixes in enumerate((mix0, mix1, mix2, mix3)):
        weight = jnp.where(half == 0, own[kind[10 + rel], 0], sibling[kind[10 + rel], 0])
        new = jnp.dot(mixes[0], weight, preferred_element_type=f32)
        part = new if part is None else part + new

    @pl.when(half == 0)
    def _():
        out_ref[...] = part

    @pl.when(half == 1)
    def _():
        out_ref[...] += part


def plain_product(kind, mixes, own, sibling):
    rows, width = mixes[0].shape[1], own.shape[3]
    return pl.pallas_call(
        plain_kernel,
        grid=(2,),
        out_shape=jax.ShapeDtypeStruct((rows, width), f32),
        in_specs=[in_smem()] + [half_block(mix.shape) for mix in mixes] + [in_vmem()] * 2,
        out_specs=pl.BlockSpec((rows, width), lambda i: (0, 0)),
        compiler_params=kernel_params(),
        cost_estimate=takes(6),
    )(kind, *mixes, own, sibling)


def gate_kernel(
    kind,
    lengths,
    mix0,
    mix1,
    mix2,
    mix3,
    own,
    sibling,
    normed,
    kept0,
    sent0,
    kept1,
    sent1,
    total,
):
    half = pl.program_id(0)
    part = None
    for rel, mixes in enumerate((mix0, mix1, mix2, mix3)):
        weight = jnp.where(half == 0, own[kind[10 + rel], 0], sibling[kind[10 + rel], 0])
        new = jnp.dot(mixes[0], weight, preferred_element_type=f32)
        part = new if part is None else part + new

    @pl.when(half == 0)
    def _():
        total[...] = part

    @pl.when(half == 1)
    def _():
        gate = total[...] + part
        value = normed[...] * (gate * jax.nn.sigmoid(gate))
        row = lax.broadcasted_iota(jnp.int32, (BLK, value.shape[1]), 0)
        is_long = kind[0] == 1
        half_rows = BLK // 2

        def lived(n):
            block = value[n * BLK : (n + 1) * BLK]
            return jnp.where(row < lengths[n], block, 0.0).astype(bf16)

        for line in range(kept0.shape[1]):
            for block in range(2):
                even, odd = lived(4 * line + block), lived(4 * line + 2 + block)
                kept = jnp.where(is_long, even, odd)
                sent = jnp.where(is_long, odd, even)
                kept0[block, line] = kept[:half_rows]
                kept1[block, line] = kept[half_rows:]
                sent0[block, line] = sent[:half_rows]
                sent1[block, line] = sent[half_rows:]


def gated(kind, lengths, mixes, own, sibling, normed):
    rows, width = normed.shape
    quarter = jax.ShapeDtypeStruct((2, rows // TILE, BLK // 2, width), bf16)
    return pl.pallas_call(
        gate_kernel,
        grid=(2,),
        out_shape=[quarter] * 4,
        in_specs=[in_smem()] * 2 + [half_block(mix.shape) for mix in mixes] + [in_vmem()] * 3,
        out_specs=[pl.BlockSpec(quarter.shape, lambda i: (0, 0, 0, 0))] * 4,
        scratch_shapes=[pltpu.VMEM((rows, width), f32)],
        compiler_params=kernel_params(),
        cost_estimate=takes(7),
    )(kind, lengths, *mixes, own, sibling, normed)


def head_blocks(heads):
    width = heads * BLK
    tall = lax.broadcasted_iota(jnp.int32, (width, width), 0) // BLK
    wide = lax.broadcasted_iota(jnp.int32, (width, width), 1) // BLK
    return tall == wide


def state_kernel(lengths, carry, k_ref, v_ref, w_ref, s_ref, state_ref, entered_ref, hold):
    span, width = BLK, k_ref.shape[1]
    heads = width // span
    row = lax.broadcasted_iota(jnp.int32, (span, width), 0)
    lane = lax.broadcasted_iota(jnp.int32, (span, width), 1)
    for h in range(heads):
        hold[:, h * span : (h + 1) * span] = s_ref[h]

    @pl.loop(0, k_ref.shape[0] // span, unroll=8)
    def _(n):
        at = pl.ds(pl.multiple_of(n * span, span), span)
        live = row < lengths[n]
        k = jnp.where(live, k_ref[at, :], 0.0)
        total = jnp.where(live, w_ref[at, :], 0.0)
        after_row = jnp.zeros_like(total)
        half = 1
        while half < span:
            upper = (row & half) != 0
            across = jnp.where(
                upper, pltpu.roll(total, half, 0), pltpu.roll(total, span - half, 0)
            )
            after_row = after_row + jnp.where(upper, 0.0, across)
            total = total + across
            half *= 2
        added = lax.dot_general(
            (k * jnp.exp(after_row)).astype(bf16),
            v_ref[at, :].astype(bf16),
            (((0,), (0,)), ((), ())),
            preferred_element_type=f32,
        )
        fresh = jnp.zeros((span, width), f32)
        for h in range(heads):
            fresh = jnp.where(lane // span == h, added[h * span : (h + 1) * span], fresh)
        twice = jnp.concatenate([total] * 2, axis=0)
        turned_parts = []
        for p in range(width // (2 * span)):
            flipped = jnp.transpose(twice[:, p * 2 * span : (p + 1) * 2 * span])
            turned_parts.append(
                jnp.where(lane[:, : 2 * span] < span, flipped[:span], flipped[span:])
            )
        fade = jnp.exp(jnp.concatenate(turned_parts, axis=1))
        entered = hold[...] * carry[0]
        entered_ref[n] = entered.astype(bf16)
        state = fade * entered + fresh
        hold[...] = state
        for h in range(heads):
            state_ref[n, h] = state[:, h * span : (h + 1) * span]


def states_of(lengths, carry, k, v, w, state):
    rows, width = k.shape
    heads = width // BLK
    return pl.pallas_call(
        state_kernel,
        out_shape=[
            jax.ShapeDtypeStruct((rows // BLK, heads, BLK, BLK), f32),
            jax.ShapeDtypeStruct((rows // BLK, BLK, width), bf16),
        ],
        in_specs=[in_smem()] * 2 + [in_vmem()] * 4,
        out_specs=[in_vmem()] * 2,
        scratch_shapes=[pltpu.VMEM((BLK, width), f32)],
        compiler_params=kernel_params(),
        cost_estimate=takes(7),
    )(lengths, carry, k, v, w, state)


def sweep_kernel(lengths, r_ref, k_ref, v_ref, w_ref, entered_ref, u_ref, gain, bias, out_ref):
    span, width = BLK, r_ref.shape[1]
    heads = width // span
    row = lax.broadcasted_iota(jnp.int32, (span, width), 0)
    lane = lax.broadcasted_iota(jnp.int32, (span, width), 1)
    col = lane % span
    same_head = head_blocks(heads)

    def spread(value):
        stacked = jnp.concatenate([value.astype(bf16)] * heads, axis=0)
        return jnp.where(same_head, stacked, jnp.zeros_like(stacked))

    def against(a, b):
        return lax.dot_general(a, b, (((1,), (1,)), ((), ())), preferred_element_type=f32)

    @pl.loop(0, r_ref.shape[0] // span, unroll=4)
    def _(n):
        at = pl.ds(pl.multiple_of(n * span, span), span)
        live = row < lengths[n]
        r, v = r_ref[at, :], v_ref[at, :]
        k = jnp.where(live, k_ref[at, :], 0.0)
        total = jnp.where(live, w_ref[at, :], 0.0)
        before = jnp.zeros_like(total)
        after_row = jnp.zeros_like(total)
        scores = against((r * u_ref[...]).astype(bf16), spread(k))
        scores = jnp.where(row == col, scores, 0.0)
        level = 0
        while (1 << level) < span:
            half = 1 << level
            upper = (row & half) != 0
            if level:
                scale = jnp.exp(jnp.where(upper, before, after_row))
                part = against((r * scale).astype(bf16), spread(k * scale))
            else:
                part = against(r.astype(bf16), spread(k))
            pair = upper & (((row >> level) ^ (col >> level)) == 1)
            scores = jnp.where(pair, part, scores)
            across = jnp.where(
                upper, pltpu.roll(total, half, 0), pltpu.roll(total, span - half, 0)
            )
            before = before + jnp.where(upper, across, 0.0)
            after_row = after_row + jnp.where(upper, 0.0, across)
            total = total + across
            level += 1
        out = jnp.dot(scores.astype(bf16), spread(v), preferred_element_type=f32)
        out = out + jnp.dot(
            (r * jnp.exp(before)).astype(bf16),
            spread(entered_ref[n]),
            preferred_element_type=f32,
        )
        out_ref[at, :] = out

    ones = jnp.where(same_head, 1.0, 0.0).astype(bf16)

    def head_mean(value):
        high = value.astype(bf16)
        low = (value - high.astype(f32)).astype(bf16)
        both = jnp.dot(high, ones, preferred_element_type=f32) + jnp.dot(
            low, ones, preferred_element_type=f32
        )
        return both * (1.0 / span)

    @pl.loop(0, r_ref.shape[0] // TILE, unroll=2)
    def _(tile):
        at = pl.ds(pl.multiple_of(tile * TILE, TILE), TILE)
        value = out_ref[at, :]
        centred = value - head_mean(value)
        spread_of = head_mean(centred * centred)
        out_ref[at, :] = centred * lax.rsqrt(spread_of + norm_eps) * gain[...] + bias[...]


def sweep(lengths, r, k, v, w, entered, bonus, gain, bias):
    return pl.pallas_call(
        sweep_kernel,
        out_shape=jax.ShapeDtypeStruct(r.shape, f32),
        in_specs=[in_smem()] + [in_vmem()] * 8,
        out_specs=in_vmem(),
        compiler_params=kernel_params(),
        cost_estimate=takes(12),
    )(lengths, r, k, v, w, entered, bonus, gain, bias)


def final_kernel(block_of, h0, h1, h2, h3, weight, o0, o1, o2, o3, hold):
    @pl.loop(0, hold.shape[1] // TILE, unroll=2)
    def _(tile):
        at = pl.ds(pl.multiple_of(tile * TILE, TILE), TILE)
        total = None
        for k, piece in enumerate((h0, h1, h2, h3)):
            part = jnp.dot(piece[...], weight[k, :, at], preferred_element_type=f32)
            total = part if total is None else total + part
        hold[:, at] = total.astype(bf16)

    block = hold.shape[0] // 4
    for rel, out in enumerate((o0, o1, o2, o3)):
        at = pl.ds(pl.multiple_of(block_of[rel] * block, block), block)
        out[...] = hold[at, :].reshape(out.shape)


def final_product(block_of, pieces, weight, lines):
    rows, width = pieces[0].shape[0], weight.shape[2]
    out = jax.ShapeDtypeStruct((lines, rows // 4 // lines, width), bf16)
    return pl.pallas_call(
        final_kernel,
        out_shape=[out] * 4,
        in_specs=[in_smem()] + [in_vmem()] * 5,
        out_specs=[in_vmem()] * 4,
        scratch_shapes=[pltpu.VMEM((rows, width), bf16)],
        compiler_params=kernel_params(),
        cost_estimate=takes(4.5),
    )(block_of, *pieces, weight)


def lay_kernel(at, *refs):
    pieces, out_ref = refs[:-1], refs[-1]
    rows, width = pieces[0].shape
    lines = out_ref.shape[1] // width
    for n, piece in enumerate(pieces):
        column = pl.multiple_of(at[n % lines] * width, width)
        out_ref[n // lines * rows : (n // lines + 1) * rows, pl.ds(column, width)] = piece[...]


def laid(at, pieces, lines):
    rows, width = pieces[0].shape
    return pl.pallas_call(
        lay_kernel,
        out_shape=jax.ShapeDtypeStruct((len(pieces) // lines * rows, lines * width), bf16),
        in_specs=[in_smem()] + [in_vmem()] * len(pieces),
        out_specs=in_vmem(),
        compiler_params=kernel_params(),
        cost_estimate=takes(2),
    )(at, *pieces)


def after(value, *others):
    return lax.optimization_barrier((value,) + others)[0]


def turned(x, axis, by):
    length = lax.axis_size(axis)
    return lax.ppermute(x, axis, [(i, (i + by) % length) for i in range(length)])


def flipped_core(x):
    return lax.ppermute(x, "core", [(0, 1), (1, 0)])


def over_x(x):
    return lax.ppermute(x, "x", [(0, 1), (1, 0)])


def over_y(x):
    return lax.ppermute(x, "y", [(0, 1), (1, 0)])


def dealt(blocks, z):
    length = lax.axis_size("z")
    return [blocks(z)] + [turned(blocks((z + k) % length), "z", k) for k in range(1, length)]


def near_along(piece):
    two = turned(piece, "z", 2)
    one = lax.ppermute(piece, "z", [(0, 1), (1, 2), (2, 3)])
    three = lax.ppermute(piece, "z", [(1, 0), (2, 1), (3, 2)])
    return one, two, three


def far_along(two):
    return lax.ppermute(two, "z", [(1, 0), (2, 3)])


def spread_along(piece, z):
    one, two, three = near_along(piece)
    return piece, one, two, three, far_along(two)


def in_place(spread, z, at=0):
    piece, one, two, three, far = spread
    whole = jnp.zeros((4,) + piece.shape, piece.dtype)
    for k, part in ((1, one), (2, two), (3, three)):
        whole = lax.dynamic_update_index_in_dim(whole, part, (z - k) % 4, 0)
    far_at = jnp.where(z == 0, 3, jnp.where(z == 3, 0, z))
    whole = lax.dynamic_update_index_in_dim(whole, far, far_at, 0)
    return lax.dynamic_update_index_in_dim(whole, piece, z, 0)


def in_order(pieces, z):
    length = len(pieces)
    whole = jnp.zeros((length,) + pieces[0].shape, pieces[0].dtype)
    for k, piece in enumerate(pieces):
        whole = lax.dynamic_update_index_in_dim(whole, piece, (z - k) % length, 0)
    return whole


def on_core(
    continued_prompt_entries,
    padded_prompt_entries,
    prompt_live_extents,
    preceding_entry_line,
    carried_memory,
    token_mixing_ratios,
    acceptance_transform,
    lookup_transform,
    payload_transform,
    gating_transform,
    fading_baseline,
    fading_left_factor,
    fading_right_factor,
    present_reward,
    group_layer_scaling,
    group_layer_shift_term,
    final_transform,
):
    z, core = lax.axis_index("z"), lax.axis_index("core")
    y, x = lax.axis_index("y"), lax.axis_index("x")
    mp = 2 * y + x
    is_long = core == 0
    lines = lax.axis_size("z")
    group_rows, columns = continued_prompt_entries.shape
    requests = prompt_live_extents.shape[0]
    slot_rows = group_rows // requests
    heads, span = present_reward.shape
    heads = heads // lines
    width = heads * span
    depth = acceptance_transform.shape[0]
    rows = 2 * lines * group_rows

    kind = jnp.stack(
        [is_long.astype(jnp.int32), jnp.where(is_long, rows, slot_rows).astype(jnp.int32)]
        + [(mp ^ rel).astype(jnp.int32) for rel in range(4)]
        + [((z - k) % lines).astype(jnp.int32) for k in range(4)]
        + [((z - (mp ^ rel)) % lines).astype(jnp.int32) for rel in range(4)]
    )
    given = given_to_other_core(
        kind, prompt_live_extents, continued_prompt_entries, padded_prompt_entries
    )
    taken = flipped_core(given)
    block = block_of_chip(
        kind,
        prompt_live_extents,
        continued_prompt_entries,
        padded_prompt_entries,
        taken,
        preceding_entry_line[None],
    )
    (
        block,
        acceptance_transform,
        lookup_transform,
        payload_transform,
        gating_transform,
        final_transform,
        token_mixing_ratios,
        fading_left_factor,
        fading_right_factor,
        fading_baseline,
        present_reward,
        group_layer_scaling,
        group_layer_shift_term,
        carried_memory,
    ) = lax.optimization_barrier(
        (
            block,
            acceptance_transform,
            lookup_transform,
            payload_transform,
            gating_transform,
            final_transform,
            token_mixing_ratios,
            fading_left_factor,
            fading_right_factor,
            fading_baseline,
            present_reward,
            group_layer_scaling,
            group_layer_shift_term,
            carried_memory,
        )
    )
    one, two, three = near_along(block)
    own_x, own_y = over_x(block), over_y(block)
    one, two, three, own_x, own_y = lax.optimization_barrier((one, two, three, own_x, own_y))
    far = far_along(two)
    own_xy = (over_y(own_x[0]), over_x(own_y[1]))
    far, own_xy = lax.optimization_barrier((far, own_xy))
    rest = jnp.stack([jnp.where(z == 0, far, one), two, jnp.where(z == 3, far, three)], axis=1)
    rest_x, rest_y = over_x(rest), over_y(rest)
    extents = in_order(
        [part[2 * group_rows + 1, : 2 * requests] for part in (block[0],) + tuple(rest[0])], z
    ).reshape(2 * lines * requests)
    extents = jnp.where(is_long, slot_rows, extents.astype(jnp.int32)).astype(jnp.int32)

    def chunk_order(whole):
        split = whole.reshape((4, 2, depth) + whole.shape[1:])
        parts = []
        for rel in range(4):
            both = split[mp ^ rel]
            parts.append(jnp.where(is_long, both, both[::-1]))
        return parts

    ratios = [part.transpose(0, 2, 1) for part in chunk_order(token_mixing_ratios.T)]
    left = chunk_order(fading_left_factor)

    def columns_of(weights, *ready):
        stacked = jnp.stack(weights)
        blocks = [
            lax.dynamic_slice_in_dim(stacked, (z + k) % lines * width, width, 2)
            for k in range(lines)
        ]
        blocks = lax.optimization_barrier((tuple(blocks),) + ready)[0]
        return (blocks[0],) + tuple(turned(blocks[k], "z", k) for k in range(1, lines))

    def both_cores(pieces):
        own = jnp.stack(pieces)
        return own, flipped_core(own)

    kv_pieces = columns_of([lookup_transform, payload_transform], rest, own_xy)
    kv_pieces, rest_x, rest_y = lax.optimization_barrier((kv_pieces, rest_x, rest_y))
    rest_xy = (over_y(rest_x[0]), over_x(rest_y[1]))
    r_pieces = columns_of([acceptance_transform], rest_x, rest_y, kv_pieces)
    own_kv, sibling_kv = both_cores(kv_pieces)
    rest_xy, r_pieces = lax.optimization_barrier((rest_xy, r_pieces))
    gate_pieces = columns_of([gating_transform], r_pieces, rest_xy)
    own_r, sibling_r = both_cores(r_pieces)

    def mine_of(vector):
        return lax.dynamic_slice_in_dim(vector, z * width, width, 0)[None]

    kv_own, kv0, r0, gate0, low0 = mixes_of(kind, block, rest, ratios[0], left[0])
    kv1, r1, gate1, low1, *parts = mix_and_project(
        1, kind, own_x, rest_x, ratios[1], left[1], own_kv, kv_own
    )
    kv2, r2, gate2, low2, *parts = mix_and_project(
        2, kind, own_y, rest_y, ratios[2], left[2], own_kv, *parts
    )
    keys, values, decay, r3, gate3 = projected(
        kind,
        (kv0, kv1, kv2),
        (low0, low1, low2),
        parts,
        own_xy,
        rest_xy,
        ratios[3],
        left[3],
        own_kv,
        sibling_kv,
        lax.dynamic_slice_in_dim(fading_right_factor, z * width, width, 1),
        mine_of(fading_baseline),
    )
    entered = lax.dynamic_slice_in_dim(carried_memory, z * heads, heads, 0)
    bonus = lax.dynamic_slice_in_dim(present_reward, z * heads, heads, 0).reshape(1, width)
    states, states_in = states_of(
        extents,
        is_long.astype(f32)[None],
        keys,
        values,
        decay,
        jnp.where(is_long, entered, 0.0),
    )
    states = states.reshape(lines, 2, requests, heads, span, span)
    passed = flipped_core(lax.dynamic_index_in_dim(states, 1 - core, 1, keepdims=False))
    held = lax.dynamic_index_in_dim(states, core, 1, keepdims=False)
    bundle = jnp.concatenate(
        [jnp.where(is_long, held, passed)[:, -1:], jnp.where(is_long, passed, held)], axis=1
    ).astype(bf16)
    bundle = after(bundle, gate_pieces)
    r3 = after(r3, bundle)
    arrived = dealt(lambda j: lax.dynamic_index_in_dim(bundle, j, 0, keepdims=False), z)
    recept = plain_product(kind, (r0, r1, r2, r3), own_r, sibling_r)
    normed = sweep(
        extents,
        recept,
        keys,
        values,
        decay,
        states_in,
        bonus,
        mine_of(group_layer_scaling),
        mine_of(group_layer_shift_term),
    )
    own_gate, sibling_gate = both_cores(after(gate_pieces, states))
    normed, arrived = lax.optimization_barrier((normed, arrived))
    kept0, sent0, kept1, sent1 = gated(
        kind, extents, (gate0, gate1, gate2, gate3), own_gate, sibling_gate, normed
    )

    arrived = in_order(arrived, z).astype(f32)
    span_states = arrived[:, 0].reshape(1, lines * heads, span, span)
    request_states = jnp.swapaxes(arrived[:, 1:], 0, 1).reshape(
        requests, lines * heads, span, span
    )

    wide_out = 2 * final_transform.shape[1]
    beside = flipped_core(final_transform)
    out_weight = jnp.concatenate(
        [
            jnp.where(is_long, final_transform, beside),
            jnp.where(is_long, beside, final_transform),
        ],
        axis=1,
    ).reshape(lines, width, wide_out)
    out_weight = jnp.stack(
        [
            lax.dynamic_index_in_dim(out_weight, (z - k) % lines, 0, keepdims=False)
            for k in range(lines)
        ]
    )
    order = jnp.stack([(z - k) % lines for k in range(lines)]).astype(jnp.int32)
    block_of = jnp.stack(
        [(((y ^ (rel >> 1)) ^ core) * 2 + (x ^ (rel & 1))).astype(jnp.int32) for rel in range(4)]
    )
    spreads = []
    for kept, sent in ((kept0, sent0), (kept1, sent1)):
        part = jnp.concatenate([kept, flipped_core(sent)], axis=0)
        part = part.reshape(2 * rows // 4, width)
        if spreads:
            part = after(part, spreads[0][2])
        spreads.append(spread_along(part, z))
    out_pieces = []
    for piece, one, two, three, far in spreads:
        one = jnp.where(z == 0, far, one)
        three = jnp.where(z == 3, far, three)
        here, to_x, to_y, to_xy = final_product(
            block_of, (piece, one, two, three), out_weight, lines
        )
        across = lax.ppermute(to_xy, ("y", "x"), [(i, 3 - i) for i in range(4)])
        mixed_part = (
            here.astype(f32)
            + over_x(to_x).astype(f32)
            + over_y(to_y).astype(f32)
            + across.astype(f32)
        ).astype(bf16)
        out_pieces += dealt(
            lambda j: lax.dynamic_index_in_dim(mixed_part, j, 0, keepdims=False), z
        )
    mixed = laid(order, out_pieces, lines)[None]
    return mixed, span_states, request_states


def rows_kept_solution(mesh):
    placed = (
        P("seq", "mp"),
        P("seq", "mp"),
        P("seq"),
        P("mp"),
        P("mp", None, None),
        P(),
        P("seq", "mp"),
        P("seq", "mp"),
        P("seq", "mp"),
        P("seq", "mp"),
        P("mp"),
        P(),
        P(None, "mp"),
        P("mp", None),
        P("mp"),
        P("mp"),
        P("mp", "seq"),
    )
    return jax.shard_map(
        on_device,
        mesh=mesh,
        in_specs=placed,
        out_specs=(P("seq", "mp", None), P("seq", "mp", None, None), P("seq", "mp", None, None)),
        check_vma=False,
    )


def heads_kept_solution(mesh):
    seq, mp = mesh.shape["seq"], mesh.shape["mp"]
    split = Mesh(mesh.devices.reshape(seq // 2, 2, 2, mp // 2), ("z", "core", "y", "x"))
    s, m = ("z", "core"), ("y", "x")
    placed = (
        P(s, m),
        P(s, m),
        P(s),
        P(m),
        P(m, None, None),
        P(),
        P(s, m),
        P(s, m),
        P(s, m),
        P(s, m),
        P(m),
        P(),
        P(None, m),
        P(m, None),
        P(m),
        P(m),
        P(m, s),
    )
    return jax.shard_map(
        on_core,
        mesh=split,
        in_specs=placed,
        out_specs=(P(s, m, None), P(s, m, None, None), P(s, m, None, None)),
        check_vma=False,
    )


def solution(mesh):
    if mesh.shape["mp"] == 4 and mesh.shape["seq"] == 8:
        return heads_kept_solution(mesh)
    return rows_kept_solution(mesh)
```

```python
import jax
import jax.numpy as jnp
from jax import lax
from jax.experimental import pallas as pl
from jax.experimental.pallas import tpu as pltpu
from jax.sharding import Mesh
from jax.sharding import PartitionSpec as P

BLK = 64


norm_eps = 0.00064
highest = lax.Precision.HIGHEST


def passed_along(x, axis, by):
    length = lax.axis_size(axis)
    pairs = [(i, i + by) for i in range(length) if 0 <= i + by < length]
    return lax.ppermute(x, axis, pairs)


def entering(value, axis, join, neutral):
    count, mine = (lax.axis_size(axis), lax.axis_index(axis))
    pieces = jax.tree.map(lambda part: lax.all_gather(part, axis), value)
    total = jax.tree.map(
        lambda part, zero: jnp.full_like(part, 0) + jnp.asarray(zero, part.dtype), value, neutral
    )

    def hop(position, total):
        longer = join(total, jax.tree.map(lambda part: part[position], pieces))
        return jax.tree.map(lambda new, old: jnp.where(position < mine, new, old), longer, total)

    return lax.fori_loop(0, count - 1, hop, total)


def mix_rows(current, previous, weight):
    here = current.astype(jnp.float32)
    return (here + weight[None, :] * (previous.astype(jnp.float32) - here)).astype(jnp.bfloat16)


def block_sweep(
    evolving_memory,
    acceptance_entries,
    lookup_entries,
    payload_entries,
    log_fading_amount,
    diagonal_reward,
):
    inclusive = jnp.cumsum(log_fading_amount, axis=0)
    exclusive = inclusive - log_fading_amount
    recept_scaled = acceptance_entries * jnp.exp(exclusive)
    keys_scaled = lookup_entries * jnp.exp(-inclusive)
    scores = jnp.einsum("ihc,jhc->hij", recept_scaled, keys_scaled, precision=highest)
    count = acceptance_entries.shape[0]
    row_index = lax.broadcasted_iota(jnp.int32, (count, count), 0)
    col_index = lax.broadcasted_iota(jnp.int32, (count, count), 1)
    scores = jnp.where((row_index > col_index)[None], scores, 0.0)
    diagonal_contribution = jnp.sum(
        acceptance_entries * diagonal_reward[None] * lookup_entries, axis=-1, keepdims=True
    )
    answer_lines = (
        jnp.einsum("hij,jhd->ihd", scores, payload_entries, precision=highest)
        + diagonal_contribution * payload_entries
    )
    answer_lines = answer_lines + jnp.einsum(
        "ihc,hcd->ihd", recept_scaled, evolving_memory, precision=highest
    )
    total = inclusive[-1]
    carried = lookup_entries * jnp.exp(total[None] - inclusive)
    new_state = jnp.exp(total)[:, :, None] * evolving_memory + jnp.einsum(
        "jhc,jhd->hcd", carried, payload_entries, precision=highest
    )
    return (new_state, answer_lines)


def continued_recurrence(
    acceptance_entries, lookup_entries, payload_entries, log_fading_amount, diagonal_reward
):
    length, per_group_view, embedding_dimension = acceptance_entries.shape
    blocks = length // BLK

    def step(evolving_memory, entry_lines):
        return block_sweep(
            evolving_memory,
            entry_lines[0],
            entry_lines[1],
            entry_lines[2],
            entry_lines[3],
            diagonal_reward,
        )

    shaped = tuple(
        (
            a.reshape(blocks, BLK, per_group_view, embedding_dimension)
            for a in (acceptance_entries, lookup_entries, payload_entries, log_fading_amount)
        )
    )
    evolving_memory, results = lax.scan(
        step,
        jnp.zeros((per_group_view, embedding_dimension, embedding_dimension), jnp.float32),
        shaped,
    )
    return (evolving_memory, results.reshape(length, per_group_view, embedding_dimension))


def combine(earlier, later):
    return (earlier[0] + later[0], jnp.exp(later[0])[:, :, None] * earlier[1] + later[1])


def shifted_rows(current, edge_row, long_rows, requests, slot_rows):
    feature_part = current.shape[1]
    long_prev = jnp.concatenate([edge_row, current[: long_rows - 1]], axis=0)
    short_view = current[long_rows:].reshape(requests, slot_rows, feature_part)
    short_prev = jnp.concatenate(
        [jnp.zeros((requests, 1, feature_part), current.dtype), short_view[:, :-1]], axis=1
    )
    short_prev = short_prev.reshape(requests * slot_rows, feature_part)
    return jnp.concatenate([long_prev, short_prev], axis=0)


def on_device(
    continued_prompt_entries,
    padded_prompt_entries,
    prompt_live_extents,
    preceding_entry_line,
    carried_memory,
    token_mixing_ratios,
    acceptance_transform,
    lookup_transform,
    payload_transform,
    gating_transform,
    fading_baseline,
    fading_left_factor,
    fading_right_factor,
    present_reward,
    group_layer_scaling,
    group_layer_shift_term,
    final_transform,
):
    long_rows = continued_prompt_entries.shape[0]
    requests = prompt_live_extents.shape[0]
    slot_rows = padded_prompt_entries.shape[0] // requests
    per_group_view, embedding_dimension = present_reward.shape
    arrived = passed_along(continued_prompt_entries[-1:], "seq", 1)
    first = lax.axis_index("seq") == 0
    edge_row = jnp.where(first, preceding_entry_line[None, :], arrived)
    current = jnp.concatenate([continued_prompt_entries, padded_prompt_entries], axis=0)
    current, edge_full = (
        lax.all_gather(current, "mp", axis=1, tiled=True),
        lax.all_gather(edge_row, "mp", axis=1, tiled=True),
    )
    previous = shifted_rows(current, edge_full, long_rows, requests, slot_rows)
    mixes = [mix_rows(current, previous, token_mixing_ratios[index]) for index in range(5)]
    total_rows = current.shape[0]
    columns = acceptance_transform.shape[1]
    pieces = (
        lax.all_gather(acceptance_transform, "seq", axis=0, tiled=True),
        lax.all_gather(lookup_transform, "seq", axis=0, tiled=True),
        lax.all_gather(payload_transform, "seq", axis=0, tiled=True),
        lax.all_gather(gating_transform, "seq", axis=0, tiled=True),
    )
    acceptance_entries, lookup_entries, payload_entries, gate = tuple(
        (
            jnp.dot(source, piece, preferred_element_type=jnp.float32)
            for source, piece in zip(mixes[:4], pieces)
        )
    )
    squeezed = jnp.tanh(
        jnp.dot(mixes[4], fading_left_factor, preferred_element_type=jnp.float32)
    ).astype(jnp.bfloat16)
    log_fading_amount = -jnp.exp(
        fading_baseline[None, :]
        + jnp.dot(squeezed, fading_right_factor, preferred_element_type=jnp.float32)
    )
    recept3, keys3, values3, decay3 = [
        a.reshape(total_rows, per_group_view, embedding_dimension)
        for a in (acceptance_entries, lookup_entries, payload_entries, log_fading_amount)
    ]
    local_state, long_out = continued_recurrence(
        recept3[:long_rows],
        keys3[:long_rows],
        values3[:long_rows],
        decay3[:long_rows],
        present_reward,
    )
    long_decay = decay3[:long_rows]
    group_total = jnp.sum(long_decay, axis=0)
    blank = (
        jnp.zeros((per_group_view, embedding_dimension), jnp.float32),
        jnp.zeros((per_group_view, embedding_dimension, embedding_dimension), jnp.float32),
    )
    prefix_total, prefix_state = entering((group_total, local_state), "seq", combine, blank)
    incoming = jnp.exp(prefix_total)[:, :, None] * carried_memory + prefix_state
    before_row = jnp.cumsum(long_decay, axis=0) - long_decay
    long_out = long_out + jnp.einsum(
        "ihc,hcd->ihd", recept3[:long_rows] * jnp.exp(before_row), incoming, precision=highest
    )
    span_end = jnp.exp(group_total)[:, :, None] * incoming + local_state
    live_rows = (
        lax.broadcasted_iota(jnp.int32, (requests, slot_rows), 1) < prompt_live_extents[:, None]
    )
    live_flat = live_rows.reshape(requests * slot_rows).astype(jnp.float32)[:, None, None]
    short_shape = (requests, slot_rows, per_group_view, embedding_dimension)
    short_recept = recept3[long_rows:].reshape(short_shape)
    short_keys = (keys3[long_rows:] * live_flat).reshape(short_shape)
    short_values = values3[long_rows:].reshape(short_shape)
    short_decay = (decay3[long_rows:] * live_flat).reshape(short_shape)
    zeroed_memory = jnp.zeros(
        (per_group_view, embedding_dimension, embedding_dimension), jnp.float32
    )

    def request_pass(acceptance_lines, lookup_table, payload_table, fading_table):
        return block_sweep(
            zeroed_memory,
            acceptance_lines,
            lookup_table,
            payload_table,
            fading_table,
            present_reward,
        )

    request_states, short_out = jax.vmap(request_pass)(
        short_recept, short_keys, short_values, short_decay
    )
    wkv = jnp.concatenate(
        [long_out, short_out.reshape(requests * slot_rows, per_group_view, embedding_dimension)],
        axis=0,
    )
    mean = jnp.mean(wkv, axis=-1, keepdims=True)
    centred = wkv - mean
    variance = jnp.mean(centred * centred, axis=-1, keepdims=True)
    normed = (centred * lax.rsqrt(variance + norm_eps)).reshape(
        total_rows, columns
    ) * group_layer_scaling[None, :] + group_layer_shift_term[None, :]
    row_live = jnp.concatenate(
        [jnp.ones((long_rows,), dtype=bool), live_rows.reshape(requests * slot_rows)], axis=0
    )
    hidden = jnp.where(row_live[:, None], normed * jax.nn.silu(gate), 0.0).astype(jnp.bfloat16)
    full_out = lax.all_gather(final_transform, "seq", axis=1, tiled=True)
    mixed_rows = lax.psum_scatter(
        jnp.dot(hidden, full_out, preferred_element_type=jnp.float32),
        "mp",
        scatter_dimension=0,
        tiled=True,
    )
    return (mixed_rows.astype(jnp.bfloat16)[None], span_end[None], request_states)


f32 = jnp.float32
bf16 = jnp.bfloat16
VMEM_LIMIT = 24 * 1024 * 1024
TILE = 256


def in_vmem():
    return pl.BlockSpec(memory_space=pltpu.VMEM)


def in_smem():
    return pl.BlockSpec(memory_space=pltpu.SMEM)


def takes(us):
    return pl.CostEstimate(
        flops=int(us * 1.15e9), bytes_accessed=int(us * 3.0e6), transcendentals=0
    )


def kernel_params():
    return pltpu.CompilerParams(vmem_limit_bytes=VMEM_LIMIT)


EXTRA = 16


def here_and_step(x_ref, is_long, period, tile):
    rows = x_ref.shape[1] - EXTRA
    here = x_ref[tile, 0:rows, :].astype(f32)
    above = x_ref[jnp.maximum(tile - 1, 0), rows - 16 : rows, :].astype(f32)[15:16]
    first = jnp.where(is_long == 1, x_ref[0, rows : rows + 16, :].astype(f32)[0:1], 0.0)
    row = lax.broadcasted_iota(jnp.int32, here.shape, 0)
    before = jnp.where(row == 0, above, pltpu.roll(here, 1, 0))
    start = ((row + tile * rows) & (period - 1)) == 0
    before = jnp.where(start, first, before)
    return here, before - here


def given_kernel(kind, extents, long_ref, short_ref, out_ref):
    rows = long_ref.shape[0]
    is_long = kind[0] == 1
    out_ref[0:rows, :] = jnp.where(is_long, short_ref[...], long_ref[...])
    lane = lax.broadcasted_iota(jnp.int32, (EXTRA, out_ref.shape[1]), 1)
    line = jnp.zeros(lane.shape, f32)
    for n in range(extents.shape[0]):
        line = jnp.where(lane == n, extents[n].astype(f32), line)
    out_ref[rows : rows + EXTRA, :] = line.astype(bf16)


def given_to_other_core(kind, extents, long_rows, short_rows):
    rows, columns = long_rows.shape
    return pl.pallas_call(
        given_kernel,
        out_shape=jax.ShapeDtypeStruct((rows + EXTRA, columns), bf16),
        in_specs=[in_smem()] * 2 + [in_vmem()] * 2,
        out_specs=in_vmem(),
        compiler_params=kernel_params(),
        cost_estimate=takes(1.5),
    )(kind, extents, long_rows, short_rows)


def block_kernel(kind, extents, long_ref, short_ref, taken, edge, out_ref):
    rows = long_ref.shape[0]
    depth = out_ref.shape[2]
    is_long = kind[0] == 1
    count = extents.shape[0]
    row = lax.broadcasted_iota(jnp.int32, (EXTRA, depth), 0)
    lane = lax.broadcasted_iota(jnp.int32, (EXTRA, depth), 1)
    other = taken[rows : rows + EXTRA, 0:depth].astype(f32)
    line = jnp.where(is_long, pltpu.roll(other, count, 1), other)
    own_at = jnp.where(is_long, 0, count)
    for n in range(count):
        line = jnp.where(lane == own_at + n, extents[n].astype(f32), line)
    for half in range(2):
        start = jnp.where(is_long, half, 1 - half) * depth
        at = pl.ds(pl.multiple_of(start, depth), depth)
        got = taken[0:rows, at]
        out_ref[half, 0:rows, :] = jnp.where(is_long, long_ref[:, at], got)
        out_ref[half, rows : 2 * rows, :] = jnp.where(is_long, got, short_ref[:, at])
        first = edge[:, at].astype(f32)
        out_ref[half, 2 * rows :, :] = jnp.where(row == 0, first, line).astype(bf16)


def block_of_chip(kind, extents, long_rows, short_rows, taken, edge):
    rows, columns = long_rows.shape
    return pl.pallas_call(
        block_kernel,
        out_shape=jax.ShapeDtypeStruct((2, 2 * rows + EXTRA, columns // 2), bf16),
        in_specs=[in_smem()] * 2 + [in_vmem()] * 4,
        out_specs=in_vmem(),
        compiler_params=kernel_params(),
        cost_estimate=takes(1.5),
    )(kind, extents, long_rows, short_rows, taken, edge)


def half_block(shape):
    return pl.BlockSpec((1,) + shape[1:], lambda i: (i,) + (0,) * (len(shape) - 1))


def gather_blocks(kind, own, rest, held):
    held[kind[6]] = own[...]
    for k in range(3):
        held[kind[7 + k]] = rest[k]


def keep_kv(half, which, at, value, kv_own, kv_sibling):
    @pl.when(half == 0)
    def _():
        kv_own[which, at, :] = value

    @pl.when(half == 1)
    def _():
        kv_sibling[which, at, :] = value


def mix_kernel(
    kind, own, rest, ratios, left, kv_own, kv_sibling, r_mix, gate_mix, squeezed, held
):
    gather_blocks(kind, own.at[0], rest.at[0], held)

    @pl.loop(0, held.shape[0], unroll=2)
    def _(tile):
        here, step = here_and_step(held, kind[0], kind[1], tile)
        at = pl.ds(pl.multiple_of(tile * TILE, TILE), TILE)

        def mix(which):
            return (here + ratios[0, which : which + 1, :] * step).astype(bf16)

        r_mix[0, at, :] = mix(0)
        for which in range(2):
            keep_kv(pl.program_id(0), which, at, mix(1 + which), kv_own, kv_sibling)
        gate_mix[0, at, :] = mix(3)
        squeezed[0, at, :] = jnp.dot(mix(4), left[0], preferred_element_type=f32)


def mixes_of(kind, own, rest, ratios, left):
    rows, depth = own.shape[1] - EXTRA, own.shape[2]
    lines = rest.shape[1] + 1
    whole = lines * rows
    outs = [
        jax.ShapeDtypeStruct((2, whole, depth), bf16),
        jax.ShapeDtypeStruct((2, whole, depth), bf16),
        jax.ShapeDtypeStruct((2, whole, depth), bf16),
        jax.ShapeDtypeStruct((2, whole, depth), bf16),
        jax.ShapeDtypeStruct((2, whole, left.shape[2]), f32),
    ]
    return pl.pallas_call(
        mix_kernel,
        grid=(2,),
        out_shape=outs,
        in_specs=[in_smem()] + [half_block(a.shape) for a in (own, rest, ratios, left)],
        out_specs=[pl.BlockSpec(outs[0].shape, lambda i: (0, 0, 0))] * 2
        + [half_block(out.shape) for out in outs[2:]],
        scratch_shapes=[pltpu.VMEM((lines, rows + EXTRA, depth), bf16)],
        compiler_params=kernel_params(),
        cost_estimate=takes(7),
    )(kind, own, rest, ratios, left)


def mix_project_kernel(rel, kind, own, rest, ratios, left, own_kv, *refs):
    earlier = refs[:-7]
    kv_sibling, r_mix, gate_mix, squeezed, keys_ref, values_ref, held = refs[-7:]
    half = pl.program_id(0)
    gather_blocks(kind, own.at[0], rest.at[0], held)

    @pl.loop(0, held.shape[0], unroll=2)
    def _(tile):
        here, step = here_and_step(held, kind[0], kind[1], tile)
        at = pl.ds(pl.multiple_of(tile * TILE, TILE), TILE)

        def mix(which):
            return (here + ratios[0, which : which + 1, :] * step).astype(bf16)

        r_mix[0, at, :] = mix(0)
        gate_mix[0, at, :] = mix(3)
        squeezed[0, at, :] = jnp.dot(mix(4), left[0], preferred_element_type=f32)

        @pl.when(half == 0)
        def _():
            for which, out in enumerate((keys_ref, values_ref)):
                part = jnp.dot(
                    mix(1 + which), own_kv[kind[10 + rel], which], preferred_element_type=f32
                )
                if len(earlier) == 1:
                    part = part + jnp.dot(
                        earlier[0][which, at, :],
                        own_kv[kind[10], which],
                        preferred_element_type=f32,
                    )
                else:
                    part = part + earlier[which][at, :]
                out[at, :] = part

        @pl.when(half == 1)
        def _():
            for which in range(2):
                kv_sibling[which, at, :] = mix(1 + which)


def mix_and_project(rel, kind, own, rest, ratios, left, own_kv, *earlier):
    rows, depth = own.shape[1] - EXTRA, own.shape[2]
    lines = rest.shape[1] + 1
    whole, width = lines * rows, own_kv.shape[3]
    kept = jax.ShapeDtypeStruct((2, whole, depth), bf16)
    outs = [
        jax.ShapeDtypeStruct((2, whole, depth), bf16),
        jax.ShapeDtypeStruct((2, whole, depth), bf16),
        jax.ShapeDtypeStruct((2, whole, left.shape[2]), f32),
    ]
    flat = jax.ShapeDtypeStruct((whole, width), f32)
    whole_of = pl.BlockSpec((whole, width), lambda i: (0, 0))
    return pl.pallas_call(
        lambda *refs: mix_project_kernel(rel, *refs),
        grid=(2,),
        out_shape=[kept] + outs + [flat] * 2,
        in_specs=[in_smem()]
        + [half_block(a.shape) for a in (own, rest, ratios, left)]
        + [in_vmem()] * (1 + len(earlier)),
        out_specs=[pl.BlockSpec(kept.shape, lambda i: (0, 0, 0))]
        + [half_block(out.shape) for out in outs]
        + [whole_of] * 2,
        scratch_shapes=[pltpu.VMEM((lines, rows + EXTRA, depth), bf16)],
        compiler_params=kernel_params(),
        cost_estimate=takes(6),
    )(kind, own, rest, ratios, left, own_kv, *earlier)


def project_kernel(
    kind,
    mix0,
    mix1,
    mix2,
    low0,
    low1,
    low2,
    keys_part,
    values_part,
    own0,
    own1,
    rest0,
    rest1,
    ratios,
    left,
    own_kv,
    sibling_kv,
    right,
    base,
    keys_ref,
    values_ref,
    decay_ref,
    r_mix,
    gate_mix,
    held,
):
    tile = pl.program_id(0)

    @pl.when(tile == 0)
    def _():
        for half, (own, rest) in enumerate(((own0, rest0), (own1, rest1))):
            gather_blocks(kind, own, rest, held.at[half])

    totals = [keys_part[...], values_part[...]]
    squeezed = low0[0] + low0[1] + low1[0] + low1[1] + low2[0] + low2[1]
    for half in range(2):
        here, step = here_and_step(held.at[half], kind[0], kind[1], tile)
        weight = (own_kv, sibling_kv)[half]

        def mix(which):
            return (here + ratios[half, which : which + 1, :] * step).astype(bf16)

        r_mix[half] = mix(0)
        gate_mix[half] = mix(3)
        for which in range(2):
            totals[which] += jnp.dot(
                mix(1 + which), weight[kind[13], which], preferred_element_type=f32
            )
        squeezed = squeezed + jnp.dot(mix(4), left[half], preferred_element_type=f32)
    for rel, mixes in enumerate((mix0, mix1, mix2)):
        for which in range(2):
            totals[which] += jnp.dot(
                mixes[which], sibling_kv[kind[10 + rel], which], preferred_element_type=f32
            )
    keys_ref[...] = totals[0]
    values_ref[...] = totals[1]
    squeezed = jnp.tanh(squeezed).astype(bf16)
    grown = jnp.dot(squeezed, right[...], preferred_element_type=f32)
    decay_ref[...] = -jnp.exp(base[...] + grown)


def projected(kind, mixes, lows, parts, owns, rests, *rest):
    rows, width = parts[0].shape
    rank, depth = lows[0].shape[2], owns[0].shape[1]
    flat = jax.ShapeDtypeStruct((rows, width), f32)
    wide = jax.ShapeDtypeStruct((2, rows, depth), bf16)
    tile_of = pl.BlockSpec((TILE, width), lambda i: (i, 0))
    wide_of = pl.BlockSpec((2, TILE, depth), lambda i: (0, i, 0))
    return pl.pallas_call(
        project_kernel,
        grid=(rows // TILE,),
        out_shape=[flat] * 3 + [wide] * 2,
        in_specs=[in_smem()]
        + [wide_of] * 3
        + [pl.BlockSpec((2, TILE, rank), lambda i: (0, i, 0))] * 3
        + [tile_of] * 2
        + [in_vmem()] * (4 + len(rest)),
        out_specs=[tile_of] * 3 + [wide_of] * 2,
        scratch_shapes=[pltpu.VMEM((2, rests[0].shape[0] + 1) + owns[0].shape, bf16)],
        compiler_params=kernel_params(),
        cost_estimate=takes(8),
    )(kind, *mixes, *lows, *parts, *owns, *rests, *rest)


def plain_kernel(kind, mix0, mix1, mix2, mix3, own, sibling, out_ref):
    half = pl.program_id(0)
    part = None
    for rel, mixes in enumerate((mix0, mix1, mix2, mix3)):
        weight = jnp.where(half == 0, own[kind[10 + rel], 0], sibling[kind[10 + rel], 0])
        new = jnp.dot(mixes[0], weight, preferred_element_type=f32)
        part = new if part is None else part + new

    @pl.when(half == 0)
    def _():
        out_ref[...] = part

    @pl.when(half == 1)
    def _():
        out_ref[...] += part


def plain_product(kind, mixes, own, sibling):
    rows, width = mixes[0].shape[1], own.shape[3]
    return pl.pallas_call(
        plain_kernel,
        grid=(2,),
        out_shape=jax.ShapeDtypeStruct((rows, width), f32),
        in_specs=[in_smem()] + [half_block(mix.shape) for mix in mixes] + [in_vmem()] * 2,
        out_specs=pl.BlockSpec((rows, width), lambda i: (0, 0)),
        compiler_params=kernel_params(),
        cost_estimate=takes(6),
    )(kind, *mixes, own, sibling)


def gate_kernel(
    kind,
    lengths,
    mix0,
    mix1,
    mix2,
    mix3,
    own,
    sibling,
    normed,
    kept0,
    sent0,
    kept1,
    sent1,
    total,
):
    half = pl.program_id(0)
    part = None
    for rel, mixes in enumerate((mix0, mix1, mix2, mix3)):
        weight = jnp.where(half == 0, own[kind[10 + rel], 0], sibling[kind[10 + rel], 0])
        new = jnp.dot(mixes[0], weight, preferred_element_type=f32)
        part = new if part is None else part + new

    @pl.when(half == 0)
    def _():
        total[...] = part

    @pl.when(half == 1)
    def _():
        gate = total[...] + part
        value = normed[...] * (gate * jax.nn.sigmoid(gate))
        row = lax.broadcasted_iota(jnp.int32, (BLK, value.shape[1]), 0)
        is_long = kind[0] == 1
        half_rows = BLK // 2

        def lived(n):
            block = value[n * BLK : (n + 1) * BLK]
            return jnp.where(row < lengths[n], block, 0.0).astype(bf16)

        for line in range(kept0.shape[1]):
            for block in range(2):
                even, odd = lived(4 * line + block), lived(4 * line + 2 + block)
                kept = jnp.where(is_long, even, odd)
                sent = jnp.where(is_long, odd, even)
                kept0[block, line] = kept[:half_rows]
                kept1[block, line] = kept[half_rows:]
                sent0[block, line] = sent[:half_rows]
                sent1[block, line] = sent[half_rows:]


def gated(kind, lengths, mixes, own, sibling, normed):
    rows, width = normed.shape
    quarter = jax.ShapeDtypeStruct((2, rows // TILE, BLK // 2, width), bf16)
    return pl.pallas_call(
        gate_kernel,
        grid=(2,),
        out_shape=[quarter] * 4,
        in_specs=[in_smem()] * 2 + [half_block(mix.shape) for mix in mixes] + [in_vmem()] * 3,
        out_specs=[pl.BlockSpec(quarter.shape, lambda i: (0, 0, 0, 0))] * 4,
        scratch_shapes=[pltpu.VMEM((rows, width), f32)],
        compiler_params=kernel_params(),
        cost_estimate=takes(7),
    )(kind, lengths, *mixes, own, sibling, normed)


def head_blocks(heads):
    width = heads * BLK
    tall = lax.broadcasted_iota(jnp.int32, (width, width), 0) // BLK
    wide = lax.broadcasted_iota(jnp.int32, (width, width), 1) // BLK
    return tall == wide


def state_kernel(lengths, carry, k_ref, v_ref, w_ref, s_ref, state_ref, entered_ref, hold):
    span, width = BLK, k_ref.shape[1]
    heads = width // span
    row = lax.broadcasted_iota(jnp.int32, (span, width), 0)
    lane = lax.broadcasted_iota(jnp.int32, (span, width), 1)
    for h in range(heads):
        hold[:, h * span : (h + 1) * span] = s_ref[h]

    @pl.loop(0, k_ref.shape[0] // span, unroll=8)
    def _(n):
        at = pl.ds(pl.multiple_of(n * span, span), span)
        live = row < lengths[n]
        k = jnp.where(live, k_ref[at, :], 0.0)
        total = jnp.where(live, w_ref[at, :], 0.0)
        after_row = jnp.zeros_like(total)
        half = 1
        while half < span:
            upper = (row & half) != 0
            across = jnp.where(
                upper, pltpu.roll(total, half, 0), pltpu.roll(total, span - half, 0)
            )
            after_row = after_row + jnp.where(upper, 0.0, across)
            total = total + across
            half *= 2
        added = lax.dot_general(
            (k * jnp.exp(after_row)).astype(bf16),
            v_ref[at, :].astype(bf16),
            (((0,), (0,)), ((), ())),
            preferred_element_type=f32,
        )
        fresh = jnp.zeros((span, width), f32)
        for h in range(heads):
            fresh = jnp.where(lane // span == h, added[h * span : (h + 1) * span], fresh)
        twice = jnp.concatenate([total] * 2, axis=0)
        turned_parts = []
        for p in range(width // (2 * span)):
            flipped = jnp.transpose(twice[:, p * 2 * span : (p + 1) * 2 * span])
            turned_parts.append(
                jnp.where(lane[:, : 2 * span] < span, flipped[:span], flipped[span:])
            )
        fade = jnp.exp(jnp.concatenate(turned_parts, axis=1))
        entered = hold[...] * carry[0]
        entered_ref[n] = entered.astype(bf16)
        state = fade * entered + fresh
        hold[...] = state
        for h in range(heads):
            state_ref[n, h] = state[:, h * span : (h + 1) * span]


def states_of(lengths, carry, k, v, w, state):
    rows, width = k.shape
    heads = width // BLK
    return pl.pallas_call(
        state_kernel,
        out_shape=[
            jax.ShapeDtypeStruct((rows // BLK, heads, BLK, BLK), f32),
            jax.ShapeDtypeStruct((rows // BLK, BLK, width), bf16),
        ],
        in_specs=[in_smem()] * 2 + [in_vmem()] * 4,
        out_specs=[in_vmem()] * 2,
        scratch_shapes=[pltpu.VMEM((BLK, width), f32)],
        compiler_params=kernel_params(),
        cost_estimate=takes(7),
    )(lengths, carry, k, v, w, state)


def sweep_kernel(lengths, r_ref, k_ref, v_ref, w_ref, entered_ref, u_ref, gain, bias, out_ref):
    span, width = BLK, r_ref.shape[1]
    heads = width // span
    row = lax.broadcasted_iota(jnp.int32, (span, width), 0)
    lane = lax.broadcasted_iota(jnp.int32, (span, width), 1)
    col = lane % span
    same_head = head_blocks(heads)

    def spread(value):
        stacked = jnp.concatenate([value.astype(bf16)] * heads, axis=0)
        return jnp.where(same_head, stacked, jnp.zeros_like(stacked))

    def against(a, b):
        return lax.dot_general(a, b, (((1,), (1,)), ((), ())), preferred_element_type=f32)

    @pl.loop(0, r_ref.shape[0] // span, unroll=8)
    def _(n):
        at = pl.ds(pl.multiple_of(n * span, span), span)
        live = row < lengths[n]
        r, v = r_ref[at, :], v_ref[at, :]
        k = jnp.where(live, k_ref[at, :], 0.0)
        total = jnp.where(live, w_ref[at, :], 0.0)
        before = jnp.zeros_like(total)
        after_row = jnp.zeros_like(total)
        scores = against((r * u_ref[...]).astype(bf16), spread(k))
        scores = jnp.where(row == col, scores, 0.0)
        level = 0
        while (1 << level) < span:
            half = 1 << level
            upper = (row & half) != 0
            if level:
                scale = jnp.exp(jnp.where(upper, before, after_row))
                part = against((r * scale).astype(bf16), spread(k * scale))
            else:
                part = against(r.astype(bf16), spread(k))
            pair = upper & (((row >> level) ^ (col >> level)) == 1)
            scores = jnp.where(pair, part, scores)
            across = jnp.where(
                upper, pltpu.roll(total, half, 0), pltpu.roll(total, span - half, 0)
            )
            before = before + jnp.where(upper, across, 0.0)
            after_row = after_row + jnp.where(upper, 0.0, across)
            total = total + across
            level += 1
        out = jnp.dot(scores.astype(bf16), spread(v), preferred_element_type=f32)
        out = out + jnp.dot(
            (r * jnp.exp(before)).astype(bf16),
            spread(entered_ref[n]),
            preferred_element_type=f32,
        )
        out_ref[at, :] = out

    ones = jnp.where(same_head, 1.0, 0.0).astype(bf16)

    def head_mean(value):
        high = value.astype(bf16)
        low = (value - high.astype(f32)).astype(bf16)
        both = jnp.dot(high, ones, preferred_element_type=f32) + jnp.dot(
            low, ones, preferred_element_type=f32
        )
        return both * (1.0 / span)

    @pl.loop(0, r_ref.shape[0] // TILE, unroll=2)
    def _(tile):
        at = pl.ds(pl.multiple_of(tile * TILE, TILE), TILE)
        value = out_ref[at, :]
        centred = value - head_mean(value)
        spread_of = head_mean(centred * centred)
        out_ref[at, :] = centred * lax.rsqrt(spread_of + norm_eps) * gain[...] + bias[...]


def sweep(lengths, r, k, v, w, entered, bonus, gain, bias):
    return pl.pallas_call(
        sweep_kernel,
        out_shape=jax.ShapeDtypeStruct(r.shape, f32),
        in_specs=[in_smem()] + [in_vmem()] * 8,
        out_specs=in_vmem(),
        compiler_params=kernel_params(),
        cost_estimate=takes(12),
    )(lengths, r, k, v, w, entered, bonus, gain, bias)


def final_kernel(block_of, h0, h1, h2, h3, weight, o0, o1, o2, o3, hold):
    @pl.loop(0, hold.shape[1] // TILE, unroll=2)
    def _(tile):
        at = pl.ds(pl.multiple_of(tile * TILE, TILE), TILE)
        total = None
        for k, piece in enumerate((h0, h1, h2, h3)):
            part = jnp.dot(piece[...], weight[k, :, at], preferred_element_type=f32)
            total = part if total is None else total + part
        hold[:, at] = total.astype(bf16)

    block = hold.shape[0] // 4
    for rel, out in enumerate((o0, o1, o2, o3)):
        at = pl.ds(pl.multiple_of(block_of[rel] * block, block), block)
        out[...] = hold[at, :].reshape(out.shape)


def final_product(block_of, pieces, weight, lines):
    rows, width = pieces[0].shape[0], weight.shape[2]
    out = jax.ShapeDtypeStruct((lines, rows // 4 // lines, width), bf16)
    return pl.pallas_call(
        final_kernel,
        out_shape=[out] * 4,
        in_specs=[in_smem()] + [in_vmem()] * 5,
        out_specs=[in_vmem()] * 4,
        scratch_shapes=[pltpu.VMEM((rows, width), bf16)],
        compiler_params=kernel_params(),
        cost_estimate=takes(4.5),
    )(block_of, *pieces, weight)


def lay_kernel(at, *refs):
    pieces, out_ref = refs[:-1], refs[-1]
    rows, width = pieces[0].shape
    lines = out_ref.shape[1] // width
    for n, piece in enumerate(pieces):
        column = pl.multiple_of(at[n % lines] * width, width)
        out_ref[n // lines * rows : (n // lines + 1) * rows, pl.ds(column, width)] = piece[...]


def laid(at, pieces, lines):
    rows, width = pieces[0].shape
    return pl.pallas_call(
        lay_kernel,
        out_shape=jax.ShapeDtypeStruct((len(pieces) // lines * rows, lines * width), bf16),
        in_specs=[in_smem()] + [in_vmem()] * len(pieces),
        out_specs=in_vmem(),
        compiler_params=kernel_params(),
        cost_estimate=takes(2),
    )(at, *pieces)


def after(value, *others):
    return lax.optimization_barrier((value,) + others)[0]


def turned(x, axis, by):
    length = lax.axis_size(axis)
    return lax.ppermute(x, axis, [(i, (i + by) % length) for i in range(length)])


def flipped_core(x):
    return lax.ppermute(x, "core", [(0, 1), (1, 0)])


def over_x(x):
    return lax.ppermute(x, "x", [(0, 1), (1, 0)])


def over_y(x):
    return lax.ppermute(x, "y", [(0, 1), (1, 0)])


def dealt(blocks, z):
    length = lax.axis_size("z")
    return [blocks(z)] + [turned(blocks((z + k) % length), "z", k) for k in range(1, length)]


def near_along(piece):
    two = turned(piece, "z", 2)
    one = lax.ppermute(piece, "z", [(0, 1), (1, 2), (2, 3)])
    three = lax.ppermute(piece, "z", [(1, 0), (2, 1), (3, 2)])
    return one, two, three


def far_along(two):
    return lax.ppermute(two, "z", [(1, 0), (2, 3)])


def spread_along(piece, z):
    one, two, three = near_along(piece)
    return piece, one, two, three, far_along(two)


def in_place(spread, z, at=0):
    piece, one, two, three, far = spread
    whole = jnp.zeros((4,) + piece.shape, piece.dtype)
    for k, part in ((1, one), (2, two), (3, three)):
        whole = lax.dynamic_update_index_in_dim(whole, part, (z - k) % 4, 0)
    far_at = jnp.where(z == 0, 3, jnp.where(z == 3, 0, z))
    whole = lax.dynamic_update_index_in_dim(whole, far, far_at, 0)
    return lax.dynamic_update_index_in_dim(whole, piece, z, 0)


def in_order(pieces, z):
    length = len(pieces)
    whole = jnp.zeros((length,) + pieces[0].shape, pieces[0].dtype)
    for k, piece in enumerate(pieces):
        whole = lax.dynamic_update_index_in_dim(whole, piece, (z - k) % length, 0)
    return whole


def on_core(
    continued_prompt_entries,
    padded_prompt_entries,
    prompt_live_extents,
    preceding_entry_line,
    carried_memory,
    token_mixing_ratios,
    acceptance_transform,
    lookup_transform,
    payload_transform,
    gating_transform,
    fading_baseline,
    fading_left_factor,
    fading_right_factor,
    present_reward,
    group_layer_scaling,
    group_layer_shift_term,
    final_transform,
):
    z, core = lax.axis_index("z"), lax.axis_index("core")
    y, x = lax.axis_index("y"), lax.axis_index("x")
    mp = 2 * y + x
    is_long = core == 0
    lines = lax.axis_size("z")
    group_rows, columns = continued_prompt_entries.shape
    requests = prompt_live_extents.shape[0]
    slot_rows = group_rows // requests
    heads, span = present_reward.shape
    heads = heads // lines
    width = heads * span
    depth = acceptance_transform.shape[0]
    rows = 2 * lines * group_rows

    kind = jnp.stack(
        [is_long.astype(jnp.int32), jnp.where(is_long, rows, slot_rows).astype(jnp.int32)]
        + [(mp ^ rel).astype(jnp.int32) for rel in range(4)]
        + [((z - k) % lines).astype(jnp.int32) for k in range(4)]
        + [((z - (mp ^ rel)) % lines).astype(jnp.int32) for rel in range(4)]
    )
    given = given_to_other_core(
        kind, prompt_live_extents, continued_prompt_entries, padded_prompt_entries
    )
    taken = flipped_core(given)
    block = block_of_chip(
        kind,
        prompt_live_extents,
        continued_prompt_entries,
        padded_prompt_entries,
        taken,
        preceding_entry_line[None],
    )
    (
        block,
        acceptance_transform,
        lookup_transform,
        payload_transform,
        gating_transform,
        final_transform,
        token_mixing_ratios,
        fading_left_factor,
        fading_right_factor,
        fading_baseline,
        present_reward,
        group_layer_scaling,
        group_layer_shift_term,
        carried_memory,
    ) = lax.optimization_barrier(
        (
            block,
            acceptance_transform,
            lookup_transform,
            payload_transform,
            gating_transform,
            final_transform,
            token_mixing_ratios,
            fading_left_factor,
            fading_right_factor,
            fading_baseline,
            present_reward,
            group_layer_scaling,
            group_layer_shift_term,
            carried_memory,
        )
    )
    def blocks_of(*weights):
        stacked = jnp.stack(weights)
        return tuple(
            lax.dynamic_slice_in_dim(stacked, (z + k) % lines * width, width, 2)
            for k in range(lines)
        )

    def both_cores(pieces):
        own = jnp.stack(pieces)
        return own, flipped_core(own)

    kv = blocks_of(lookup_transform, payload_transform)
    r = blocks_of(acceptance_transform)
    gate = blocks_of(gating_transform)
    one, two, three = near_along(block)
    own_x, own_y = over_x(block), over_y(block)
    one, two, three, own_x, own_y, kv, r = lax.optimization_barrier(
        (one, two, three, own_x, own_y, kv, r)
    )
    far = far_along(two)
    own_xy = (over_y(own_x[0]), over_x(own_y[1]))
    kv_two = turned(kv[2], "z", 2)
    far, own_xy, kv, r = lax.optimization_barrier((far, own_xy, kv, r))
    rest = jnp.stack([jnp.where(z == 0, far, one), two, jnp.where(z == 3, far, three)], axis=1)
    rest_x, rest_y = over_x(rest), over_y(rest)
    extents = in_order(
        [part[2 * group_rows + 1, : 2 * requests] for part in (block[0],) + tuple(rest[0])], z
    ).reshape(2 * lines * requests)
    extents = jnp.where(is_long, slot_rows, extents.astype(jnp.int32)).astype(jnp.int32)

    def chunk_order(whole):
        split = whole.reshape((4, 2, depth) + whole.shape[1:])
        parts = []
        for rel in range(4):
            both = split[mp ^ rel]
            parts.append(jnp.where(is_long, both, both[::-1]))
        return parts

    ratios = [part.transpose(0, 2, 1) for part in chunk_order(token_mixing_ratios.T)]
    left = chunk_order(fading_left_factor)

    kv_one, kv_three = turned(kv[1], "z", 1), turned(kv[3], "z", 3)
    rest_x, rest_y, kv_one, kv_two, kv_three, r, gate = lax.optimization_barrier(
        (rest_x, rest_y, kv_one, kv_two, kv_three, r, gate)
    )
    rest_xy = (over_y(rest_x[0]), over_x(rest_y[1]))
    own_kv, sibling_kv = both_cores((kv[0], kv_one, kv_two, kv_three))
    r_one, r_two, r_three = (turned(r[k], "z", k) for k in range(1, lines))
    rest_xy, r_one, r_two, r_three, gate = lax.optimization_barrier(
        (rest_xy, r_one, r_two, r_three, gate)
    )
    gate_two = turned(gate[2], "z", 2)
    gate_pieces = (gate[0], turned(gate[1], "z", 1), gate_two, turned(gate[3], "z", 3))
    own_r, sibling_r = both_cores((r[0], r_one, r_two, r_three))

    def mine_of(vector):
        return lax.dynamic_slice_in_dim(vector, z * width, width, 0)[None]

    kv_own, kv0, r0, gate0, low0 = mixes_of(kind, block, rest, ratios[0], left[0])
    kv1, r1, gate1, low1, *parts = mix_and_project(
        1, kind, own_x, rest_x, ratios[1], left[1], own_kv, kv_own
    )
    kv2, r2, gate2, low2, *parts = mix_and_project(
        2, kind, own_y, rest_y, ratios[2], left[2], own_kv, *parts
    )
    keys, values, decay, r3, gate3 = projected(
        kind,
        (kv0, kv1, kv2),
        (low0, low1, low2),
        parts,
        own_xy,
        rest_xy,
        ratios[3],
        left[3],
        own_kv,
        sibling_kv,
        lax.dynamic_slice_in_dim(fading_right_factor, z * width, width, 1),
        mine_of(fading_baseline),
    )
    entered = lax.dynamic_slice_in_dim(carried_memory, z * heads, heads, 0)
    bonus = lax.dynamic_slice_in_dim(present_reward, z * heads, heads, 0).reshape(1, width)
    states, states_in = states_of(
        extents,
        is_long.astype(f32)[None],
        keys,
        values,
        decay,
        jnp.where(is_long, entered, 0.0),
    )
    states = states.reshape(lines, 2, requests, heads, span, span)
    passed = flipped_core(lax.dynamic_index_in_dim(states, 1 - core, 1, keepdims=False))
    held = lax.dynamic_index_in_dim(states, core, 1, keepdims=False)
    bundle = jnp.concatenate(
        [jnp.where(is_long, held, passed)[:, -1:], jnp.where(is_long, passed, held)], axis=1
    ).astype(bf16)
    bundle = after(bundle, gate_pieces)
    r3 = after(r3, bundle)
    arrived = dealt(lambda j: lax.dynamic_index_in_dim(bundle, j, 0, keepdims=False), z)
    recept = plain_product(kind, (r0, r1, r2, r3), own_r, sibling_r)
    normed = sweep(
        extents,
        recept,
        keys,
        values,
        decay,
        states_in,
        bonus,
        mine_of(group_layer_scaling),
        mine_of(group_layer_shift_term),
    )
    own_gate, sibling_gate = both_cores(after(gate_pieces, states))
    kept0, sent0, kept1, sent1 = gated(
        kind, extents, (gate0, gate1, gate2, gate3), own_gate, sibling_gate, normed
    )

    kept0, sent0, kept1, sent1, arrived = lax.optimization_barrier(
        (kept0, sent0, kept1, sent1, arrived)
    )
    arrived = in_order(arrived, z).astype(f32)
    span_states = arrived[:, 0].reshape(1, lines * heads, span, span)
    request_states = jnp.swapaxes(arrived[:, 1:], 0, 1).reshape(
        requests, lines * heads, span, span
    )

    wide_out = 2 * final_transform.shape[1]
    beside = flipped_core(final_transform)
    out_weight = jnp.concatenate(
        [
            jnp.where(is_long, final_transform, beside),
            jnp.where(is_long, beside, final_transform),
        ],
        axis=1,
    ).reshape(lines, width, wide_out)
    out_weight = jnp.stack(
        [
            lax.dynamic_index_in_dim(out_weight, (z - k) % lines, 0, keepdims=False)
            for k in range(lines)
        ]
    )
    order = jnp.stack([(z - k) % lines for k in range(lines)]).astype(jnp.int32)
    block_of = jnp.stack(
        [(((y ^ (rel >> 1)) ^ core) * 2 + (x ^ (rel & 1))).astype(jnp.int32) for rel in range(4)]
    )
    spreads = []
    for kept, sent in ((kept0, sent0), (kept1, sent1)):
        part = jnp.concatenate([kept, flipped_core(sent)], axis=0)
        part = part.reshape(2 * rows // 4, width)
        if spreads:
            part = after(part, spreads[0][2])
        spreads.append(spread_along(part, z))
    out_pieces = []
    for piece, one, two, three, far in spreads:
        one = jnp.where(z == 0, far, one)
        three = jnp.where(z == 3, far, three)
        here, to_x, to_y, to_xy = final_product(
            block_of, (piece, one, two, three), out_weight, lines
        )
        across = lax.ppermute(to_xy, ("y", "x"), [(i, 3 - i) for i in range(4)])
        mixed_part = (
            here.astype(f32)
            + over_x(to_x).astype(f32)
            + over_y(to_y).astype(f32)
            + across.astype(f32)
        ).astype(bf16)
        out_pieces += dealt(
            lambda j: lax.dynamic_index_in_dim(mixed_part, j, 0, keepdims=False), z
        )
    mixed = laid(order, out_pieces, lines)[None]
    return mixed, span_states, request_states


def rows_kept_solution(mesh):
    placed = (
        P("seq", "mp"),
        P("seq", "mp"),
        P("seq"),
        P("mp"),
        P("mp", None, None),
        P(),
        P("seq", "mp"),
        P("seq", "mp"),
        P("seq", "mp"),
        P("seq", "mp"),
        P("mp"),
        P(),
        P(None, "mp"),
        P("mp", None),
        P("mp"),
        P("mp"),
        P("mp", "seq"),
    )
    return jax.shard_map(
        on_device,
        mesh=mesh,
        in_specs=placed,
        out_specs=(P("seq", "mp", None), P("seq", "mp", None, None), P("seq", "mp", None, None)),
        check_vma=False,
    )


def heads_kept_solution(mesh):
    seq, mp = mesh.shape["seq"], mesh.shape["mp"]
    split = Mesh(mesh.devices.reshape(seq // 2, 2, 2, mp // 2), ("z", "core", "y", "x"))
    s, m = ("z", "core"), ("y", "x")
    placed = (
        P(s, m),
        P(s, m),
        P(s),
        P(m),
        P(m, None, None),
        P(),
        P(s, m),
        P(s, m),
        P(s, m),
        P(s, m),
        P(m),
        P(),
        P(None, m),
        P(m, None),
        P(m),
        P(m),
        P(m, s),
    )
    return jax.shard_map(
        on_core,
        mesh=split,
        in_specs=placed,
        out_specs=(P(s, m, None), P(s, m, None, None), P(s, m, None, None)),
        check_vma=False,
    )


def solution(mesh):
    if mesh.shape["mp"] == 4 and mesh.shape["seq"] == 8:
        return heads_kept_solution(mesh)
    return rows_kept_solution(mesh)
```

```python
import jax
import jax.numpy as jnp
from jax import lax
from jax.experimental import pallas as pl
from jax.experimental.pallas import tpu as pltpu
from jax.sharding import Mesh
from jax.sharding import PartitionSpec as P

BLK = 64


norm_eps = 0.00064
highest = lax.Precision.HIGHEST


def passed_along(x, axis, by):
    length = lax.axis_size(axis)
    pairs = [(i, i + by) for i in range(length) if 0 <= i + by < length]
    return lax.ppermute(x, axis, pairs)


def entering(value, axis, join, neutral):
    count, mine = (lax.axis_size(axis), lax.axis_index(axis))
    pieces = jax.tree.map(lambda part: lax.all_gather(part, axis), value)
    total = jax.tree.map(
        lambda part, zero: jnp.full_like(part, 0) + jnp.asarray(zero, part.dtype), value, neutral
    )

    def hop(position, total):
        longer = join(total, jax.tree.map(lambda part: part[position], pieces))
        return jax.tree.map(lambda new, old: jnp.where(position < mine, new, old), longer, total)

    return lax.fori_loop(0, count - 1, hop, total)


def mix_rows(current, previous, weight):
    here = current.astype(jnp.float32)
    return (here + weight[None, :] * (previous.astype(jnp.float32) - here)).astype(jnp.bfloat16)


def block_sweep(
    evolving_memory,
    acceptance_entries,
    lookup_entries,
    payload_entries,
    log_fading_amount,
    diagonal_reward,
):
    inclusive = jnp.cumsum(log_fading_amount, axis=0)
    exclusive = inclusive - log_fading_amount
    recept_scaled = acceptance_entries * jnp.exp(exclusive)
    keys_scaled = lookup_entries * jnp.exp(-inclusive)
    scores = jnp.einsum("ihc,jhc->hij", recept_scaled, keys_scaled, precision=highest)
    count = acceptance_entries.shape[0]
    row_index = lax.broadcasted_iota(jnp.int32, (count, count), 0)
    col_index = lax.broadcasted_iota(jnp.int32, (count, count), 1)
    scores = jnp.where((row_index > col_index)[None], scores, 0.0)
    diagonal_contribution = jnp.sum(
        acceptance_entries * diagonal_reward[None] * lookup_entries, axis=-1, keepdims=True
    )
    answer_lines = (
        jnp.einsum("hij,jhd->ihd", scores, payload_entries, precision=highest)
        + diagonal_contribution * payload_entries
    )
    answer_lines = answer_lines + jnp.einsum(
        "ihc,hcd->ihd", recept_scaled, evolving_memory, precision=highest
    )
    total = inclusive[-1]
    carried = lookup_entries * jnp.exp(total[None] - inclusive)
    new_state = jnp.exp(total)[:, :, None] * evolving_memory + jnp.einsum(
        "jhc,jhd->hcd", carried, payload_entries, precision=highest
    )
    return (new_state, answer_lines)


def continued_recurrence(
    acceptance_entries, lookup_entries, payload_entries, log_fading_amount, diagonal_reward
):
    length, per_group_view, embedding_dimension = acceptance_entries.shape
    blocks = length // BLK

    def step(evolving_memory, entry_lines):
        return block_sweep(
            evolving_memory,
            entry_lines[0],
            entry_lines[1],
            entry_lines[2],
            entry_lines[3],
            diagonal_reward,
        )

    shaped = tuple(
        (
            a.reshape(blocks, BLK, per_group_view, embedding_dimension)
            for a in (acceptance_entries, lookup_entries, payload_entries, log_fading_amount)
        )
    )
    evolving_memory, results = lax.scan(
        step,
        jnp.zeros((per_group_view, embedding_dimension, embedding_dimension), jnp.float32),
        shaped,
    )
    return (evolving_memory, results.reshape(length, per_group_view, embedding_dimension))


def combine(earlier, later):
    return (earlier[0] + later[0], jnp.exp(later[0])[:, :, None] * earlier[1] + later[1])


def shifted_rows(current, edge_row, long_rows, requests, slot_rows):
    feature_part = current.shape[1]
    long_prev = jnp.concatenate([edge_row, current[: long_rows - 1]], axis=0)
    short_view = current[long_rows:].reshape(requests, slot_rows, feature_part)
    short_prev = jnp.concatenate(
        [jnp.zeros((requests, 1, feature_part), current.dtype), short_view[:, :-1]], axis=1
    )
    short_prev = short_prev.reshape(requests * slot_rows, feature_part)
    return jnp.concatenate([long_prev, short_prev], axis=0)


def on_device(
    continued_prompt_entries,
    padded_prompt_entries,
    prompt_live_extents,
    preceding_entry_line,
    carried_memory,
    token_mixing_ratios,
    acceptance_transform,
    lookup_transform,
    payload_transform,
    gating_transform,
    fading_baseline,
    fading_left_factor,
    fading_right_factor,
    present_reward,
    group_layer_scaling,
    group_layer_shift_term,
    final_transform,
):
    long_rows = continued_prompt_entries.shape[0]
    requests = prompt_live_extents.shape[0]
    slot_rows = padded_prompt_entries.shape[0] // requests
    per_group_view, embedding_dimension = present_reward.shape
    arrived = passed_along(continued_prompt_entries[-1:], "seq", 1)
    first = lax.axis_index("seq") == 0
    edge_row = jnp.where(first, preceding_entry_line[None, :], arrived)
    current = jnp.concatenate([continued_prompt_entries, padded_prompt_entries], axis=0)
    current, edge_full = (
        lax.all_gather(current, "mp", axis=1, tiled=True),
        lax.all_gather(edge_row, "mp", axis=1, tiled=True),
    )
    previous = shifted_rows(current, edge_full, long_rows, requests, slot_rows)
    mixes = [mix_rows(current, previous, token_mixing_ratios[index]) for index in range(5)]
    total_rows = current.shape[0]
    columns = acceptance_transform.shape[1]
    pieces = (
        lax.all_gather(acceptance_transform, "seq", axis=0, tiled=True),
        lax.all_gather(lookup_transform, "seq", axis=0, tiled=True),
        lax.all_gather(payload_transform, "seq", axis=0, tiled=True),
        lax.all_gather(gating_transform, "seq", axis=0, tiled=True),
    )
    acceptance_entries, lookup_entries, payload_entries, gate = tuple(
        (
            jnp.dot(source, piece, preferred_element_type=jnp.float32)
            for source, piece in zip(mixes[:4], pieces)
        )
    )
    squeezed = jnp.tanh(
        jnp.dot(mixes[4], fading_left_factor, preferred_element_type=jnp.float32)
    ).astype(jnp.bfloat16)
    log_fading_amount = -jnp.exp(
        fading_baseline[None, :]
        + jnp.dot(squeezed, fading_right_factor, preferred_element_type=jnp.float32)
    )
    recept3, keys3, values3, decay3 = [
        a.reshape(total_rows, per_group_view, embedding_dimension)
        for a in (acceptance_entries, lookup_entries, payload_entries, log_fading_amount)
    ]
    local_state, long_out = continued_recurrence(
        recept3[:long_rows],
        keys3[:long_rows],
        values3[:long_rows],
        decay3[:long_rows],
        present_reward,
    )
    long_decay = decay3[:long_rows]
    group_total = jnp.sum(long_decay, axis=0)
    blank = (
        jnp.zeros((per_group_view, embedding_dimension), jnp.float32),
        jnp.zeros((per_group_view, embedding_dimension, embedding_dimension), jnp.float32),
    )
    prefix_total, prefix_state = entering((group_total, local_state), "seq", combine, blank)
    incoming = jnp.exp(prefix_total)[:, :, None] * carried_memory + prefix_state
    before_row = jnp.cumsum(long_decay, axis=0) - long_decay
    long_out = long_out + jnp.einsum(
        "ihc,hcd->ihd", recept3[:long_rows] * jnp.exp(before_row), incoming, precision=highest
    )
    span_end = jnp.exp(group_total)[:, :, None] * incoming + local_state
    live_rows = (
        lax.broadcasted_iota(jnp.int32, (requests, slot_rows), 1) < prompt_live_extents[:, None]
    )
    live_flat = live_rows.reshape(requests * slot_rows).astype(jnp.float32)[:, None, None]
    short_shape = (requests, slot_rows, per_group_view, embedding_dimension)
    short_recept = recept3[long_rows:].reshape(short_shape)
    short_keys = (keys3[long_rows:] * live_flat).reshape(short_shape)
    short_values = values3[long_rows:].reshape(short_shape)
    short_decay = (decay3[long_rows:] * live_flat).reshape(short_shape)
    zeroed_memory = jnp.zeros(
        (per_group_view, embedding_dimension, embedding_dimension), jnp.float32
    )

    def request_pass(acceptance_lines, lookup_table, payload_table, fading_table):
        return block_sweep(
            zeroed_memory,
            acceptance_lines,
            lookup_table,
            payload_table,
            fading_table,
            present_reward,
        )

    request_states, short_out = jax.vmap(request_pass)(
        short_recept, short_keys, short_values, short_decay
    )
    wkv = jnp.concatenate(
        [long_out, short_out.reshape(requests * slot_rows, per_group_view, embedding_dimension)],
        axis=0,
    )
    mean = jnp.mean(wkv, axis=-1, keepdims=True)
    centred = wkv - mean
    variance = jnp.mean(centred * centred, axis=-1, keepdims=True)
    normed = (centred * lax.rsqrt(variance + norm_eps)).reshape(
        total_rows, columns
    ) * group_layer_scaling[None, :] + group_layer_shift_term[None, :]
    row_live = jnp.concatenate(
        [jnp.ones((long_rows,), dtype=bool), live_rows.reshape(requests * slot_rows)], axis=0
    )
    hidden = jnp.where(row_live[:, None], normed * jax.nn.silu(gate), 0.0).astype(jnp.bfloat16)
    full_out = lax.all_gather(final_transform, "seq", axis=1, tiled=True)
    mixed_rows = lax.psum_scatter(
        jnp.dot(hidden, full_out, preferred_element_type=jnp.float32),
        "mp",
        scatter_dimension=0,
        tiled=True,
    )
    return (mixed_rows.astype(jnp.bfloat16)[None], span_end[None], request_states)


f32 = jnp.float32
bf16 = jnp.bfloat16
VMEM_LIMIT = 24 * 1024 * 1024
TILE = 256


def in_vmem():
    return pl.BlockSpec(memory_space=pltpu.VMEM)


def in_smem():
    return pl.BlockSpec(memory_space=pltpu.SMEM)


def takes(us):
    return pl.CostEstimate(
        flops=int(us * 2.3e9), bytes_accessed=int(us * 6.0e6), transcendentals=0
    )


def kernel_params():
    return pltpu.CompilerParams(vmem_limit_bytes=VMEM_LIMIT)


EXTRA = 16


def here_and_step(x_ref, is_long, period, tile):
    rows = x_ref.shape[1] - EXTRA
    here = x_ref[tile, 0:rows, :].astype(f32)
    above = x_ref[jnp.maximum(tile - 1, 0), rows - 16 : rows, :].astype(f32)[15:16]
    first = jnp.where(is_long == 1, x_ref[0, rows : rows + 16, :].astype(f32)[0:1], 0.0)
    row = lax.broadcasted_iota(jnp.int32, here.shape, 0)
    before = jnp.where(row == 0, above, pltpu.roll(here, 1, 0))
    start = ((row + tile * rows) & (period - 1)) == 0
    before = jnp.where(start, first, before)
    return here, before - here


def given_kernel(kind, extents, long_ref, short_ref, out_ref):
    rows = long_ref.shape[0]
    is_long = kind[0] == 1
    out_ref[0:rows, :] = jnp.where(is_long, short_ref[...], long_ref[...])
    lane = lax.broadcasted_iota(jnp.int32, (EXTRA, out_ref.shape[1]), 1)
    line = jnp.zeros(lane.shape, f32)
    for n in range(extents.shape[0]):
        line = jnp.where(lane == n, extents[n].astype(f32), line)
    out_ref[rows : rows + EXTRA, :] = line.astype(bf16)


def given_to_other_core(kind, extents, long_rows, short_rows):
    rows, columns = long_rows.shape
    return pl.pallas_call(
        given_kernel,
        out_shape=jax.ShapeDtypeStruct((rows + EXTRA, columns), bf16),
        in_specs=[in_smem()] * 2 + [in_vmem()] * 2,
        out_specs=in_vmem(),
        compiler_params=kernel_params(),
        cost_estimate=takes(1.5),
    )(kind, extents, long_rows, short_rows)


def block_kernel(kind, extents, long_ref, short_ref, taken, edge, out_ref):
    rows = long_ref.shape[0]
    depth = out_ref.shape[2]
    is_long = kind[0] == 1
    count = extents.shape[0]
    row = lax.broadcasted_iota(jnp.int32, (EXTRA, depth), 0)
    lane = lax.broadcasted_iota(jnp.int32, (EXTRA, depth), 1)
    other = taken[rows : rows + EXTRA, 0:depth].astype(f32)
    line = jnp.where(is_long, pltpu.roll(other, count, 1), other)
    own_at = jnp.where(is_long, 0, count)
    for n in range(count):
        line = jnp.where(lane == own_at + n, extents[n].astype(f32), line)
    for half in range(2):
        start = jnp.where(is_long, half, 1 - half) * depth
        at = pl.ds(pl.multiple_of(start, depth), depth)
        got = taken[0:rows, at]
        out_ref[half, 0:rows, :] = jnp.where(is_long, long_ref[:, at], got)
        out_ref[half, rows : 2 * rows, :] = jnp.where(is_long, got, short_ref[:, at])
        first = edge[:, at].astype(f32)
        out_ref[half, 2 * rows :, :] = jnp.where(row == 0, first, line).astype(bf16)


def block_of_chip(kind, extents, long_rows, short_rows, taken, edge):
    rows, columns = long_rows.shape
    return pl.pallas_call(
        block_kernel,
        out_shape=jax.ShapeDtypeStruct((2, 2 * rows + EXTRA, columns // 2), bf16),
        in_specs=[in_smem()] * 2 + [in_vmem()] * 4,
        out_specs=in_vmem(),
        compiler_params=kernel_params(),
        cost_estimate=takes(1.5),
    )(kind, extents, long_rows, short_rows, taken, edge)


def half_block(shape):
    return pl.BlockSpec((1,) + shape[1:], lambda i: (i,) + (0,) * (len(shape) - 1))


def gather_blocks(kind, own, rest, held):
    held[kind[6]] = own[...]
    for k in range(3):
        held[kind[7 + k]] = rest[k]


def keep_kv(half, which, at, value, kv_own, kv_sibling):
    @pl.when(half == 0)
    def _():
        kv_own[which, at, :] = value

    @pl.when(half == 1)
    def _():
        kv_sibling[which, at, :] = value


def mix_kernel(
    kind, own, rest, ratios, left, kv_own, kv_sibling, r_mix, gate_mix, squeezed, held
):
    gather_blocks(kind, own.at[0], rest.at[0], held)

    @pl.loop(0, held.shape[0], unroll=2)
    def _(tile):
        here, step = here_and_step(held, kind[0], kind[1], tile)
        at = pl.ds(pl.multiple_of(tile * TILE, TILE), TILE)

        def mix(which):
            return (here + ratios[0, which : which + 1, :] * step).astype(bf16)

        r_mix[0, at, :] = mix(0)
        for which in range(2):
            keep_kv(pl.program_id(0), which, at, mix(1 + which), kv_own, kv_sibling)
        gate_mix[0, at, :] = mix(3)
        squeezed[0, at, :] = jnp.dot(mix(4), left[0], preferred_element_type=f32)


def mixes_of(kind, own, rest, ratios, left):
    rows, depth = own.shape[1] - EXTRA, own.shape[2]
    lines = rest.shape[1] + 1
    whole = lines * rows
    outs = [
        jax.ShapeDtypeStruct((2, whole, depth), bf16),
        jax.ShapeDtypeStruct((2, whole, depth), bf16),
        jax.ShapeDtypeStruct((2, whole, depth), bf16),
        jax.ShapeDtypeStruct((2, whole, depth), bf16),
        jax.ShapeDtypeStruct((2, whole, left.shape[2]), f32),
    ]
    return pl.pallas_call(
        mix_kernel,
        grid=(2,),
        out_shape=outs,
        in_specs=[in_smem()] + [half_block(a.shape) for a in (own, rest, ratios, left)],
        out_specs=[pl.BlockSpec(outs[0].shape, lambda i: (0, 0, 0))] * 2
        + [half_block(out.shape) for out in outs[2:]],
        scratch_shapes=[pltpu.VMEM((lines, rows + EXTRA, depth), bf16)],
        compiler_params=kernel_params(),
        cost_estimate=takes(7),
    )(kind, own, rest, ratios, left)


def mix_project_kernel(rel, kind, own, rest, ratios, left, own_kv, *refs):
    earlier = refs[:-7]
    kv_sibling, r_mix, gate_mix, squeezed, keys_ref, values_ref, held = refs[-7:]
    half = pl.program_id(0)
    gather_blocks(kind, own.at[0], rest.at[0], held)

    @pl.loop(0, held.shape[0], unroll=2)
    def _(tile):
        here, step = here_and_step(held, kind[0], kind[1], tile)
        at = pl.ds(pl.multiple_of(tile * TILE, TILE), TILE)

        def mix(which):
            return (here + ratios[0, which : which + 1, :] * step).astype(bf16)

        r_mix[0, at, :] = mix(0)
        gate_mix[0, at, :] = mix(3)
        squeezed[0, at, :] = jnp.dot(mix(4), left[0], preferred_element_type=f32)

        @pl.when(half == 0)
        def _():
            for which, out in enumerate((keys_ref, values_ref)):
                part = jnp.dot(
                    mix(1 + which), own_kv[kind[10 + rel], which], preferred_element_type=f32
                )
                if len(earlier) == 1:
                    part = part + jnp.dot(
                        earlier[0][which, at, :],
                        own_kv[kind[10], which],
                        preferred_element_type=f32,
                    )
                else:
                    part = part + earlier[which][at, :]
                out[at, :] = part

        @pl.when(half == 1)
        def _():
            for which in range(2):
                kv_sibling[which, at, :] = mix(1 + which)


def mix_and_project(rel, kind, own, rest, ratios, left, own_kv, *earlier):
    rows, depth = own.shape[1] - EXTRA, own.shape[2]
    lines = rest.shape[1] + 1
    whole, width = lines * rows, own_kv.shape[3]
    kept = jax.ShapeDtypeStruct((2, whole, depth), bf16)
    outs = [
        jax.ShapeDtypeStruct((2, whole, depth), bf16),
        jax.ShapeDtypeStruct((2, whole, depth), bf16),
        jax.ShapeDtypeStruct((2, whole, left.shape[2]), f32),
    ]
    flat = jax.ShapeDtypeStruct((whole, width), f32)
    whole_of = pl.BlockSpec((whole, width), lambda i: (0, 0))
    return pl.pallas_call(
        lambda *refs: mix_project_kernel(rel, *refs),
        grid=(2,),
        out_shape=[kept] + outs + [flat] * 2,
        in_specs=[in_smem()]
        + [half_block(a.shape) for a in (own, rest, ratios, left)]
        + [in_vmem()] * (1 + len(earlier)),
        out_specs=[pl.BlockSpec(kept.shape, lambda i: (0, 0, 0))]
        + [half_block(out.shape) for out in outs]
        + [whole_of] * 2,
        scratch_shapes=[pltpu.VMEM((lines, rows + EXTRA, depth), bf16)],
        compiler_params=kernel_params(),
        cost_estimate=takes(6),
    )(kind, own, rest, ratios, left, own_kv, *earlier)


def project_kernel(
    kind,
    mix0,
    mix1,
    mix2,
    low0,
    low1,
    low2,
    keys_part,
    values_part,
    own0,
    own1,
    rest0,
    rest1,
    ratios,
    left,
    own_kv,
    sibling_kv,
    right,
    base,
    keys_ref,
    values_ref,
    decay_ref,
    r_mix,
    gate_mix,
    held,
):
    tile = pl.program_id(0)

    @pl.when(tile == 0)
    def _():
        for half, (own, rest) in enumerate(((own0, rest0), (own1, rest1))):
            gather_blocks(kind, own, rest, held.at[half])

    totals = [keys_part[...], values_part[...]]
    squeezed = low0[0] + low0[1] + low1[0] + low1[1] + low2[0] + low2[1]
    for half in range(2):
        here, step = here_and_step(held.at[half], kind[0], kind[1], tile)
        weight = (own_kv, sibling_kv)[half]

        def mix(which):
            return (here + ratios[half, which : which + 1, :] * step).astype(bf16)

        r_mix[half] = mix(0)
        gate_mix[half] = mix(3)
        for which in range(2):
            totals[which] += jnp.dot(
                mix(1 + which), weight[kind[13], which], preferred_element_type=f32
            )
        squeezed = squeezed + jnp.dot(mix(4), left[half], preferred_element_type=f32)
    for rel, mixes in enumerate((mix0, mix1, mix2)):
        for which in range(2):
            totals[which] += jnp.dot(
                mixes[which], sibling_kv[kind[10 + rel], which], preferred_element_type=f32
            )
    keys_ref[...] = totals[0]
    values_ref[...] = totals[1]
    squeezed = jnp.tanh(squeezed).astype(bf16)
    grown = jnp.dot(squeezed, right[...], preferred_element_type=f32)
    decay_ref[...] = -jnp.exp(base[...] + grown)


def projected(kind, mixes, lows, parts, owns, rests, *rest):
    rows, width = parts[0].shape
    rank, depth = lows[0].shape[2], owns[0].shape[1]
    flat = jax.ShapeDtypeStruct((rows, width), f32)
    wide = jax.ShapeDtypeStruct((2, rows, depth), bf16)
    tile_of = pl.BlockSpec((TILE, width), lambda i: (i, 0))
    wide_of = pl.BlockSpec((2, TILE, depth), lambda i: (0, i, 0))
    return pl.pallas_call(
        project_kernel,
        grid=(rows // TILE,),
        out_shape=[flat] * 3 + [wide] * 2,
        in_specs=[in_smem()]
        + [wide_of] * 3
        + [pl.BlockSpec((2, TILE, rank), lambda i: (0, i, 0))] * 3
        + [tile_of] * 2
        + [in_vmem()] * (4 + len(rest)),
        out_specs=[tile_of] * 3 + [wide_of] * 2,
        scratch_shapes=[pltpu.VMEM((2, rests[0].shape[0] + 1) + owns[0].shape, bf16)],
        compiler_params=kernel_params(),
        cost_estimate=takes(8),
    )(kind, *mixes, *lows, *parts, *owns, *rests, *rest)


def plain_kernel(kind, mix0, mix1, mix2, mix3, own, sibling, out_ref):
    half = pl.program_id(0)
    part = None
    for rel, mixes in enumerate((mix0, mix1, mix2, mix3)):
        weight = jnp.where(half == 0, own[kind[10 + rel], 0], sibling[kind[10 + rel], 0])
        new = jnp.dot(mixes[0], weight, preferred_element_type=f32)
        part = new if part is None else part + new

    @pl.when(half == 0)
    def _():
        out_ref[...] = part

    @pl.when(half == 1)
    def _():
        out_ref[...] += part


def plain_product(kind, mixes, own, sibling):
    rows, width = mixes[0].shape[1], own.shape[3]
    return pl.pallas_call(
        plain_kernel,
        grid=(2,),
        out_shape=jax.ShapeDtypeStruct((rows, width), f32),
        in_specs=[in_smem()] + [half_block(mix.shape) for mix in mixes] + [in_vmem()] * 2,
        out_specs=pl.BlockSpec((rows, width), lambda i: (0, 0)),
        compiler_params=kernel_params(),
        cost_estimate=takes(6),
    )(kind, *mixes, own, sibling)


def gate_kernel(
    kind,
    lengths,
    mix0,
    mix1,
    mix2,
    mix3,
    own,
    sibling,
    normed,
    kept0,
    sent0,
    kept1,
    sent1,
    total,
):
    half = pl.program_id(0)
    part = None
    for rel, mixes in enumerate((mix0, mix1, mix2, mix3)):
        weight = jnp.where(half == 0, own[kind[10 + rel], 0], sibling[kind[10 + rel], 0])
        new = jnp.dot(mixes[0], weight, preferred_element_type=f32)
        part = new if part is None else part + new

    @pl.when(half == 0)
    def _():
        total[...] = part

    @pl.when(half == 1)
    def _():
        gate = total[...] + part
        value = normed[...] * (gate * jax.nn.sigmoid(gate))
        row = lax.broadcasted_iota(jnp.int32, (BLK, value.shape[1]), 0)
        is_long = kind[0] == 1
        half_rows = BLK // 2

        def lived(n):
            block = value[n * BLK : (n + 1) * BLK]
            return jnp.where(row < lengths[n], block, 0.0).astype(bf16)

        for line in range(kept0.shape[1]):
            for block in range(2):
                even, odd = lived(4 * line + block), lived(4 * line + 2 + block)
                kept = jnp.where(is_long, even, odd)
                sent = jnp.where(is_long, odd, even)
                kept0[block, line] = kept[:half_rows]
                kept1[block, line] = kept[half_rows:]
                sent0[block, line] = sent[:half_rows]
                sent1[block, line] = sent[half_rows:]


def gated(kind, lengths, mixes, own, sibling, normed):
    rows, width = normed.shape
    quarter = jax.ShapeDtypeStruct((2, rows // TILE, BLK // 2, width), bf16)
    return pl.pallas_call(
        gate_kernel,
        grid=(2,),
        out_shape=[quarter] * 4,
        in_specs=[in_smem()] * 2 + [half_block(mix.shape) for mix in mixes] + [in_vmem()] * 3,
        out_specs=[pl.BlockSpec(quarter.shape, lambda i: (0, 0, 0, 0))] * 4,
        scratch_shapes=[pltpu.VMEM((rows, width), f32)],
        compiler_params=kernel_params(),
        cost_estimate=takes(7),
    )(kind, lengths, *mixes, own, sibling, normed)


def head_blocks(heads):
    width = heads * BLK
    tall = lax.broadcasted_iota(jnp.int32, (width, width), 0) // BLK
    wide = lax.broadcasted_iota(jnp.int32, (width, width), 1) // BLK
    return tall == wide


def state_kernel(lengths, carry, k_ref, v_ref, w_ref, s_ref, state_ref, entered_ref, hold):
    span, width = BLK, k_ref.shape[1]
    heads = width // span
    row = lax.broadcasted_iota(jnp.int32, (span, width), 0)
    lane = lax.broadcasted_iota(jnp.int32, (span, width), 1)
    for h in range(heads):
        hold[:, h * span : (h + 1) * span] = s_ref[h]

    @pl.loop(0, k_ref.shape[0] // span, unroll=8)
    def _(n):
        at = pl.ds(pl.multiple_of(n * span, span), span)
        live = row < lengths[n]
        k = jnp.where(live, k_ref[at, :], 0.0)
        total = jnp.where(live, w_ref[at, :], 0.0)
        after_row = jnp.zeros_like(total)
        half = 1
        while half < span:
            upper = (row & half) != 0
            across = jnp.where(
                upper, pltpu.roll(total, half, 0), pltpu.roll(total, span - half, 0)
            )
            after_row = after_row + jnp.where(upper, 0.0, across)
            total = total + across
            half *= 2
        added = lax.dot_general(
            (k * jnp.exp(after_row)).astype(bf16),
            v_ref[at, :].astype(bf16),
            (((0,), (0,)), ((), ())),
            preferred_element_type=f32,
        )
        fresh = jnp.zeros((span, width), f32)
        for h in range(heads):
            fresh = jnp.where(lane // span == h, added[h * span : (h + 1) * span], fresh)
        twice = jnp.concatenate([total] * 2, axis=0)
        turned_parts = []
        for p in range(width // (2 * span)):
            flipped = jnp.transpose(twice[:, p * 2 * span : (p + 1) * 2 * span])
            turned_parts.append(
                jnp.where(lane[:, : 2 * span] < span, flipped[:span], flipped[span:])
            )
        fade = jnp.exp(jnp.concatenate(turned_parts, axis=1))
        entered = hold[...] * carry[0]
        entered_ref[n] = entered.astype(bf16)
        state = fade * entered + fresh
        hold[...] = state
        for h in range(heads):
            state_ref[n, h] = state[:, h * span : (h + 1) * span]


def states_of(lengths, carry, k, v, w, state):
    rows, width = k.shape
    heads = width // BLK
    return pl.pallas_call(
        state_kernel,
        out_shape=[
            jax.ShapeDtypeStruct((rows // BLK, heads, BLK, BLK), f32),
            jax.ShapeDtypeStruct((rows // BLK, BLK, width), bf16),
        ],
        in_specs=[in_smem()] * 2 + [in_vmem()] * 4,
        out_specs=[in_vmem()] * 2,
        scratch_shapes=[pltpu.VMEM((BLK, width), f32)],
        compiler_params=kernel_params(),
        cost_estimate=takes(7),
    )(lengths, carry, k, v, w, state)


def sweep_kernel(lengths, r_ref, k_ref, v_ref, w_ref, entered_ref, u_ref, gain, bias, out_ref):
    span, width = BLK, r_ref.shape[1]
    heads = width // span
    row = lax.broadcasted_iota(jnp.int32, (span, width), 0)
    lane = lax.broadcasted_iota(jnp.int32, (span, width), 1)
    col = lane % span
    same_head = head_blocks(heads)

    def spread(value):
        stacked = jnp.concatenate([value.astype(bf16)] * heads, axis=0)
        return jnp.where(same_head, stacked, jnp.zeros_like(stacked))

    def against(a, b):
        return lax.dot_general(a, b, (((1,), (1,)), ((), ())), preferred_element_type=f32)

    @pl.loop(0, r_ref.shape[0] // span, unroll=8)
    def _(n):
        at = pl.ds(pl.multiple_of(n * span, span), span)
        live = row < lengths[n]
        r, v = r_ref[at, :], v_ref[at, :]
        k = jnp.where(live, k_ref[at, :], 0.0)
        total = jnp.where(live, w_ref[at, :], 0.0)
        before = jnp.zeros_like(total)
        after_row = jnp.zeros_like(total)
        scores = against((r * u_ref[...]).astype(bf16), spread(k))
        scores = jnp.where(row == col, scores, 0.0)
        level = 0
        while (1 << level) < span:
            half = 1 << level
            upper = (row & half) != 0
            if level:
                scale = jnp.exp(jnp.where(upper, before, after_row))
                part = against((r * scale).astype(bf16), spread(k * scale))
            else:
                part = against(r.astype(bf16), spread(k))
            pair = upper & (((row >> level) ^ (col >> level)) == 1)
            scores = jnp.where(pair, part, scores)
            across = jnp.where(
                upper, pltpu.roll(total, half, 0), pltpu.roll(total, span - half, 0)
            )
            before = before + jnp.where(upper, across, 0.0)
            after_row = after_row + jnp.where(upper, 0.0, across)
            total = total + across
            level += 1
        out = jnp.dot(scores.astype(bf16), spread(v), preferred_element_type=f32)
        out = out + jnp.dot(
            (r * jnp.exp(before)).astype(bf16),
            spread(entered_ref[n]),
            preferred_element_type=f32,
        )
        out_ref[at, :] = out

    ones = jnp.where(same_head, 1.0, 0.0).astype(bf16)

    def head_mean(value):
        high = value.astype(bf16)
        low = (value - high.astype(f32)).astype(bf16)
        both = jnp.dot(high, ones, preferred_element_type=f32) + jnp.dot(
            low, ones, preferred_element_type=f32
        )
        return both * (1.0 / span)

    @pl.loop(0, r_ref.shape[0] // TILE, unroll=2)
    def _(tile):
        at = pl.ds(pl.multiple_of(tile * TILE, TILE), TILE)
        value = out_ref[at, :]
        centred = value - head_mean(value)
        spread_of = head_mean(centred * centred)
        out_ref[at, :] = centred * lax.rsqrt(spread_of + norm_eps) * gain[...] + bias[...]


def sweep(lengths, r, k, v, w, entered, bonus, gain, bias):
    return pl.pallas_call(
        sweep_kernel,
        out_shape=jax.ShapeDtypeStruct(r.shape, f32),
        in_specs=[in_smem()] + [in_vmem()] * 8,
        out_specs=in_vmem(),
        compiler_params=kernel_params(),
        cost_estimate=takes(12),
    )(lengths, r, k, v, w, entered, bonus, gain, bias)


def final_kernel(block_of, h0, h1, h2, h3, weight, o0, o1, o2, o3, hold):
    @pl.loop(0, hold.shape[1] // TILE, unroll=2)
    def _(tile):
        at = pl.ds(pl.multiple_of(tile * TILE, TILE), TILE)
        total = None
        for k, piece in enumerate((h0, h1, h2, h3)):
            part = jnp.dot(piece[...], weight[k, :, at], preferred_element_type=f32)
            total = part if total is None else total + part
        hold[:, at] = total.astype(bf16)

    block = hold.shape[0] // 4
    for rel, out in enumerate((o0, o1, o2, o3)):
        at = pl.ds(pl.multiple_of(block_of[rel] * block, block), block)
        out[...] = hold[at, :].reshape(out.shape)


def final_product(block_of, pieces, weight, lines):
    rows, width = pieces[0].shape[0], weight.shape[2]
    out = jax.ShapeDtypeStruct((lines, rows // 4 // lines, width), bf16)
    return pl.pallas_call(
        final_kernel,
        out_shape=[out] * 4,
        in_specs=[in_smem()] + [in_vmem()] * 5,
        out_specs=[in_vmem()] * 4,
        scratch_shapes=[pltpu.VMEM((rows, width), bf16)],
        compiler_params=kernel_params(),
        cost_estimate=takes(4.5),
    )(block_of, *pieces, weight)


def lay_kernel(at, *refs):
    pieces, out_ref = refs[:-1], refs[-1]
    rows, width = pieces[0].shape
    lines = out_ref.shape[1] // width
    for n, piece in enumerate(pieces):
        column = pl.multiple_of(at[n % lines] * width, width)
        out_ref[n // lines * rows : (n // lines + 1) * rows, pl.ds(column, width)] = piece[...]


def laid(at, pieces, lines):
    rows, width = pieces[0].shape
    return pl.pallas_call(
        lay_kernel,
        out_shape=jax.ShapeDtypeStruct((len(pieces) // lines * rows, lines * width), bf16),
        in_specs=[in_smem()] + [in_vmem()] * len(pieces),
        out_specs=in_vmem(),
        compiler_params=kernel_params(),
        cost_estimate=takes(2),
    )(at, *pieces)


def after(value, *others):
    return lax.optimization_barrier((value,) + others)[0]


def turned(x, axis, by):
    length = lax.axis_size(axis)
    return lax.ppermute(x, axis, [(i, (i + by) % length) for i in range(length)])


def flipped_core(x):
    return lax.ppermute(x, "core", [(0, 1), (1, 0)])


def over_x(x):
    return lax.ppermute(x, "x", [(0, 1), (1, 0)])


def over_y(x):
    return lax.ppermute(x, "y", [(0, 1), (1, 0)])


def dealt(blocks, z):
    length = lax.axis_size("z")
    return [blocks(z)] + [turned(blocks((z + k) % length), "z", k) for k in range(1, length)]


def near_along(piece):
    two = turned(piece, "z", 2)
    one = lax.ppermute(piece, "z", [(0, 1), (1, 2), (2, 3)])
    three = lax.ppermute(piece, "z", [(1, 0), (2, 1), (3, 2)])
    return one, two, three


def far_along(two):
    return lax.ppermute(two, "z", [(1, 0), (2, 3)])


def spread_along(piece, z):
    one, two, three = near_along(piece)
    return piece, one, two, three, far_along(two)


def in_place(spread, z, at=0):
    piece, one, two, three, far = spread
    whole = jnp.zeros((4,) + piece.shape, piece.dtype)
    for k, part in ((1, one), (2, two), (3, three)):
        whole = lax.dynamic_update_index_in_dim(whole, part, (z - k) % 4, 0)
    far_at = jnp.where(z == 0, 3, jnp.where(z == 3, 0, z))
    whole = lax.dynamic_update_index_in_dim(whole, far, far_at, 0)
    return lax.dynamic_update_index_in_dim(whole, piece, z, 0)


def in_order(pieces, z):
    length = len(pieces)
    whole = jnp.zeros((length,) + pieces[0].shape, pieces[0].dtype)
    for k, piece in enumerate(pieces):
        whole = lax.dynamic_update_index_in_dim(whole, piece, (z - k) % length, 0)
    return whole


def on_core(
    continued_prompt_entries,
    padded_prompt_entries,
    prompt_live_extents,
    preceding_entry_line,
    carried_memory,
    token_mixing_ratios,
    acceptance_transform,
    lookup_transform,
    payload_transform,
    gating_transform,
    fading_baseline,
    fading_left_factor,
    fading_right_factor,
    present_reward,
    group_layer_scaling,
    group_layer_shift_term,
    final_transform,
):
    z, core = lax.axis_index("z"), lax.axis_index("core")
    y, x = lax.axis_index("y"), lax.axis_index("x")
    mp = 2 * y + x
    is_long = core == 0
    lines = lax.axis_size("z")
    group_rows, columns = continued_prompt_entries.shape
    requests = prompt_live_extents.shape[0]
    slot_rows = group_rows // requests
    heads, span = present_reward.shape
    heads = heads // lines
    width = heads * span
    depth = acceptance_transform.shape[0]
    rows = 2 * lines * group_rows

    kind = jnp.stack(
        [is_long.astype(jnp.int32), jnp.where(is_long, rows, slot_rows).astype(jnp.int32)]
        + [(mp ^ rel).astype(jnp.int32) for rel in range(4)]
        + [((z - k) % lines).astype(jnp.int32) for k in range(4)]
        + [((z - (mp ^ rel)) % lines).astype(jnp.int32) for rel in range(4)]
    )
    given = given_to_other_core(
        kind, prompt_live_extents, continued_prompt_entries, padded_prompt_entries
    )
    taken = flipped_core(given)
    block = block_of_chip(
        kind,
        prompt_live_extents,
        continued_prompt_entries,
        padded_prompt_entries,
        taken,
        preceding_entry_line[None],
    )
    (
        block,
        acceptance_transform,
        lookup_transform,
        payload_transform,
        gating_transform,
        final_transform,
        token_mixing_ratios,
        fading_left_factor,
        fading_right_factor,
        fading_baseline,
        present_reward,
        group_layer_scaling,
        group_layer_shift_term,
        carried_memory,
    ) = lax.optimization_barrier(
        (
            block,
            acceptance_transform,
            lookup_transform,
            payload_transform,
            gating_transform,
            final_transform,
            token_mixing_ratios,
            fading_left_factor,
            fading_right_factor,
            fading_baseline,
            present_reward,
            group_layer_scaling,
            group_layer_shift_term,
            carried_memory,
        )
    )
    def blocks_of(*weights):
        stacked = jnp.stack(weights)
        return tuple(
            lax.dynamic_slice_in_dim(stacked, (z + k) % lines * width, width, 2)
            for k in range(lines)
        )

    def both_cores(pieces):
        own = jnp.stack(pieces)
        return own, flipped_core(own)

    kv = blocks_of(lookup_transform, payload_transform)
    r = blocks_of(acceptance_transform)
    gate = blocks_of(gating_transform)
    one, two, three = near_along(block)
    own_x, own_y = over_x(block), over_y(block)
    one, two, three, own_x, own_y, kv, r = lax.optimization_barrier(
        (one, two, three, own_x, own_y, kv, r)
    )
    far = far_along(two)
    own_xy = (over_y(own_x[0]), over_x(own_y[1]))
    kv_two = turned(kv[2], "z", 2)
    far, own_xy, kv, r = lax.optimization_barrier((far, own_xy, kv, r))
    rest = jnp.stack([jnp.where(z == 0, far, one), two, jnp.where(z == 3, far, three)], axis=1)
    rest_x, rest_y = over_x(rest), over_y(rest)
    extents = in_order(
        [part[2 * group_rows + 1, : 2 * requests] for part in (block[0],) + tuple(rest[0])], z
    ).reshape(2 * lines * requests)
    extents = jnp.where(is_long, slot_rows, extents.astype(jnp.int32)).astype(jnp.int32)

    def chunk_order(whole):
        split = whole.reshape((4, 2, depth) + whole.shape[1:])
        parts = []
        for rel in range(4):
            both = split[mp ^ rel]
            parts.append(jnp.where(is_long, both, both[::-1]))
        return parts

    ratios = [part.transpose(0, 2, 1) for part in chunk_order(token_mixing_ratios.T)]
    left = chunk_order(fading_left_factor)

    kv_one, kv_three = turned(kv[1], "z", 1), turned(kv[3], "z", 3)
    rest_x, rest_y, kv_one, kv_two, kv_three, r, gate = lax.optimization_barrier(
        (rest_x, rest_y, kv_one, kv_two, kv_three, r, gate)
    )
    rest_xy = (over_y(rest_x[0]), over_x(rest_y[1]))
    own_kv, sibling_kv = both_cores((kv[0], kv_one, kv_two, kv_three))
    r_one, r_two, r_three = (turned(r[k], "z", k) for k in range(1, lines))
    rest_xy, r_one, r_two, r_three, gate = lax.optimization_barrier(
        (rest_xy, r_one, r_two, r_three, gate)
    )
    gate_two = turned(gate[2], "z", 2)
    gate_pieces = (gate[0], turned(gate[1], "z", 1), gate_two, turned(gate[3], "z", 3))
    own_r, sibling_r = both_cores((r[0], r_one, r_two, r_three))

    def mine_of(vector):
        return lax.dynamic_slice_in_dim(vector, z * width, width, 0)[None]

    kv_own, kv0, r0, gate0, low0 = mixes_of(kind, block, rest, ratios[0], left[0])
    kv1, r1, gate1, low1, *parts = mix_and_project(
        1, kind, own_x, rest_x, ratios[1], left[1], own_kv, kv_own
    )
    kv2, r2, gate2, low2, *parts = mix_and_project(
        2, kind, own_y, rest_y, ratios[2], left[2], own_kv, *parts
    )
    keys, values, decay, r3, gate3 = projected(
        kind,
        (kv0, kv1, kv2),
        (low0, low1, low2),
        parts,
        own_xy,
        rest_xy,
        ratios[3],
        left[3],
        own_kv,
        sibling_kv,
        lax.dynamic_slice_in_dim(fading_right_factor, z * width, width, 1),
        mine_of(fading_baseline),
    )
    entered = lax.dynamic_slice_in_dim(carried_memory, z * heads, heads, 0)
    bonus = lax.dynamic_slice_in_dim(present_reward, z * heads, heads, 0).reshape(1, width)
    states, states_in = states_of(
        extents,
        is_long.astype(f32)[None],
        keys,
        values,
        decay,
        jnp.where(is_long, entered, 0.0),
    )
    states = states.reshape(lines, 2, requests, heads, span, span)
    passed = flipped_core(lax.dynamic_index_in_dim(states, 1 - core, 1, keepdims=False))
    held = lax.dynamic_index_in_dim(states, core, 1, keepdims=False)
    bundle = jnp.concatenate(
        [jnp.where(is_long, held, passed)[:, -1:], jnp.where(is_long, passed, held)], axis=1
    ).astype(bf16)
    bundle = after(bundle, gate_pieces)
    r3 = after(r3, bundle)
    arrived = dealt(lambda j: lax.dynamic_index_in_dim(bundle, j, 0, keepdims=False), z)
    recept = plain_product(kind, (r0, r1, r2, r3), own_r, sibling_r)
    normed = sweep(
        extents,
        recept,
        keys,
        values,
        decay,
        states_in,
        bonus,
        mine_of(group_layer_scaling),
        mine_of(group_layer_shift_term),
    )
    own_gate, sibling_gate = both_cores(after(gate_pieces, states))
    kept0, sent0, kept1, sent1 = gated(
        kind, extents, (gate0, gate1, gate2, gate3), own_gate, sibling_gate, normed
    )

    kept0, sent0, kept1, sent1, arrived = lax.optimization_barrier(
        (kept0, sent0, kept1, sent1, arrived)
    )
    arrived = in_order(arrived, z).astype(f32)
    span_states = arrived[:, 0].reshape(1, lines * heads, span, span)
    request_states = jnp.swapaxes(arrived[:, 1:], 0, 1).reshape(
        requests, lines * heads, span, span
    )

    wide_out = 2 * final_transform.shape[1]
    beside = flipped_core(final_transform)
    out_weight = jnp.concatenate(
        [
            jnp.where(is_long, final_transform, beside),
            jnp.where(is_long, beside, final_transform),
        ],
        axis=1,
    ).reshape(lines, width, wide_out)
    out_weight = jnp.stack(
        [
            lax.dynamic_index_in_dim(out_weight, (z - k) % lines, 0, keepdims=False)
            for k in range(lines)
        ]
    )
    order = jnp.stack([(z - k) % lines for k in range(lines)]).astype(jnp.int32)
    block_of = jnp.stack(
        [(((y ^ (rel >> 1)) ^ core) * 2 + (x ^ (rel & 1))).astype(jnp.int32) for rel in range(4)]
    )
    spreads = []
    for kept, sent in ((kept0, sent0), (kept1, sent1)):
        part = jnp.concatenate([kept, flipped_core(sent)], axis=0)
        part = part.reshape(2 * rows // 4, width)
        if spreads:
            part = after(part, spreads[0][2])
        spreads.append(spread_along(part, z))
    out_pieces = []
    for piece, one, two, three, far in spreads:
        one = jnp.where(z == 0, far, one)
        three = jnp.where(z == 3, far, three)
        here, to_x, to_y, to_xy = final_product(
            block_of, (piece, one, two, three), out_weight, lines
        )
        across = lax.ppermute(to_xy, ("y", "x"), [(i, 3 - i) for i in range(4)])
        mixed_part = (
            here.astype(f32)
            + over_x(to_x).astype(f32)
            + over_y(to_y).astype(f32)
            + across.astype(f32)
        ).astype(bf16)
        out_pieces += dealt(
            lambda j: lax.dynamic_index_in_dim(mixed_part, j, 0, keepdims=False), z
        )
    mixed = laid(order, out_pieces, lines)[None]
    return mixed, span_states, request_states


def rows_kept_solution(mesh):
    placed = (
        P("seq", "mp"),
        P("seq", "mp"),
        P("seq"),
        P("mp"),
        P("mp", None, None),
        P(),
        P("seq", "mp"),
        P("seq", "mp"),
        P("seq", "mp"),
        P("seq", "mp"),
        P("mp"),
        P(),
        P(None, "mp"),
        P("mp", None),
        P("mp"),
        P("mp"),
        P("mp", "seq"),
    )
    return jax.shard_map(
        on_device,
        mesh=mesh,
        in_specs=placed,
        out_specs=(P("seq", "mp", None), P("seq", "mp", None, None), P("seq", "mp", None, None)),
        check_vma=False,
    )


def heads_kept_solution(mesh):
    seq, mp = mesh.shape["seq"], mesh.shape["mp"]
    split = Mesh(mesh.devices.reshape(seq // 2, 2, 2, mp // 2), ("z", "core", "y", "x"))
    s, m = ("z", "core"), ("y", "x")
    placed = (
        P(s, m),
        P(s, m),
        P(s),
        P(m),
        P(m, None, None),
        P(),
        P(s, m),
        P(s, m),
        P(s, m),
        P(s, m),
        P(m),
        P(),
        P(None, m),
        P(m, None),
        P(m),
        P(m),
        P(m, s),
    )
    return jax.shard_map(
        on_core,
        mesh=split,
        in_specs=placed,
        out_specs=(P(s, m, None), P(s, m, None, None), P(s, m, None, None)),
        check_vma=False,
    )


def solution(mesh):
    if mesh.shape["mp"] == 4 and mesh.shape["seq"] == 8:
        return heads_kept_solution(mesh)
    return rows_kept_solution(mesh)
```
